32 devices in a mesh: space: 8 (over z, x), vel: 4 (over y, core).
Axes of the slice: x: 2, y: 2, z: 4, core: 2. Of those that a mesh axis runs over, the one named last changes fastest.
Arguments:
- populations: float32 [64, 512, 2048], P('vel', 'space'), may hold values from 0.2 to 41, as said below
- shift_x: int32 [64], P('vel'), may hold values from -8 to 8, as said below
- shift_y: int32 [64], P('vel'), may hold values from -8 to 8, as said below
- frac_x: float32 [64], P('vel'), may hold values from 0 to 1
- frac_y: float32 [64], P('vel'), may hold values from 0 to 1
- inflow: float32 [64], P('vel'), may hold values from 0.5 to 2
- wall_state: float32 [64], P('vel'), may hold values from 0.5 to 2
- heights: int32 [2048], replicated, may hold values from 0 to 128
- impact_frequency_factor: float32 [], replicated, may hold values from 0.5 to 2
Outputs:
- relaxed: float32 [64, 512, 2048], P('vel', 'space')
The draws below stay inside these ranges and needn't reach their ends.
Inputs may be any that keep to these rules, and one draw needn't show every extreme that they name: `populations`: positive. `shift_x`: the values -8 and 8 both occur. `shift_y`: the values -8 and 8 both occur.
All inputs are finite; a program needn't handle non-finite values.
Results may differ from the reference program's by a relative error of at most 0.00002.
Values sent between devices are 32-bit elements; how exact they have to be, the bound alone decides.
No kernel may reach another device: no remote copies, remote signals or barrier semaphores. Data moves between devices by JAX's collectives and lax.ppermute only.
A program may use at most 128 MiB of HBM per device.

```python
import math
import jax
import jax.numpy as jnp
from jax import lax

SPEED_TALLY = 64
NX = 2048
CFL = 8
NY = 512


def draw_populations(key, part):
    first_key = jax.random.fold_in(jax.random.fold_in(key, 5), 0)
    level = jnp.arange(SPEED_TALLY, dtype=jnp.float32) / (SPEED_TALLY - 1)
    amplitude = 3.0 ** level
    rough = jnp.exp(jax.random.uniform(first_key, (SPEED_TALLY, NY, NX), jnp.float32, -1.0, 1.0))
    return amplitude[:, None, None] * rough


def pick_shifts(key):
    first_key, second_key = jax.random.split(key)
    values = jax.random.randint(first_key, (SPEED_TALLY,), -CFL, CFL + 1, dtype=jnp.int32)
    order = jax.random.permutation(second_key, SPEED_TALLY)
    values = values.at[order[0]].set(-CFL)
    return values.at[order[1]].set(CFL)


def draw_shift_x(key, part):
    return pick_shifts(jax.random.fold_in(key, 11))


def draw_shift_y(key, part):
    return pick_shifts(jax.random.fold_in(key, 23))


def draw_heights(key, part):
    first_key, second_key = jax.random.split(jax.random.fold_in(key, 37))
    start_col = jax.random.randint(first_key, (), 0, NX // 4 + 1, dtype=jnp.int32)
    rise_rate = jax.random.randint(second_key, (), 2, 9, dtype=jnp.int32)
    column = jnp.arange(NX, dtype=jnp.int32)
    return jnp.clip((column - start_col) * rise_rate // 4, 0, min(NX, NY) // 4)


def shard_levels(key, extent, shards, low, largest):
    def one(dim, shards_of):
        steps = jax.random.uniform(jax.random.fold_in(jax.random.fold_in(key, 6), dim), (shards_of,), jnp.float32, low / len(shards), largest / len(shards))
        return jnp.repeat(jnp.exp(steps), extent[dim] // shards_of).reshape((-1,) + (1,) * (len(extent) - dim - 1))

    gain = one(*shards[0])
    for cut in shards[1:]:
        gain = gain * one(*cut)
    return gain


def setup_inputs(seed: int = 0) -> dict:
    streams_of = jax.random.split(jax.random.key(seed), 10)
    populations = draw_populations(jax.random.fold_in(streams_of[9], 71), 0)
    shift_x = draw_shift_x(jax.random.fold_in(streams_of[9], 71), 0)
    shift_y = draw_shift_y(jax.random.fold_in(streams_of[9], 71), 0)
    frac_x = jnp.clip(1.0 * jax.random.uniform(streams_of[3], (SPEED_TALLY,), jnp.float32) ** shard_levels(streams_of[3], (SPEED_TALLY,), ((0, 4),), -0.2, 0.2), 0.0, 1.0)
    frac_y = jnp.clip(1.0 * jax.random.uniform(streams_of[4], (SPEED_TALLY,), jnp.float32) ** shard_levels(streams_of[4], (SPEED_TALLY,), ((0, 4),), -0.2, 0.2), 0.0, 1.0)
    inflow = jnp.clip(jnp.exp(math.log(2.0) - 1.3862944 * jax.random.uniform(streams_of[5], (SPEED_TALLY,), jnp.float32) ** shard_levels(streams_of[5], (SPEED_TALLY,), ((0, 4),), -0.2, 0.2)), 0.5, 2.0)
    wall_state = jnp.clip(jnp.exp(math.log(2.0) - 1.3862944 * jax.random.uniform(streams_of[6], (SPEED_TALLY,), jnp.float32) ** shard_levels(streams_of[6], (SPEED_TALLY,), ((0, 4),), -0.2, 0.2)), 0.5, 2.0)
    heights = draw_heights(jax.random.fold_in(streams_of[9], 71), 0)
    impact_frequency_factor = jnp.clip(jax.random.uniform(streams_of[8], (), jnp.float32, 0.5, 2.0), 0.5, 2.0)
    return {"populations": populations, "shift_x": shift_x, "shift_y": shift_y, "frac_x": frac_x, "frac_y": frac_y, "inflow": inflow, "wall_state": wall_state, "heights": heights, "impact_frequency_factor": impact_frequency_factor}


def advect_plane(plane, whole_part, frac_part, fill_value, which_dim):
    rim_width = CFL + 1
    border_shape = list(plane.shape)
    border_shape[which_dim] = rim_width
    border = jnp.full(tuple(border_shape), fill_value, jnp.float32)
    padded = jnp.concatenate([border, plane, border], which_dim)
    length = plane.shape[which_dim]
    nearer = lax.dynamic_slice_in_dim(padded, rim_width - whole_part, length, which_dim)
    further = lax.dynamic_slice_in_dim(padded, rim_width - whole_part - 1, length, which_dim)
    return (1.0 - frac_part) * nearer + frac_part * further

def maxwellian_profiles(particle_concentration, flux_x, flux_y, motion_work_share, impact_frequency_factor):
    average_drift_horizontal = flux_x / particle_concentration
    average_drift_vertical = flux_y / particle_concentration
    cellwise_thermal_spread = 0.5 * (motion_work_share / particle_concentration - average_drift_horizontal * average_drift_horizontal - average_drift_vertical * average_drift_vertical)
    approach_weighting = 1.0 - jnp.exp(-impact_frequency_factor * particle_concentration / (SPEED_TALLY * jnp.sqrt(cellwise_thermal_spread)))
    highest_ceiling = particle_concentration / (2.0 * math.pi * cellwise_thermal_spread)
    reciprocal_doubled_thermal = 0.5 / cellwise_thermal_spread
    return (average_drift_horizontal, average_drift_vertical, reciprocal_doubled_thermal, highest_ceiling, approach_weighting)

def reference(populations, shift_x, shift_y, frac_x, frac_y, inflow, wall_state, heights, impact_frequency_factor):
    row_index = jnp.arange(NY, dtype=jnp.int32)[:, None]
    solid_mask = row_index < heights[None, :]

    def move_one(items):
        plane, whole_x, whole_y, part_x, part_y, fill_value, wall_value = items
        plane = advect_plane(plane, whole_x, part_x, fill_value, 1)
        plane = advect_plane(plane, whole_y, part_y, fill_value, 0)
        return jnp.where(solid_mask, wall_value, plane)
    after_move = lax.map(move_one, (populations, shift_x, shift_y, frac_x, frac_y, inflow, wall_state))
    vel_x = shift_x.astype(jnp.float32) + frac_x
    vel_y = shift_y.astype(jnp.float32) + frac_y

    def accumulate(carry, items):
        plane, along_x, along_y = items
        return ((carry[0] + plane, carry[1] + plane * along_x, carry[2] + plane * along_y, carry[3] + plane * (along_x * along_x + along_y * along_y)), None)
    zero_plane = jnp.zeros((NY, NX), jnp.float32)
    aggregate_moments = lax.scan(accumulate, (zero_plane, zero_plane, zero_plane, zero_plane), (after_move, vel_x, vel_y))[0]
    average_drift_horizontal, average_drift_vertical, reciprocal_doubled_thermal, highest_ceiling, approach_weighting = maxwellian_profiles(aggregate_moments[0], aggregate_moments[1], aggregate_moments[2], aggregate_moments[3], impact_frequency_factor)

    def relax_one(items):
        plane, along_x, along_y = items
        horizontal_spacing = along_x - average_drift_horizontal
        vertical_spacing = along_y - average_drift_vertical
        maxwellian_state = highest_ceiling * jnp.exp(-(horizontal_spacing * horizontal_spacing + vertical_spacing * vertical_spacing) * reciprocal_doubled_thermal)
        return plane + approach_weighting * (maxwellian_state - plane)
    return lax.map(relax_one, (after_move, vel_x, vel_y))
```

```python
import functools
import math

import jax
import jax.numpy as jnp
from jax import lax
from jax.experimental import pallas as pl
from jax.experimental.pallas import tpu as pltpu
from jax.sharding import PartitionSpec as P

SPEED_TALLY = 64
CFL = 8
LOW_ROWS = CFL + 1
HIGH_ROWS = CFL
ROW = 8
LANE = 128
PAD = 24
F32 = jnp.float32
VMEM_LIMIT = 56 * 1024 * 1024

SMEM_SPEC = pl.BlockSpec(memory_space=pltpu.SMEM)
ANY_SPEC = pl.BlockSpec(memory_space=pl.ANY)
VMEM_SPEC = pl.BlockSpec(memory_space=pltpu.VMEM)


def params():
    return pltpu.CompilerParams(vmem_limit_bytes=VMEM_LIMIT)


def low_need(shift):
    return jnp.where(shift >= 0, shift + 1, 0)


def high_need(shift):
    return jnp.where(shift < 0, -shift, 0)


def pack_kernel(cuts, sy_ref, pop_ref, *refs):
    outs = refs[: len(cuts)]
    tail, head, low_pack, high_pack, sem_in, sem_out = refs[len(cuts) :]
    planes, row_tiles, lane_tiles = pop_ref.shape[:3]
    copies = [
        pltpu.make_async_copy(pop_ref.at[:, row_tiles - 2], tail.at[:, :, 0:8, :], sem_in.at[0]),
        pltpu.make_async_copy(pop_ref.at[:, row_tiles - 1], tail.at[:, :, 8:16, :], sem_in.at[1]),
        pltpu.make_async_copy(pop_ref.at[:, 0], head, sem_in.at[2]),
    ]
    for copy in copies:
        copy.start()
    for copy in copies:
        copy.wait()

    def one(v, offsets):
        low, high = offsets
        shift = sy_ref[v]

        @pl.when(shift >= 0)
        def _():
            for t in range(lane_tiles):
                low_pack[t, pl.ds(low, 8), :] = tail[v, t, pl.ds(15 - shift, 8), :]

        @pl.when(shift == CFL)
        def _():
            for t in range(lane_tiles):
                low_pack[t, pl.ds(low + 8, 8), :] = tail[v, t, pl.ds(15, 8), :]

        @pl.when(shift < 0)
        def _():
            for t in range(lane_tiles):
                high_pack[t, pl.ds(high, 8), :] = head[v, t]

        return low + low_need(shift), high + high_need(shift)

    lax.fori_loop(0, planes, one, (jnp.int32(0), jnp.int32(0)))
    copies = []
    for i, (pack, start, stop) in enumerate(cuts):
        source = (low_pack, high_pack)[pack].at[:, start:stop, :]
        copies.append(pltpu.make_async_copy(source, outs[i], sem_out.at[i]))
        copies[-1].start()
    for copy in copies:
        copy.wait()


def pack_rows(shift_y, pop, cuts):
    planes, _, lane_tiles = pop.shape[:3]
    return pl.pallas_call(
        functools.partial(pack_kernel, cuts),
        out_shape=[
            jax.ShapeDtypeStruct((lane_tiles, stop - start, LANE), F32) for _, start, stop in cuts
        ],
        in_specs=[SMEM_SPEC, ANY_SPEC],
        out_specs=[ANY_SPEC] * len(cuts),
        scratch_shapes=[
            pltpu.VMEM((planes, lane_tiles, 24, LANE), F32),
            pltpu.VMEM((planes, lane_tiles, 8, LANE), F32),
            pltpu.VMEM((lane_tiles, planes * LOW_ROWS + 16, LANE), F32),
            pltpu.VMEM((lane_tiles, planes * HIGH_ROWS + 16, LANE), F32),
            pltpu.SemaphoreType.DMA((3,)),
            pltpu.SemaphoreType.DMA((len(cuts),)),
        ],
        compiler_params=params(),
        name="pack_rows",
    )(shift_y, pop)


def load_tiles(pop_ref, padded, tiles, sems):
    lane_tiles = pop_ref.shape[2]
    copies = []
    for n, i in enumerate(tiles):
        target = padded.at[:, 1 : 1 + lane_tiles, PAD + ROW * i : PAD + ROW * (i + 1), :]
        copies.append(pltpu.make_async_copy(pop_ref.at[:, i], target, sems.at[n]))
        copies[-1].start()
    return copies


def fill_rows(padded, v, columns, start, count, value):
    block = jnp.full((ROW, LANE), value, F32)
    for t in columns:
        for r in range(start, start + count, ROW):
            padded[v, t, r : r + ROW, :] = block


def prepare_heights(heights_ref, bars):
    lane_tiles = heights_ref.shape[0]
    sublane = lax.broadcasted_iota(jnp.int32, (ROW, LANE), 0)
    for t in range(lane_tiles):
        bars[t] = jnp.broadcast_to(heights_ref[t : t + 1, :], (ROW, LANE)) - sublane


def advect_tile(padded, target, bars, v, j, first_row, scalars, solid_value):
    sx, sy, fx, fy = scalars
    lane_tiles = padded.shape[1] - 2
    lane = lax.broadcasted_iota(jnp.int32, (ROW, LANE), 1)
    start = PAD + ROW * j - sy
    near_roll = jnp.where(sx < 0, sx + LANE, sx)
    far_roll = jnp.where(sx + 1 < 0, sx + 1 + LANE, sx + 1)

    def moved(t):
        nearer = padded[v, t + 1, pl.ds(start, ROW), :]
        further = padded[v, t + 1, pl.ds(start - 1, ROW), :]
        line = (1.0 - fy) * nearer + fy * further
        return pltpu.roll(line, near_roll, 1), pltpu.roll(line, far_roll, 1)

    def finish(t, near, far):
        value = (1.0 - fx) * near + fx * far
        solid = first_row < bars[t]
        target[t] = jnp.where(solid, solid_value, value)

    @pl.when(sx >= 0)
    def _():
        own_near, own_far = lane >= sx, lane >= sx + 1
        before = moved(-1)
        for t in range(lane_tiles):
            here = moved(t)
            finish(
                t,
                jnp.where(own_near, here[0], before[0]),
                jnp.where(own_far, here[1], before[1]),
            )
            before = here

    @pl.when(sx < 0)
    def _():
        own_near, own_far = lane < sx + LANE, lane < sx + 1 + LANE
        here = moved(0)
        for t in range(lane_tiles):
            after = moved(t + 1)
            finish(
                t,
                jnp.where(own_near, here[0], after[0]),
                jnp.where(own_far, here[1], after[1]),
            )
            here = after


def velocity(sx_ref, sy_ref, fx_ref, fy_ref, v):
    return sx_ref[v].astype(F32) + fx_ref[v], sy_ref[v].astype(F32) + fy_ref[v]


def sum_moments(planes_ref, weights, lane_tile_range):
    sums = [[None] * 4 for _ in lane_tile_range]
    for v, (along_x, along_y) in enumerate(weights):
        square = along_x * along_x + along_y * along_y
        for n, t in enumerate(lane_tile_range):
            f = planes_ref[v, t]
            terms = (f, f * along_x, f * along_y, f * square)
            sums[n] = [b if a is None else a + b for a, b in zip(sums[n], terms)]
    return sums


def advance_kernel(tiles, raw_tiles, edges, meta_ref, sx_ref, sy_ref, fx_ref, fy_ref, inflow_ref,
                   wall_ref, heights_ref, pop_ref, *refs):
    if edges:
        mine_ref, theirs_ref, padded, planes_buf, moments, bars, sem_in, sem_out = refs
    else:
        planes_ref, mine_ref, theirs_ref, padded, planes_buf, moments, bars, sem_in, sem_out = refs
    planes, row_tiles, lane_tiles = pop_ref.shape[:3]
    half = lane_tiles // 2
    rows = row_tiles * ROW
    row0, first, last, core = (meta_ref[i] for i in range(4))
    loads = load_tiles(pop_ref, padded, raw_tiles, sem_in)
    prepare_heights(heights_ref, bars)

    def fill(v, _):
        value = inflow_ref[v]
        fill_rows(padded, v, (0, lane_tiles + 1), PAD, rows, value)
        if edges:
            columns = range(lane_tiles + 2)
            fill_rows(padded, v, columns, 0, PAD, jnp.where(first == 1, value, 0.0))
            fill_rows(padded, v, columns, PAD + rows, PAD, jnp.where(last == 1, value, 0.0))
        return 0

    lax.fori_loop(0, planes, fill, 0)
    for load in loads:
        load.wait()

    weights = [velocity(sx_ref, sy_ref, fx_ref, fy_ref, v) for v in range(planes)]

    def tile_planes(j, k, outside):
        def one(v, _):
            scalars = sx_ref[v], sy_ref[v], fx_ref[v], fy_ref[v]
            solid_value = jnp.where(outside, 0.0, wall_ref[v])
            advect_tile(padded, planes_buf.at[v, k], bars, v, j, row0 + ROW * j, scalars, solid_value)
            return 0

        lax.fori_loop(0, planes, one, 0)

    if not edges:
        count = len(tiles)

        def step(k, _):
            tile_planes(tiles[0] + k, k, False)
            for h in range(2):
                sums = sum_moments(planes_buf.at[:, k], weights, range(h * half, (h + 1) * half))
                slot = jnp.bitwise_xor(core, h)
                for t in range(half):
                    for m in range(4):
                        moments[slot, (k * 4 + m) * half + t] = sums[t][m]
            return 0

        lax.fori_loop(0, count, step, 0)
        copies = [
            pltpu.make_async_copy(planes_buf, planes_ref, sem_out.at[2]),
            pltpu.make_async_copy(moments.at[0], mine_ref, sem_out.at[0]),
            pltpu.make_async_copy(moments.at[1], theirs_ref, sem_out.at[1]),
        ]
    else:
        def step(k, _):
            j = jnp.where(k < 3, k - 1, row_tiles - 4 + k)
            tile_planes(j, 0, (j < 0) | (j >= row_tiles))
            for h in range(2):
                sums = sum_moments(planes_buf.at[:, 0], weights, range(h * half, (h + 1) * half))
                slot = jnp.bitwise_xor(core, h)

                @pl.when(k < 5)
                def _():
                    for t in range(half):
                        for m in range(4):
                            moments[slot, (k * 4 + m) * half + t] = sums[t][m]

                @pl.when(k == 5)
                def _():
                    for t in range(half):
                        for m in range(4):
                            moments[slot, 20 * half + m, t : t + 1, :] = sums[t][m][0:1, :]

            return 0

        lax.fori_loop(0, 6, step, 0)
        copies = [
            pltpu.make_async_copy(moments.at[0], mine_ref, sem_out.at[0]),
            pltpu.make_async_copy(moments.at[1], theirs_ref, sem_out.at[1]),
        ]
    for copy in copies:
        copy.start()
    for copy in copies:
        copy.wait()


def advance(tiles, edges, meta, small, heights, pop):
    planes, row_tiles, lane_tiles = pop.shape[:3]
    half = lane_tiles // 2
    if edges:
        raw_tiles = [0, 1, 2, row_tiles - 3, row_tiles - 2, row_tiles - 1]
        blocks = 20 * half + 4
        depth = 1
    else:
        raw_tiles = list(range(tiles[0] - 2, tiles[-1] + 2))
        blocks = len(tiles) * 4 * half
        depth = len(tiles)
    half_sums = jax.ShapeDtypeStruct((blocks, ROW, LANE), F32)
    out_shape = [half_sums, half_sums]
    if not edges:
        out_shape = [jax.ShapeDtypeStruct((planes, depth, lane_tiles, ROW, LANE), F32)] + out_shape
    return pl.pallas_call(
        functools.partial(advance_kernel, tiles, raw_tiles, edges),
        out_shape=out_shape,
        in_specs=[SMEM_SPEC] * 7 + [VMEM_SPEC, ANY_SPEC],
        out_specs=[ANY_SPEC] * len(out_shape),
        scratch_shapes=[
            pltpu.VMEM((planes, lane_tiles + 2, row_tiles * ROW + 2 * PAD, LANE), F32),
            pltpu.VMEM((planes, depth, lane_tiles, ROW, LANE), F32),
            pltpu.VMEM((2, blocks, ROW, LANE), F32),
            pltpu.VMEM((lane_tiles, ROW, LANE), jnp.int32),
            pltpu.SemaphoreType.DMA((len(raw_tiles),)),
            pltpu.SemaphoreType.DMA((3,)),
        ],
        compiler_params=params(),
        name="advance_edges" if edges else "advance_inside",
    )(meta, *small, heights, pop)


def join_kernel(edge_ref, low_ref, high_ref, out_ref):
    per_tile = high_ref.shape[0]
    half = per_tile // 4
    out_ref[0:per_tile] = edge_ref[0:per_tile] + low_ref[0:per_tile]
    out_ref[2 * per_tile :] = edge_ref[2 * per_tile :] + high_ref[...]
    top = lax.broadcasted_iota(jnp.int32, (ROW, LANE), 0) == 0
    for m in range(4):
        for t in range(half):
            n = per_tile + m * half + t
            row = jnp.broadcast_to(low_ref[per_tile + m, t : t + 1, :], (ROW, LANE))
            out_ref[n] = edge_ref[n] + jnp.where(top, row, 0.0)


def join(edge, from_low, from_high):
    return pl.pallas_call(
        join_kernel,
        out_shape=jax.ShapeDtypeStruct(edge.shape, F32),
        in_specs=[VMEM_SPEC] * 3,
        out_specs=VMEM_SPEC,
        compiler_params=params(),
        name="join_edges",
    )(edge, from_low, from_high)


def profile(density, flux_x, flux_y, energy, factor):
    inverse = 1.0 / density
    mean_x = flux_x * inverse
    mean_y = flux_y * inverse
    temperature = 0.5 * (energy * inverse - mean_x * mean_x - mean_y * mean_y)
    rate = 1.0 - jnp.exp(-factor * density / (SPEED_TALLY * jnp.sqrt(temperature)))
    height = rate * (density / (2.0 * math.pi * temperature))
    return mean_x, mean_y, -0.5 / temperature, height, 1.0 - rate


def relax_tile(get, put, sums, core, factor, weights, lane_tiles, k):
    half = lane_tiles // 2
    for t in range(lane_tiles):
        h, n = divmod(t, half)
        values = []
        for m in range(4):
            index = (k * 4 + m) * half + n
            own = sums[0][index] + sums[1][index]
            other = sums[2][index] + sums[3][index]
            values.append(jnp.where(core == h, own, other))
        mean_x, mean_y, scale, height, keep = profile(*values, factor)
        for v, (along_x, along_y) in enumerate(weights):
            gap_x = along_x - mean_x
            gap_y = along_y - mean_y
            state = height * jnp.exp((gap_x * gap_x + gap_y * gap_y) * scale)
            put(v, t, keep * get(v, t) + state)


def relax_kernel(meta_ref, sx_ref, sy_ref, fx_ref, fy_ref, factor_ref, planes_ref, s0, s1, s2, s3,
                 *refs):
    out_ref = refs[-1]
    planes, _, lane_tiles = planes_ref.shape[:3]
    weights = [velocity(sx_ref, sy_ref, fx_ref, fy_ref, v) for v in range(planes)]

    def put(v, t, value):
        out_ref[v, 0, t] = value

    relax_tile(
        lambda v, t: planes_ref[v, 0, t], put, (s0, s1, s2, s3), meta_ref[3], factor_ref[0], weights,
        lane_tiles, 0,
    )


def relax(meta, small, factor, after_move, sums, out, out_shape, first_tile):
    planes, count, lane_tiles = after_move.shape[:3]
    per_tile = 4 * lane_tiles // 2
    plane_block = (planes, 1, lane_tiles, ROW, LANE)
    operands = [meta, *small[:4], factor, after_move, *sums]
    in_specs = (
        [SMEM_SPEC] * 6
        + [pl.BlockSpec(plane_block, lambda k: (0, k, 0, 0, 0))]
        + [pl.BlockSpec((per_tile, ROW, LANE), lambda k: (k, 0, 0))] * 4
    )
    aliases = {}
    if out is not None:
        aliases = {len(operands): 0}
        operands.append(out)
        in_specs.append(ANY_SPEC)
    return pl.pallas_call(
        relax_kernel,
        grid=(count,),
        out_shape=out_shape,
        in_specs=in_specs,
        out_specs=pl.BlockSpec(plane_block, lambda k: (0, first_tile + k, 0, 0, 0)),
        input_output_aliases=aliases,
        compiler_params=params(),
        name="relax_inside",
    )(*operands)


def relax_edges_kernel(meta_ref, sx_ref, sy_ref, fx_ref, fy_ref, inflow_ref, wall_ref, factor_ref,
                       heights_ref, pop_ref, low_ref, high_ref, s0, s1, s2, s3, before_ref, out_ref,
                       padded, planes_buf, low_buf, high_buf, bars, sem_in, sem_out):
    planes, row_tiles, lane_tiles = pop_ref.shape[:3]
    rows = row_tiles * ROW
    row0, first, last, core = (meta_ref[i] for i in range(4))
    raw_tiles = [0, 1, 2, row_tiles - 3, row_tiles - 2, row_tiles - 1]
    loads = load_tiles(pop_ref, padded, raw_tiles, sem_in)
    for n, (source, buf) in enumerate(((low_ref, low_buf), (high_ref, high_buf))):
        target = buf.at[:, 16 : 16 + source.shape[1], :]
        loads.append(pltpu.make_async_copy(source, target, sem_in.at[len(raw_tiles) + n]))
        loads[-1].start()
    prepare_heights(heights_ref, bars)
    for load in loads:
        load.wait()

    def fill(v, offsets):
        low, high = offsets
        value = inflow_ref[v]
        shift = sy_ref[v]
        fill_rows(padded, v, (0, lane_tiles + 1), PAD - 16, rows + 24, value)

        @pl.when((shift >= 0) & (first == 1))
        def _():
            fill_rows(padded, v, range(1, lane_tiles + 1), PAD - 16, 16, value)

        @pl.when((shift < 0) & (last == 1))
        def _():
            fill_rows(padded, v, range(1, lane_tiles + 1), PAD + rows, 8, value)

        @pl.when((shift >= 0) & (first == 0))
        def _():
            for t in range(lane_tiles):
                for r in range(0, 16, ROW):
                    piece = low_buf[t, pl.ds(low + shift + 1 + r, ROW), :]
                    padded[v, t + 1, PAD - 16 + r : PAD - 16 + r + ROW, :] = piece

        @pl.when((shift < 0) & (last == 0))
        def _():
            for t in range(lane_tiles):
                padded[v, t + 1, PAD + rows : PAD + rows + ROW, :] = high_buf[
                    t, pl.ds(16 + high, ROW), :
                ]

        return low + low_need(shift), high + high_need(shift)

    lax.fori_loop(0, planes, fill, (jnp.int32(0), jnp.int32(0)))
    weights = [velocity(sx_ref, sy_ref, fx_ref, fy_ref, v) for v in range(planes)]

    def tile_of(k):
        return jnp.where(k < 2, k, row_tiles - 1)

    def step(k, _):
        j = tile_of(k)

        def one(v, _):
            scalars = sx_ref[v], sy_ref[v], fx_ref[v], fy_ref[v]
            advect_tile(padded, planes_buf.at[v, k], bars, v, j, row0 + ROW * j, scalars, wall_ref[v])
            return 0

        lax.fori_loop(0, planes, one, 0)

        def put(v, t, value):
            planes_buf[v, k, t] = value

        relax_tile(
            lambda v, t: planes_buf[v, k, t], put, (s0, s1, s2, s3), core, factor_ref[0], weights,
            lane_tiles, k,
        )
        return 0

    lax.fori_loop(0, 3, step, 0)
    copies = []
    for k in range(3):
        j = (0, 1, row_tiles - 1)[k]
        copies.append(pltpu.make_async_copy(planes_buf.at[:, k], out_ref.at[:, j], sem_out.at[k]))
        copies[-1].start()
    for copy in copies:
        copy.wait()


def relax_edges(meta, small, factor, heights, pop, low_rows, high_rows, sums, out):
    planes, row_tiles, lane_tiles = pop.shape[:3]
    operands = [meta, *small, factor, heights, pop, low_rows, high_rows, *sums, out]
    return pl.pallas_call(
        relax_edges_kernel,
        out_shape=jax.ShapeDtypeStruct(out.shape, F32),
        in_specs=[SMEM_SPEC] * 8 + [VMEM_SPEC] + [ANY_SPEC] * 3 + [VMEM_SPEC] * 4 + [ANY_SPEC],
        out_specs=ANY_SPEC,
        scratch_shapes=[
            pltpu.VMEM((planes, lane_tiles + 2, row_tiles * ROW + 2 * PAD, LANE), F32),
            pltpu.VMEM((planes, 3, lane_tiles, ROW, LANE), F32),
            pltpu.VMEM((lane_tiles, planes * LOW_ROWS + 32, LANE), F32),
            pltpu.VMEM((lane_tiles, planes * HIGH_ROWS + 32, LANE), F32),
            pltpu.VMEM((lane_tiles, ROW, LANE), jnp.int32),
            pltpu.SemaphoreType.DMA((8,)),
            pltpu.SemaphoreType.DMA((3,)),
        ],
        input_output_aliases={len(operands) - 1: 0},
        compiler_params=params(),
        name="relax_edges",
    )(*operands)


def per_device(populations, shift_x, shift_y, frac_x, frac_y, inflow, wall_state, heights,
               impact_frequency_factor):
    planes, row_count, col_count = populations.shape
    space_count, vel_count = lax.axis_size("space"), lax.axis_size("vel")
    row_tiles, lane_tiles = row_count // ROW, col_count // LANE
    half = lane_tiles // 2
    space, vel = lax.axis_index("space"), lax.axis_index("vel")
    forward = [(i, i + 1) for i in range(space_count - 1)]
    backward = [(target, source) for source, target in forward]
    partner = [(i, i ^ 1) for i in range(vel_count)]
    across = [(i, i ^ 2) for i in range(vel_count)]

    meta = jnp.stack(
        [space * row_count, space == 0, space == space_count - 1, vel % 2]
    ).astype(jnp.int32)
    small = (shift_x, shift_y, frac_x, frac_y, inflow, wall_state)
    factor = impact_frequency_factor.reshape(1)
    bars = heights.reshape(lane_tiles, LANE)
    pop = populations.reshape(planes, row_tiles, ROW, lane_tiles, LANE).transpose(0, 1, 3, 2, 4)

    cuts = [(0, 0, planes * LOW_ROWS), (1, 0, planes * HIGH_ROWS)]
    low_out, high_out = pack_rows(shift_y, pop, cuts)
    low_rows = lax.ppermute(low_out, "space", forward)
    high_rows = lax.ppermute(high_out, "space", backward)

    def share(mine, theirs):
        return mine + lax.ppermute(theirs, "vel", partner)

    def total(sums):
        received = lax.ppermute(sums, "vel", across)
        return (
            sums,
            received,
            lax.ppermute(sums, "vel", partner),
            lax.ppermute(received, "vel", partner),
        )

    middle = row_tiles // 2
    chunks = [list(range(2, middle)), list(range(middle, row_tiles - 1))]
    moved, sums = [], []
    edge_sums = None
    for n, tiles in enumerate(chunks):
        planes_part, mine, theirs = advance(tiles, False, meta, small, bars, pop)
        moved.append(planes_part)
        sums.append(total(share(mine, theirs)))
        if n == 0:
            edge_sums = share(*advance([], True, meta, small, bars, pop))
    per_tile = 4 * half
    from_high = lax.ppermute(edge_sums[:per_tile], "space", backward)
    from_low = lax.ppermute(edge_sums[4 * per_tile :], "space", forward)
    edge_total = total(join(edge_sums[per_tile : 4 * per_tile], from_low, from_high))

    out_shape = jax.ShapeDtypeStruct(pop.shape, F32)
    out = None
    for tiles, planes_part, parts in zip(chunks, moved, sums):
        out = relax(meta, small, factor, planes_part, parts, out, out_shape, tiles[0])
    out = relax_edges(meta, small, factor, bars, pop, low_rows, high_rows, edge_total, out)
    return out.transpose(0, 1, 3, 2, 4).reshape(planes, row_count, col_count)


def solution(mesh):
    return jax.shard_map(
        per_device,
        mesh=mesh,
        in_specs=(
            P("vel", "space", None),
            P("vel"),
            P("vel"),
            P("vel"),
            P("vel"),
            P("vel"),
            P("vel"),
            P(),
            P(),
        ),
        out_specs=P("vel", "space", None),
        check_vma=False,
    )
```

```python
import functools
import math

import jax
import jax.numpy as jnp
from jax import lax
from jax.experimental import pallas as pl
from jax.experimental.pallas import tpu as pltpu
from jax.sharding import PartitionSpec as P

SPEED_TALLY = 64
CFL = 8
LOW_ROWS = CFL + 1
HIGH_ROWS = CFL
ROW = 8
LANE = 128
PAD = 24
F32 = jnp.float32
LOW_SENT = 72
HIGH_SENT = 64

SMEM_SPEC = pl.BlockSpec(memory_space=pltpu.SMEM)
ANY_SPEC = pl.BlockSpec(memory_space=pl.ANY)
VMEM_SPEC = pl.BlockSpec(memory_space=pltpu.VMEM)


def params(mebibytes):
    return pltpu.CompilerParams(vmem_limit_bytes=mebibytes * 1024 * 1024)


def cost(us):
    return pl.CostEstimate(flops=0, bytes_accessed=int(us * 3.69e6), transcendentals=0)


def low_need(shift):
    return jnp.where(shift >= 0, shift + 1, 0)


def high_need(shift):
    return jnp.where(shift < 0, -shift, 0)


def fill_rows(padded, v, columns, start, count, value):
    block = jnp.full((ROW, LANE), value, F32)
    for t in columns:
        for r in range(start, start + count, ROW):
            padded[v, t, r : r + ROW, :] = block


def prepare_heights(heights_ref, bars):
    lane_tiles = heights_ref.shape[0]
    sublane = lax.broadcasted_iota(jnp.int32, (ROW, LANE), 0)
    for t in range(lane_tiles):
        bars[t] = jnp.broadcast_to(heights_ref[t : t + 1, :], (ROW, LANE)) - sublane


def advect(padded, v, scalars, tiles):
    sx, sy, fx, fy = scalars
    lane_tiles = padded.shape[1] - 2
    lane = lax.broadcasted_iota(jnp.int32, (ROW, LANE), 1)
    near_roll = jnp.where(sx < 0, sx + LANE, sx)
    far_roll = jnp.where(sx + 1 < 0, sx + 1 + LANE, sx + 1)

    def moved(start, t):
        nearer = padded[v, t + 1, pl.ds(start, ROW), :]
        further = padded[v, t + 1, pl.ds(start - 1, ROW), :]
        line = (1.0 - fy) * nearer + fy * further
        return pltpu.roll(line, near_roll, 1), pltpu.roll(line, far_roll, 1)

    def blend(put, t, near, far):
        put(t, (1.0 - fx) * near + fx * far)

    @pl.when(sx >= 0)
    def _():
        own_near, own_far = lane >= sx, lane >= sx + 1
        for begin, put in tiles:
            before = moved(begin - sy, -1)
            for t in range(lane_tiles):
                here = moved(begin - sy, t)
                near = jnp.where(own_near, here[0], before[0])
                blend(put, t, near, jnp.where(own_far, here[1], before[1]))
                before = here

    @pl.when(sx < 0)
    def _():
        own_near, own_far = lane < sx + LANE, lane < sx + 1 + LANE
        for begin, put in tiles:
            here = moved(begin - sy, 0)
            for t in range(lane_tiles):
                after = moved(begin - sy, t + 1)
                near = jnp.where(own_near, here[0], after[0])
                blend(put, t, near, jnp.where(own_far, here[1], after[1]))
                here = after


def store_masked(target, bars, first_row, solid_value):
    def put(t, value):
        target[t] = jnp.where(first_row < bars[t], solid_value, value)

    return put


def velocity(sx_ref, sy_ref, fx_ref, fy_ref, v):
    return sx_ref[v].astype(F32) + fx_ref[v], sy_ref[v].astype(F32) + fy_ref[v]


def sum_moments(planes_ref, k, weights, lane_tile_range):
    sums = [[None] * 4 for _ in lane_tile_range]
    for v, (along_x, along_y) in enumerate(weights):
        square = along_x * along_x + along_y * along_y
        for n, t in enumerate(lane_tile_range):
            f = planes_ref[v, k, t]
            terms = (f, f * along_x, f * along_y, f * square)
            sums[n] = [b if a is None else a + b for a, b in zip(sums[n], terms)]
    return sums


def tile_loads(pop_ref, padded, raw_tiles, sems, v):
    lane_tiles = pop_ref.shape[2]
    return [
        pltpu.make_async_copy(
            pop_ref.at[v, i],
            padded.at[v, 1 : 1 + lane_tiles, PAD + ROW * i : PAD + ROW * (i + 1), :],
            sems.at[v, n],
        )
        for n, i in enumerate(raw_tiles)
    ]


def start_loads(pop_ref, padded, raw_tiles, sems):
    def one(v, _):
        for load in tile_loads(pop_ref, padded, raw_tiles, sems, v):
            load.start()
        return 0

    lax.fori_loop(0, pop_ref.shape[0], one, 0)


def inside_kernel(tiles, raw_tiles, meta_ref, sx_ref, sy_ref, fx_ref, fy_ref, inflow_ref, wall_ref,
                  heights_ref, pop_ref, _, planes_ref, sums_ref, padded, planes_buf, moments, bars, sem_in,
                  sem_planes, sem_out):
    planes, row_tiles, lane_tiles = pop_ref.shape[:3]
    half = lane_tiles // 2
    count = len(tiles)
    row0 = meta_ref[0]
    start_loads(pop_ref, padded, raw_tiles, sem_in)
    prepare_heights(heights_ref, bars)

    def out_copy(v):
        return pltpu.make_async_copy(planes_buf.at[v], planes_ref.at[v], sem_planes.at[v])

    def one(v, _):
        fill_rows(padded, v, (0, lane_tiles + 1), PAD, row_tiles * ROW, inflow_ref[v])
        for load in tile_loads(pop_ref, padded, raw_tiles, sem_in, v):
            load.wait()
        scalars = sx_ref[v], sy_ref[v], fx_ref[v], fy_ref[v]
        work = [
            (PAD + ROW * j, store_masked(planes_buf.at[v, k], bars, row0 + ROW * j, wall_ref[v]))
            for k, j in enumerate(tiles)
        ]
        advect(padded, v, scalars, work)
        out_copy(v).start()
        return 0

    lax.fori_loop(0, planes, one, 0)
    weights = [velocity(sx_ref, sy_ref, fx_ref, fy_ref, v) for v in range(planes)]

    def step(k, _):
        for h in range(2):
            sums = sum_moments(planes_buf, k, weights, range(h * half, (h + 1) * half))
            for t in range(half):
                for m in range(4):
                    moments[((h * count + k) * 4 + m) * half + t] = sums[t][m]
        return 0

    lax.fori_loop(0, count, step, 0)
    copy = pltpu.make_async_copy(moments, sums_ref, sem_out.at[0])
    copy.start()

    def finish(v, _):
        out_copy(v).wait()
        return 0

    lax.fori_loop(0, planes, finish, 0)
    copy.wait()


def advance_inside(tiles, meta, small, heights, pop, after):
    planes, row_tiles, lane_tiles = pop.shape[:3]
    count = len(tiles)
    raw_tiles = list(range(tiles[0] - 2, tiles[-1] + 2))
    blocks = 4 * lane_tiles * count
    return pl.pallas_call(
        functools.partial(inside_kernel, tiles, raw_tiles),
        out_shape=[
            jax.ShapeDtypeStruct((planes, count, lane_tiles, ROW, LANE), F32),
            jax.ShapeDtypeStruct((blocks, ROW, LANE), F32),
        ],
        in_specs=[SMEM_SPEC] * 7 + [VMEM_SPEC, ANY_SPEC, ANY_SPEC],
        out_specs=[ANY_SPEC] * 2,
        scratch_shapes=[
            pltpu.VMEM((planes, lane_tiles + 2, row_tiles * ROW + 2 * PAD, LANE), F32),
            pltpu.VMEM((planes, count, lane_tiles, ROW, LANE), F32),
            pltpu.VMEM((blocks, ROW, LANE), F32),
            pltpu.VMEM((lane_tiles, ROW, LANE), jnp.int32),
            pltpu.SemaphoreType.DMA((planes, len(raw_tiles))),
            pltpu.SemaphoreType.DMA((planes,)),
            pltpu.SemaphoreType.DMA((1,)),
        ],
        compiler_params=params(58),
        cost_estimate=cost(6),
        name="advance_inside",
    )(meta, *small, heights, pop, after)


def edges_kernel(raw_tiles, cuts, meta_ref, sx_ref, sy_ref, fx_ref, fy_ref, inflow_ref, wall_ref,
                 heights_ref, pop_ref, *refs):
    planes_ref, mine_ref, theirs_ref = refs[:3]
    packs = refs[3 : 3 + len(cuts)]
    (padded, planes_buf, moments, bars, low_pack, high_pack, sem_in, sem_planes, sem_out) = refs[
        3 + len(cuts) :
    ]
    planes, row_tiles, lane_tiles = pop_ref.shape[:3]
    half = lane_tiles // 2
    rows = row_tiles * ROW
    row0, first, last, core = (meta_ref[i] for i in range(4))
    start_loads(pop_ref, padded, raw_tiles, sem_in)
    prepare_heights(heights_ref, bars)
    zero = jnp.zeros((ROW, LANE), F32)

    def out_copy(v):
        return pltpu.make_async_copy(planes_buf.at[v, 1:4], planes_ref.at[v], sem_planes.at[v])

    def one(v, offsets):
        low, high = offsets
        value = inflow_ref[v]
        shift = sy_ref[v]
        columns = range(lane_tiles + 2)
        fill_rows(padded, v, (0, lane_tiles + 1), PAD, rows, value)
        fill_rows(padded, v, columns, 0, PAD, jnp.where(first == 1, value, 0.0))
        fill_rows(padded, v, columns, PAD + rows, PAD, jnp.where(last == 1, value, 0.0))
        up = shift >= 0
        idle_slot = jnp.where(up, 0, 4)
        for t in range(lane_tiles):
            planes_buf[v, idle_slot, t] = zero
            planes_buf[v, 5, t] = zero
        for load in tile_loads(pop_ref, padded, raw_tiles, sem_in, v):
            load.wait()
        scalars = sx_ref[v], shift, fx_ref[v], fy_ref[v]

        def entry(j, slot, solid_value):
            first_row = row0 + ROW * j
            return PAD + ROW * j, store_masked(planes_buf.at[v, slot], bars, first_row, solid_value)

        wall = wall_ref[v]
        work = [
            entry(0, 1, wall),
            entry(1, 2, wall),
            entry(row_tiles - 1, 3, wall),
            entry(jnp.where(up, row_tiles, -1), 4 - idle_slot, 0.0),
        ]
        advect(padded, v, scalars, work)
        out_copy(v).start()

        @pl.when(shift == CFL)
        def _():
            advect(padded, v, scalars, [entry(row_tiles + 1, 5, 0.0)])
            for t in range(lane_tiles):
                low_pack[t, pl.ds(low + 8, 8), :] = padded[v, t + 1, PAD + rows - 1 : PAD + rows + 7, :]

        @pl.when(up)
        def _():
            for t in range(lane_tiles):
                source = pl.ds(PAD + rows - 1 - shift, 8)
                low_pack[t, pl.ds(low, 8), :] = padded[v, t + 1, source, :]

        @pl.when(jnp.logical_not(up))
        def _():
            for t in range(lane_tiles):
                high_pack[t, pl.ds(high, 8), :] = padded[v, t + 1, PAD : PAD + 8, :]

        return low + low_need(shift), high + high_need(shift)

    lax.fori_loop(0, planes, one, (jnp.int32(0), jnp.int32(0)))
    weights = [velocity(sx_ref, sy_ref, fx_ref, fy_ref, v) for v in range(planes)]

    def step(k, _):
        for h in range(2):
            sums = sum_moments(planes_buf, k, weights, range(h * half, (h + 1) * half))
            slot = jnp.bitwise_xor(core, h)
            for t in range(half):
                for m in range(4):
                    moments[slot, (k * 4 + m) * half + t] = sums[t][m]
        return 0

    lax.fori_loop(0, 5, step, 0)
    for h in range(2):
        sums = sum_moments(planes_buf, 5, weights, range(h * half, (h + 1) * half))
        slot = jnp.bitwise_xor(core, h)
        for t in range(half):
            for m in range(4):
                moments[slot, 20 * half + m, t : t + 1, :] = sums[t][m][0:1, :]
    copies = [
        pltpu.make_async_copy(moments.at[1], theirs_ref, sem_out.at[1]),
        pltpu.make_async_copy(moments.at[0], mine_ref, sem_out.at[0]),
    ]
    for n, (pack, begin, end) in enumerate(cuts):
        source = (low_pack, high_pack)[pack].at[:, begin:end, :]
        copies.append(pltpu.make_async_copy(source, packs[n], sem_out.at[2 + n]))
    for copy in copies:
        copy.start()

    def finish(v, _):
        out_copy(v).wait()
        return 0

    lax.fori_loop(0, planes, finish, 0)
    for copy in copies:
        copy.wait()


def advance_edges(meta, small, heights, pop, cuts):
    planes, row_tiles, lane_tiles = pop.shape[:3]
    half = lane_tiles // 2
    raw_tiles = [0, 1, 2, row_tiles - 3, row_tiles - 2, row_tiles - 1]
    blocks = 20 * half + 4
    half_sums = jax.ShapeDtypeStruct((blocks, ROW, LANE), F32)
    return pl.pallas_call(
        functools.partial(edges_kernel, raw_tiles, cuts),
        out_shape=[
            jax.ShapeDtypeStruct((planes, 3, lane_tiles, ROW, LANE), F32),
            half_sums,
            half_sums,
        ]
        + [jax.ShapeDtypeStruct((lane_tiles, end - begin, LANE), F32) for _, begin, end in cuts],
        in_specs=[SMEM_SPEC] * 7 + [VMEM_SPEC, ANY_SPEC],
        out_specs=[ANY_SPEC] * (3 + len(cuts)),
        scratch_shapes=[
            pltpu.VMEM((planes, lane_tiles + 2, row_tiles * ROW + 2 * PAD, LANE), F32),
            pltpu.VMEM((planes, 6, lane_tiles, ROW, LANE), F32),
            pltpu.VMEM((2, blocks, ROW, LANE), F32),
            pltpu.VMEM((lane_tiles, ROW, LANE), jnp.int32),
            pltpu.VMEM((lane_tiles, planes * LOW_ROWS + 16, LANE), F32),
            pltpu.VMEM((lane_tiles, planes * HIGH_ROWS + 16, LANE), F32),
            pltpu.SemaphoreType.DMA((planes, len(raw_tiles))),
            pltpu.SemaphoreType.DMA((planes,)),
            pltpu.SemaphoreType.DMA((2 + len(cuts),)),
        ],
        compiler_params=params(58),
        cost_estimate=cost(6),
        name="advance_edges",
    )(meta, *small, heights, pop)


def split_kernel(mine_ref, received_ref, down_ref, edge_ref, up_ref):
    begin = 0
    for ref in (down_ref, edge_ref, up_ref):
        n = ref.shape[0]
        ref[...] = mine_ref[begin : begin + n] + received_ref[begin : begin + n]
        begin += n


def split(mine, received, per_tile):
    sizes = per_tile, 3 * per_tile, per_tile + 4
    return pl.pallas_call(
        split_kernel,
        out_shape=[jax.ShapeDtypeStruct((n, ROW, LANE), F32) for n in sizes],
        in_specs=[VMEM_SPEC] * 2,
        out_specs=[VMEM_SPEC] * 3,
        compiler_params=params(4),
        cost_estimate=cost(1),
        name="split_edges",
    )(mine, received)


def join_kernel(edge_ref, low_ref, high_ref, out_ref):
    per_tile = high_ref.shape[0]
    half = per_tile // 4
    out_ref[0:per_tile] = edge_ref[0:per_tile] + low_ref[0:per_tile]
    out_ref[2 * per_tile :] = edge_ref[2 * per_tile :] + high_ref[...]
    top = lax.broadcasted_iota(jnp.int32, (ROW, LANE), 0) == 0
    for m in range(4):
        for t in range(half):
            n = per_tile + m * half + t
            row = jnp.broadcast_to(low_ref[per_tile + m, t : t + 1, :], (ROW, LANE))
            out_ref[n] = edge_ref[n] + jnp.where(top, row, 0.0)


def join(edge, from_low, from_high):
    return pl.pallas_call(
        join_kernel,
        out_shape=jax.ShapeDtypeStruct(edge.shape, F32),
        in_specs=[VMEM_SPEC] * 3,
        out_specs=VMEM_SPEC,
        compiler_params=params(4),
        cost_estimate=cost(1),
        name="join_edges",
    )(edge, from_low, from_high)


def profile(density, flux_x, flux_y, energy, factor):
    inverse = 1.0 / density
    mean_x = flux_x * inverse
    mean_y = flux_y * inverse
    temperature = 0.5 * (energy * inverse - mean_x * mean_x - mean_y * mean_y)
    rate = 1.0 - jnp.exp(-factor * density / (SPEED_TALLY * jnp.sqrt(temperature)))
    height = rate * (density / (2.0 * math.pi * temperature))
    return mean_x, mean_y, -0.5 / temperature, height, 1.0 - rate


def relax_cells(get, put, values, factor, weights):
    mean_x, mean_y, scale, height, keep = profile(*values, factor)
    for v, (along_x, along_y) in enumerate(weights):
        gap_x = along_x - mean_x
        gap_y = along_y - mean_y
        state = height * jnp.exp((gap_x * gap_x + gap_y * gap_y) * scale)
        put(v, keep * get(v) + state)


def relax_kernel(meta_ref, sx_ref, sy_ref, fx_ref, fy_ref, factor_ref, planes_ref, own_ref, core_ref,
                 mine_ref, other_ref, out_ref):
    planes, _, half = planes_ref.shape[:3]
    weights = [velocity(sx_ref, sy_ref, fx_ref, fy_ref, v) for v in range(planes)]
    is_mine = meta_ref[3] == pl.program_id(1)
    for t in range(half):
        values = []
        for m in range(4):
            n = m * half + t
            far = jnp.where(is_mine, mine_ref[n], other_ref[n])
            values.append(own_ref[n] + core_ref[n] + far)

        def put(v, value):
            out_ref[v, 0, t] = value

        relax_cells(lambda v: planes_ref[v, 0, t], put, values, factor_ref[0], weights)


def relax_inside(meta, small, factor, after_move, own, from_core, mine, other, out_shape, first_tile):
    planes, count, lane_tiles = after_move.shape[:3]
    half = lane_tiles // 2
    plane_block = (planes, 1, half, ROW, LANE)
    sums_block = (4 * half, ROW, LANE)
    return pl.pallas_call(
        relax_kernel,
        grid=(count, 2),
        out_shape=out_shape,
        in_specs=[SMEM_SPEC] * 6
        + [pl.BlockSpec(plane_block, lambda k, h: (0, k, h, 0, 0))]
        + [pl.BlockSpec(sums_block, lambda k, h: (h * count + k, 0, 0))] * 2
        + [pl.BlockSpec(sums_block, lambda k, h: (k, 0, 0))] * 2,
        out_specs=pl.BlockSpec(plane_block, lambda k, h: (0, first_tile + k, h, 0, 0)),
        compiler_params=params(58),
        cost_estimate=cost(6),
        name="relax_inside",
    )(meta, *small[:4], factor, after_move, own, from_core, mine, other)


def relax_edges_kernel(cuts, meta_ref, sx_ref, sy_ref, fx_ref, fy_ref, inflow_ref, factor_ref,
                       heights_ref, planes_ref, s0, s1, s2, s3, *refs):
    pack_refs = refs[: len(cuts)]
    (_, out_ref, frames, planes_buf, low_buf, high_buf, bars, sem_in, sem_planes, sem_out) = refs[
        len(cuts) :
    ]
    planes, _, lane_tiles = planes_ref.shape[:3]
    row_tiles = out_ref.shape[1]
    half = lane_tiles // 2
    row0, first, last, core = (meta_ref[i] for i in range(4))

    def in_copy(v):
        return pltpu.make_async_copy(planes_ref.at[v], planes_buf.at[v], sem_planes.at[v])

    loads = []
    for n, (pack, begin, end) in enumerate(cuts):
        target = (low_buf, high_buf)[pack].at[:, 16 + begin : 16 + end, :]
        loads.append(pltpu.make_async_copy(pack_refs[n], target, sem_in.at[n]))
        loads[-1].start()

    def begin_load(v, _):
        in_copy(v).start()
        return 0

    lax.fori_loop(0, planes, begin_load, 0)
    prepare_heights(heights_ref, bars)
    for load in loads:
        load.wait()

    def add_masked(target, first_row):
        def put(t, value):
            target[t] = target[t] + jnp.where(first_row < bars[t], 0.0, value)

        return put

    def one(v, offsets):
        low, high = offsets
        value = inflow_ref[v]
        shift = sy_ref[v]
        up = shift >= 0
        in_copy(v).wait()
        scalars = sx_ref[v], shift, fx_ref[v], fy_ref[v]
        borders = (0, lane_tiles + 1)
        columns = range(lane_tiles + 2)

        @pl.when(up & (first == 0))
        def _():
            fill_rows(frames, v, borders, 8, 16, value)
            fill_rows(frames, v, columns, 24, 16, 0.0)
            for t in range(lane_tiles):
                for r in range(0, 16, ROW):
                    piece = low_buf[t, pl.ds(low + shift + 1 + r, ROW), :]
                    frames[v, t + 1, 8 + r : 8 + r + ROW, :] = piece
            advect(frames, v, scalars, [(24, add_masked(planes_buf.at[v, 0], row0))])

            @pl.when(shift == CFL)
            def _():
                advect(frames, v, scalars, [(32, add_masked(planes_buf.at[v, 1], row0 + ROW))])

        @pl.when(jnp.logical_not(up) & (last == 0))
        def _():
            fill_rows(frames, v, borders, 32, 8, value)
            fill_rows(frames, v, columns, 16, 16, 0.0)
            for t in range(lane_tiles):
                frames[v, t + 1, 32:40, :] = high_buf[t, pl.ds(16 + high, ROW), :]
            first_row = row0 + ROW * (row_tiles - 1)
            advect(frames, v, scalars, [(24, add_masked(planes_buf.at[v, 2], first_row))])

        return low + low_need(shift), high + high_need(shift)

    lax.fori_loop(0, planes, one, (jnp.int32(0), jnp.int32(0)))
    weights = [velocity(sx_ref, sy_ref, fx_ref, fy_ref, v) for v in range(planes)]

    def out_copy(k, h):
        j = jnp.where(k < 2, k, row_tiles - 1)
        lanes = pl.ds(h * half, half)
        return pltpu.make_async_copy(
            planes_buf.at[:, k, lanes], out_ref.at[:, j, lanes], sem_out.at[2 * k + h]
        )

    def step(k, _):
        for h in range(2):
            for n in range(half):
                t = h * half + n
                values = []
                for m in range(4):
                    index = (k * 4 + m) * half + n
                    values.append(
                        jnp.where(core == h, s0[index] + s1[index], s2[index] + s3[index])
                    )

                def put(v, value):
                    planes_buf[v, k, t] = value

                relax_cells(lambda v: planes_buf[v, k, t], put, values, factor_ref[0], weights)
            out_copy(k, h).start()
        return 0

    lax.fori_loop(0, 3, step, 0)
    for k in range(3):
        for h in range(2):
            out_copy(k, h).wait()


def relax_edges(meta, small, factor, heights, planes_part, sums, packs, cuts, out):
    planes, _, lane_tiles = planes_part.shape[:3]
    operands = [meta, *small[:5], factor, heights, planes_part, *sums, *packs, out]
    return pl.pallas_call(
        functools.partial(relax_edges_kernel, cuts),
        out_shape=jax.ShapeDtypeStruct(out.shape, F32),
        in_specs=[SMEM_SPEC] * 7
        + [VMEM_SPEC, ANY_SPEC]
        + [VMEM_SPEC] * 4
        + [ANY_SPEC] * (len(cuts) + 1),
        out_specs=ANY_SPEC,
        scratch_shapes=[
            pltpu.VMEM((planes, lane_tiles + 2, 48, LANE), F32),
            pltpu.VMEM((planes, 3, lane_tiles, ROW, LANE), F32),
            pltpu.VMEM((lane_tiles, planes * LOW_ROWS + 32, LANE), F32),
            pltpu.VMEM((lane_tiles, planes * HIGH_ROWS + 32, LANE), F32),
            pltpu.VMEM((lane_tiles, ROW, LANE), jnp.int32),
            pltpu.SemaphoreType.DMA((len(cuts),)),
            pltpu.SemaphoreType.DMA((planes,)),
            pltpu.SemaphoreType.DMA((6,)),
        ],
        input_output_aliases={len(operands) - 1: 0},
        compiler_params=params(58),
        cost_estimate=cost(5),
        name="relax_edges",
    )(*operands)


def per_device(populations, shift_x, shift_y, frac_x, frac_y, inflow, wall_state, heights,
               impact_frequency_factor):
    planes, row_count, col_count = populations.shape
    space_count, vel_count = lax.axis_size("space"), lax.axis_size("vel")
    row_tiles, lane_tiles = row_count // ROW, col_count // LANE
    half = lane_tiles // 2
    space, vel = lax.axis_index("space"), lax.axis_index("vel")
    core = vel % 2
    forward = [(i, i + 1) for i in range(space_count - 1)]
    backward = [(target, source) for source, target in forward]
    partner = [(i, i ^ 1) for i in range(vel_count)]
    across = [(i, i ^ 2) for i in range(vel_count)]

    meta = jnp.stack([space * row_count, space == 0, space == space_count - 1, core]).astype(jnp.int32)
    small = (shift_x, shift_y, frac_x, frac_y, inflow, wall_state)
    factor = impact_frequency_factor.reshape(1)
    bars = heights.reshape(lane_tiles, LANE)
    pop = populations.reshape(planes, row_tiles, ROW, lane_tiles, LANE).transpose(0, 1, 3, 2, 4)
    low_sent, high_sent = min(LOW_SENT, planes * LOW_ROWS), min(HIGH_SENT, planes * HIGH_ROWS)
    cuts = [
        (0, 0, low_sent),
        (1, 0, high_sent),
        (0, low_sent, planes * LOW_ROWS),
        (1, high_sent, planes * HIGH_ROWS),
    ]

    edge_planes, mine, theirs, *packs = advance_edges(meta, small, bars, pop, cuts)
    received = lax.ppermute(theirs, "vel", partner)
    tiles = list(range(2, row_tiles - 1))
    inside_planes, own = advance_inside(tiles, meta, small, bars, pop, mine)
    from_core = lax.ppermute(own, "vel", partner)
    down, edge, up = split(mine, received, 4 * half)
    from_low = lax.ppermute(up, "space", forward)
    from_high = lax.ppermute(down, "space", backward)
    low_first = lax.ppermute(packs[0], "space", forward)
    high_first = lax.ppermute(packs[1], "space", backward)

    length = own.shape[0] // 2
    begin = core * length
    crossing = lax.dynamic_slice_in_dim(own, begin, length) + lax.dynamic_slice_in_dim(
        from_core, begin, length
    )
    inside_mine = lax.ppermute(crossing, "vel", across)
    inside_other = lax.ppermute(inside_mine, "vel", partner)

    edge_sum = join(edge, from_low, from_high)
    edge_mine = lax.ppermute(edge_sum, "vel", across)
    edge_core = lax.ppermute(edge_sum, "vel", partner)
    edge_other = lax.ppermute(edge_mine, "vel", partner)

    def send_more(rows, axis_pairs, needed):
        return lax.cond(needed, lambda x: lax.ppermute(x, "space", axis_pairs), lambda x: x, rows)

    low_more = send_more(packs[2], forward, jnp.sum(low_need(shift_y)) > low_sent)
    high_more = send_more(packs[3], backward, jnp.sum(high_need(shift_y)) > high_sent)

    out_shape = jax.ShapeDtypeStruct(pop.shape, F32)
    out = relax_inside(
        meta, small, factor, inside_planes, own, from_core, inside_mine, inside_other, out_shape, tiles[0]
    )
    edge_sums = edge_sum, edge_mine, edge_core, edge_other
    halo = low_first, high_first, low_more, high_more
    out = relax_edges(meta, small, factor, bars, edge_planes, edge_sums, halo, cuts, out)
    return out.transpose(0, 1, 3, 2, 4).reshape(planes, row_count, col_count)


def solution(mesh):
    return jax.shard_map(
        per_device,
        mesh=mesh,
        in_specs=(
            P("vel", "space", None),
            P("vel"),
            P("vel"),
            P("vel"),
            P("vel"),
            P("vel"),
            P("vel"),
            P(),
            P(),
        ),
        out_specs=P("vel", "space", None),
        check_vma=False,
    )
```

```python
import functools
import math

import jax
import jax.numpy as jnp
from jax import lax
from jax.experimental import pallas as pl
from jax.experimental.pallas import tpu as pltpu
from jax.sharding import PartitionSpec as P

SPEED_TALLY = 64
CFL = 8
LOW_ROWS = CFL + 1
HIGH_ROWS = CFL
ROW = 8
LANE = 128
PAD = 16
F32 = jnp.float32
LOW_SENT = 72
HIGH_SENT = 64

SMEM_SPEC = pl.BlockSpec(memory_space=pltpu.SMEM)
ANY_SPEC = pl.BlockSpec(memory_space=pl.ANY)
HBM_SPEC = pl.BlockSpec(memory_space=pltpu.HBM)
VMEM_SPEC = pl.BlockSpec(memory_space=pltpu.VMEM)


def params(mebibytes):
    return pltpu.CompilerParams(vmem_limit_bytes=mebibytes * 1024 * 1024)


def low_need(shift):
    return jnp.where(shift >= 0, shift + 1, 0)


def high_need(shift):
    return jnp.where(shift < 0, -shift, 0)


def fill_rows(padded, v, columns, start, count, value):
    block = jnp.full((ROW, LANE), value, F32)
    for t in columns:
        for r in range(start, start + count, ROW):
            padded[v, t, r : r + ROW, :] = block


def prepare_heights(heights_ref, bars):
    lane_tiles = heights_ref.shape[0]
    sublane = lax.broadcasted_iota(jnp.int32, (ROW, LANE), 0)
    for t in range(lane_tiles):
        bars[t] = jnp.broadcast_to(heights_ref[t : t + 1, :], (ROW, LANE)) - sublane


def advect(padded, v, scalars, tiles):
    sx, sy, fx, fy = scalars
    lane_tiles = padded.shape[1] - 2
    lane = lax.broadcasted_iota(jnp.int32, (ROW, LANE), 1)
    near_roll = jnp.where(sx < 0, sx + LANE, sx)
    far_roll = jnp.where(sx + 1 < 0, sx + 1 + LANE, sx + 1)

    def moved(start, t):
        nearer = padded[v, t + 1, pl.ds(start, ROW), :]
        further = padded[v, t + 1, pl.ds(start - 1, ROW), :]
        line = (1.0 - fy) * nearer + fy * further
        return pltpu.roll(line, near_roll, 1), pltpu.roll(line, far_roll, 1)

    def blend(put, t, near, far):
        put(t, (1.0 - fx) * near + fx * far)

    @pl.when(sx >= 0)
    def _():
        own_near, own_far = lane >= sx, lane >= sx + 1
        for begin, put in tiles:
            before = moved(begin - sy, -1)
            for t in range(lane_tiles):
                here = moved(begin - sy, t)
                near = jnp.where(own_near, here[0], before[0])
                blend(put, t, near, jnp.where(own_far, here[1], before[1]))
                before = here

    @pl.when(sx < 0)
    def _():
        own_near, own_far = lane < sx + LANE, lane < sx + 1 + LANE
        for begin, put in tiles:
            here = moved(begin - sy, 0)
            for t in range(lane_tiles):
                after = moved(begin - sy, t + 1)
                near = jnp.where(own_near, here[0], after[0])
                blend(put, t, near, jnp.where(own_far, here[1], after[1]))
                here = after


def store_masked(target, bars, first_row, solid_value):
    def put(t, value):
        target[t] = jnp.where(first_row < bars[t], solid_value, value)

    return put


def velocity(sx_ref, sy_ref, fx_ref, fy_ref, v):
    return sx_ref[v].astype(F32) + fx_ref[v], sy_ref[v].astype(F32) + fy_ref[v]


def sum_moments(planes_ref, k, weights, lane_tile_range):
    sums = [[None] * 4 for _ in lane_tile_range]
    for v, (along_x, along_y) in enumerate(weights):
        square = along_x * along_x + along_y * along_y
        for n, t in enumerate(lane_tile_range):
            f = planes_ref[v, k, t]
            terms = (f, f * along_x, f * along_y, f * square)
            sums[n] = [b if a is None else a + b for a, b in zip(sums[n], terms)]
    return sums


def outer_kernel(cuts, meta_ref, sx_ref, sy_ref, fx_ref, fy_ref, inflow_ref, heights_ref, pop_ref, *refs):
    up_ref, down_ref = refs[:2]
    packs = refs[2 : 2 + len(cuts)]
    frames, outer, up_sums, down_sums, low_pack, high_pack, bars, sem_in, sem_out = refs[2 + len(cuts) :]
    planes, row_tiles, lane_tiles = pop_ref.shape[:3]
    half = lane_tiles // 2
    row0 = meta_ref[0]

    def load(v, i, row, n):
        target = frames.at[v, 1 : 1 + lane_tiles, row : row + ROW, :]
        return pltpu.make_async_copy(pop_ref.at[v, i], target, sem_in.at[v, n])

    def start(v, _):
        up = sy_ref[v] >= 0

        @pl.when(up)
        def _():
            load(v, row_tiles - 2, 8, 0).start()
            load(v, row_tiles - 1, 16, 1).start()

        @pl.when(jnp.logical_not(up))
        def _():
            load(v, 0, 16, 0).start()

        return 0

    lax.fori_loop(0, planes, start, 0)
    prepare_heights(heights_ref, bars)
    row_blocks = 8 * half
    up_sums[row_blocks:] = jnp.zeros((8, ROW, LANE), F32)

    def one(v, offsets):
        low, high = offsets
        value = inflow_ref[v]
        shift = sy_ref[v]
        scalars = sx_ref[v], shift, fx_ref[v], fy_ref[v]
        borders = (0, lane_tiles + 1)
        columns = range(lane_tiles + 2)

        @pl.when(shift >= 0)
        def _():
            fill_rows(frames, v, borders, 8, 16, value)
            fill_rows(frames, v, columns, 24, 8, 0.0)
            load(v, row_tiles - 2, 8, 0).wait()
            load(v, row_tiles - 1, 16, 1).wait()
            for t in range(lane_tiles):
                low_pack[t, pl.ds(low, 8), :] = frames[v, t + 1, pl.ds(23 - shift, 8), :]

        @pl.when(shift < 0)
        def _():
            fill_rows(frames, v, borders, 16, 8, value)
            fill_rows(frames, v, columns, 8, 8, 0.0)
            load(v, 0, 16, 0).wait()
            for t in range(lane_tiles):
                high_pack[t, pl.ds(high, 8), :] = frames[v, t + 1, 16:24, :]

        first_row = row0 + jnp.where(shift >= 0, ROW * row_tiles, -ROW)
        begin = jnp.where(shift >= 0, 24, 8)
        advect(frames, v, scalars, [(begin, store_masked(outer.at[v], bars, first_row, 0.0))])

        @pl.when(shift == CFL)
        def _():
            along_x, along_y = velocity(sx_ref, sy_ref, fx_ref, fy_ref, v)
            factors = 1.0, along_x, along_y, along_x * along_x + along_y * along_y

            def put(t, value):
                row = jnp.where(row0 + ROW * (row_tiles + 1) < bars[t], 0.0, value)
                for m in range(4):
                    n, r = row_blocks + 2 * m + t // ROW, t % ROW
                    up_sums[n, r : r + 1, :] = up_sums[n, r : r + 1, :] + (row * factors[m])[0:1, :]

            advect(frames, v, scalars, [(32, put)])
            for t in range(lane_tiles):
                low_pack[t, pl.ds(low + 8, 1), :] = frames[v, t + 1, 23:24, :]

        return low + low_need(shift), high + high_need(shift)

    lax.fori_loop(0, planes, one, (jnp.int32(0), jnp.int32(0)))

    for h in range(2):
        for rising, sums_ref in ((True, up_sums), (False, down_sums)):
            for part in range(2):
                tiles = range(h * half + part * half // 2, h * half + (part + 1) * half // 2)
                sums = [[None] * 4 for _ in tiles]
                for v in range(planes):
                    along_x, along_y = velocity(sx_ref, sy_ref, fx_ref, fy_ref, v)
                    goes = jnp.where((sy_ref[v] >= 0) == rising, 1.0, 0.0)
                    square = (along_x * along_x + along_y * along_y) * goes
                    factors = goes, along_x * goes, along_y * goes, square
                    for n, t in enumerate(tiles):
                        f = outer[v, t]
                        terms = [f * w for w in factors]
                        sums[n] = [b if a is None else a + b for a, b in zip(sums[n], terms)]
                for n, t in enumerate(tiles):
                    for m in range(4):
                        sums_ref[(h * 4 + m) * half + t - h * half] = sums[n][m]
    copies = [
        pltpu.make_async_copy(up_sums, up_ref, sem_out.at[0]),
        pltpu.make_async_copy(down_sums, down_ref, sem_out.at[1]),
    ]
    for n, (pack, begin, end) in enumerate(cuts):
        source = (low_pack, high_pack)[pack].at[:, begin:end, :]
        copies.append(pltpu.make_async_copy(source, packs[n], sem_out.at[2 + n]))
    for copy in copies:
        copy.start()
    for copy in copies:
        copy.wait()


def outer_rows(meta, small, heights, pop, cuts):
    planes, row_tiles, lane_tiles = pop.shape[:3]
    blocks = 4 * lane_tiles
    return pl.pallas_call(
        functools.partial(outer_kernel, cuts),
        out_shape=[
            jax.ShapeDtypeStruct((blocks + 8, ROW, LANE), F32),
            jax.ShapeDtypeStruct((blocks, ROW, LANE), F32),
        ]
        + [jax.ShapeDtypeStruct((lane_tiles, end - begin, LANE), F32) for _, begin, end in cuts],
        in_specs=[SMEM_SPEC] * 6 + [VMEM_SPEC, HBM_SPEC],
        out_specs=[ANY_SPEC] * (2 + len(cuts)),
        scratch_shapes=[
            pltpu.VMEM((planes, lane_tiles + 2, 40, LANE), F32),
            pltpu.VMEM((planes, lane_tiles, ROW, LANE), F32),
            pltpu.VMEM((blocks + 8, ROW, LANE), F32),
            pltpu.VMEM((blocks, ROW, LANE), F32),
            pltpu.VMEM((lane_tiles, planes * LOW_ROWS + 16, LANE), F32),
            pltpu.VMEM((lane_tiles, planes * HIGH_ROWS + 16, LANE), F32),
            pltpu.VMEM((lane_tiles, ROW, LANE), jnp.int32),
            pltpu.SemaphoreType.DMA((planes, 2)),
            pltpu.SemaphoreType.DMA((2 + len(cuts),)),
        ],
        compiler_params=params(20),
        name="outer_rows",
    )(meta, *small[:5], heights, pop)


def advance_kernel(tiles, raw_tiles, edges, meta_ref, sx_ref, sy_ref, fx_ref, fy_ref, inflow_ref,
                   wall_ref, heights_ref, pop_ref, _, planes_ref, sums_ref, padded, bars, sem_in):
    planes, row_tiles, lane_tiles = pop_ref.shape[:3]
    half = lane_tiles // 2
    count = len(tiles)
    rows = row_tiles * ROW
    row0, first, last = (meta_ref[i] for i in range(3))

    def loads(v):
        return [
            pltpu.make_async_copy(
                pop_ref.at[v, i],
                padded.at[v, 1 : 1 + lane_tiles, PAD + ROW * i : PAD + ROW * (i + 1), :],
                sem_in.at[v, n],
            )
            for n, i in enumerate(raw_tiles)
        ]

    def start(v, _):
        for load in loads(v):
            load.start()
        return 0

    lax.fori_loop(0, planes, start, 0)
    prepare_heights(heights_ref, bars)

    def one(v, _):
        value = inflow_ref[v]
        for i in raw_tiles:
            fill_rows(padded, v, (0, lane_tiles + 1), PAD + ROW * i, ROW, value)
        if edges:
            columns = range(lane_tiles + 2)
            fill_rows(padded, v, columns, 0, PAD, jnp.where(first == 1, value, 0.0))
            fill_rows(padded, v, columns, PAD + rows, ROW, jnp.where(last == 1, value, 0.0))
        for load in loads(v):
            load.wait()
        scalars = sx_ref[v], sy_ref[v], fx_ref[v], fy_ref[v]
        work = [
            (PAD + ROW * j, store_masked(planes_ref.at[v, k], bars, row0 + ROW * j, wall_ref[v]))
            for k, j in enumerate(tiles)
        ]
        advect(padded, v, scalars, work)
        return 0

    lax.fori_loop(0, planes, one, 0)
    weights = [velocity(sx_ref, sy_ref, fx_ref, fy_ref, v) for v in range(planes)]

    def step(k, _):
        for h in range(2):
            sums = sum_moments(planes_ref, k, weights, range(h * half, (h + 1) * half))
            for t in range(half):
                for m in range(4):
                    sums_ref[((h * count + k) * 4 + m) * half + t] = sums[t][m]
        return 0

    lax.fori_loop(0, count, step, 0)


def advance(tiles, edges, meta, small, heights, pop, after):
    planes, row_tiles, lane_tiles = pop.shape[:3]
    count = len(tiles)
    raw_tiles = sorted({i for j in tiles for i in range(j - 2, j + 2) if 0 <= i < row_tiles})
    blocks = 4 * lane_tiles * count
    return pl.pallas_call(
        functools.partial(advance_kernel, tiles, raw_tiles, edges),
        out_shape=[
            pltpu.VMEM((planes, count, lane_tiles, ROW, LANE), F32),
            jax.ShapeDtypeStruct((blocks, ROW, LANE), F32),
        ],
        in_specs=[SMEM_SPEC] * 7 + [VMEM_SPEC, HBM_SPEC, ANY_SPEC],
        out_specs=[VMEM_SPEC] * 2,
        scratch_shapes=[
            pltpu.VMEM((planes, lane_tiles + 2, PAD + row_tiles * ROW + ROW, LANE), F32),
            pltpu.VMEM((lane_tiles, ROW, LANE), jnp.int32),
            pltpu.SemaphoreType.DMA((planes, len(raw_tiles))),
        ],
        compiler_params=params(20),
        name="advance_edges" if edges else "advance_inside",
    )(meta, *small, heights, pop, after)


def join_kernel(own_ref, low_ref, high_ref, out_ref):
    half = high_ref.shape[0] // 8
    size = 4 * half
    top = lax.broadcasted_iota(jnp.int32, (ROW, LANE), 0) == 0
    for h in range(2):
        base = h * 3 * size
        own = slice(base, base + size)
        out_ref[own] = own_ref[own] + low_ref[h * size : (h + 1) * size]
        own = slice(base + 2 * size, base + 3 * size)
        out_ref[own] = own_ref[own] + high_ref[h * size : (h + 1) * size]
        for m in range(4):
            for n in range(half):
                t = h * half + n
                row = low_ref[8 * half + 2 * m + t // ROW, t % ROW : t % ROW + 1, :]
                index = base + size + m * half + n
                part = jnp.where(top, jnp.broadcast_to(row, (ROW, LANE)), 0.0)
                out_ref[index] = own_ref[index] + part


def join(own, from_low, from_high):
    return pl.pallas_call(
        join_kernel,
        out_shape=jax.ShapeDtypeStruct(own.shape, F32),
        in_specs=[VMEM_SPEC] * 3,
        out_specs=VMEM_SPEC,
        compiler_params=params(8),
        name="join_edges",
    )(own, from_low, from_high)


def fold_kernel(meta_ref, own_ref, core_ref, out_ref):
    length = out_ref.shape[0]
    half = pl.ds(meta_ref[3] * length, length)
    out_ref[...] = own_ref[half] + core_ref[half]


def fold(meta, own, from_core):
    return pl.pallas_call(
        fold_kernel,
        out_shape=jax.ShapeDtypeStruct((own.shape[0] // 2, ROW, LANE), F32),
        in_specs=[SMEM_SPEC] + [VMEM_SPEC] * 2,
        out_specs=VMEM_SPEC,
        compiler_params=params(8),
        name="fold_half",
    )(meta, own, from_core)


def overflow_kernel(limits, sy_ref, *refs):
    low, high = low_need(sy_ref[0]), high_need(sy_ref[0])
    for v in range(1, sy_ref.shape[0]):
        low, high = low + low_need(sy_ref[v]), high + high_need(sy_ref[v])
    refs[-1][0] = jnp.where((low > limits[0]) | (high > limits[1]), 1, 0)


def overflow(shift_y, limits, after):
    return pl.pallas_call(
        functools.partial(overflow_kernel, limits),
        out_shape=jax.ShapeDtypeStruct((1,), jnp.int32),
        in_specs=[SMEM_SPEC] + [ANY_SPEC] * len(after),
        out_specs=SMEM_SPEC,
        compiler_params=params(8),
        name="overflow",
    )(shift_y, *after)[0]


def profile(density, flux_x, flux_y, energy, factor):
    inverse = 1.0 / density
    mean_x = flux_x * inverse
    mean_y = flux_y * inverse
    temperature = 0.5 * (energy * inverse - mean_x * mean_x - mean_y * mean_y)
    rate = 1.0 - jnp.exp(-factor * density / (SPEED_TALLY * jnp.sqrt(temperature)))
    height = rate * (density / (2.0 * math.pi * temperature))
    return mean_x, mean_y, -0.5 / temperature, height, 1.0 - rate


def relax_cells(get, put, values, factor, weights):
    mean_x, mean_y, scale, height, keep = profile(*values, factor)
    for v, (along_x, along_y) in enumerate(weights):
        gap_x = along_x - mean_x
        gap_y = along_y - mean_y
        state = height * jnp.exp((gap_x * gap_x + gap_y * gap_y) * scale)
        put(v, keep * get(v) + state)


def relax_tile(planes_ref, out_buf, sums, core, factor, weights, k, h, count):
    own_ref, core_ref, mine_ref, other_ref = sums
    half = planes_ref.shape[2] // 2
    for n in range(half):
        t = h * half + n
        values = []
        for m in range(4):
            near = ((h * count + k) * 4 + m) * half + n
            far = (k * 4 + m) * half + n
            across = jnp.where(core == h, mine_ref[far], other_ref[far])
            values.append(own_ref[near] + core_ref[near] + across)

        def put(v, value):
            out_buf[v, k, t] = value

        relax_cells(lambda v: planes_ref[v, k, t], put, values, factor, weights)


def relax_kernel(first_tile, meta_ref, sx_ref, sy_ref, fx_ref, fy_ref, factor_ref, planes_ref, s0, s1, s2,
                 s3, *refs):
    out_ref, out_buf, sem_out = refs[-3:]
    planes, count, lane_tiles = planes_ref.shape[:3]
    half = lane_tiles // 2
    weights = [velocity(sx_ref, sy_ref, fx_ref, fy_ref, v) for v in range(planes)]

    def out_copy(k, h):
        lanes = pl.ds(h * half, half)
        return pltpu.make_async_copy(
            out_buf.at[:, k, lanes], out_ref.at[:, first_tile + k, lanes], sem_out.at[2 * k + h]
        )

    def step(k, _):
        for h in range(2):
            relax_tile(
                planes_ref, out_buf, (s0, s1, s2, s3), meta_ref[3], factor_ref[0], weights, k, h, count
            )
            out_copy(k, h).start()
        return 0

    lax.fori_loop(0, count, step, 0)
    for k in range(count):
        for h in range(2):
            out_copy(k, h).wait()


def relax_inside(meta, small, factor, planes_part, sums, out, out_shape, first_tile):
    planes, count, lane_tiles = planes_part.shape[:3]
    planes_part = pltpu.with_memory_space_constraint(planes_part, pltpu.VMEM)
    operands = [meta, *small[:4], factor, planes_part, *sums]
    in_specs = [SMEM_SPEC] * 6 + [VMEM_SPEC] * 5
    aliases = {}
    if out is not None:
        aliases = {len(operands): 0}
        operands.append(out)
        in_specs.append(HBM_SPEC)
    return pl.pallas_call(
        functools.partial(relax_kernel, first_tile),
        out_shape=out_shape,
        in_specs=in_specs,
        out_specs=HBM_SPEC,
        scratch_shapes=[
            pltpu.VMEM((planes, count, lane_tiles, ROW, LANE), F32),
            pltpu.SemaphoreType.DMA((2 * count,)),
        ],
        input_output_aliases=aliases,
        compiler_params=params(20),
        name="relax_inside",
    )(*operands)


def relax_edges_kernel(cuts, meta_ref, sx_ref, sy_ref, fx_ref, fy_ref, inflow_ref, factor_ref,
                       heights_ref, planes_ref, s0, s1, s2, s3, *refs):
    pack_refs = refs[: len(cuts)]
    _, out_ref, frames, out_buf, low_buf, high_buf, bars, sem_in, sem_out = refs[len(cuts) :]
    planes, _, lane_tiles = planes_ref.shape[:3]
    row_tiles = out_ref.shape[1]
    half = lane_tiles // 2
    row0, first, last, core = (meta_ref[i] for i in range(4))
    needs = [low_need(sy_ref[0]), high_need(sy_ref[0])]
    for v in range(1, planes):
        needs = [needs[0] + low_need(sy_ref[v]), needs[1] + high_need(sy_ref[v])]

    def pack_copy(n):
        pack, begin, end = cuts[n]
        target = (low_buf, high_buf)[pack].at[:, 16 + begin : 16 + end, :]
        return pltpu.make_async_copy(pack_refs[n], target, sem_in.at[n])

    for n in range(len(cuts)):
        pl.when(needs[cuts[n][0]] > cuts[n][1])(lambda n=n: pack_copy(n).start())
    prepare_heights(heights_ref, bars)
    for n in range(len(cuts)):
        pl.when(needs[cuts[n][0]] > cuts[n][1])(lambda n=n: pack_copy(n).wait())

    def add_masked(v, k, first_row):
        def put(t, value):
            out_buf[v, k, t] = planes_ref[v, k, t] + jnp.where(first_row < bars[t], 0.0, value)

        return put

    def keep(v, k):
        for t in range(lane_tiles):
            out_buf[v, k, t] = planes_ref[v, k, t]

    def one(v, offsets):
        low, high = offsets
        value = inflow_ref[v]
        shift = sy_ref[v]
        up = shift >= 0
        scalars = sx_ref[v], shift, fx_ref[v], fy_ref[v]
        borders = (0, lane_tiles + 1)
        columns = range(lane_tiles + 2)
        from_low = up & (first == 0)
        from_high = jnp.logical_not(up) & (last == 0)
        reaches_second = from_low & (shift == CFL)

        @pl.when(from_low)
        def _():
            fill_rows(frames, v, borders, 8, 16, value)
            fill_rows(frames, v, columns, 24, 16, 0.0)
            for t in range(lane_tiles):
                for r in range(0, 16, ROW):
                    piece = low_buf[t, pl.ds(low + shift + 1 + r, ROW), :]
                    frames[v, t + 1, 8 + r : 8 + r + ROW, :] = piece
            advect(frames, v, scalars, [(24, add_masked(v, 0, row0))])

        @pl.when(from_high)
        def _():
            fill_rows(frames, v, borders, 32, 8, value)
            fill_rows(frames, v, columns, 16, 16, 0.0)
            for t in range(lane_tiles):
                frames[v, t + 1, 32:40, :] = high_buf[t, pl.ds(16 + high, ROW), :]
            first_row = row0 + ROW * (row_tiles - 1)
            advect(frames, v, scalars, [(24, add_masked(v, 2, first_row))])

        @pl.when(reaches_second)
        def _():
            advect(frames, v, scalars, [(32, add_masked(v, 1, row0 + ROW))])

        pl.when(jnp.logical_not(from_low))(lambda: keep(v, 0))
        pl.when(jnp.logical_not(reaches_second))(lambda: keep(v, 1))
        pl.when(jnp.logical_not(from_high))(lambda: keep(v, 2))
        return low + low_need(shift), high + high_need(shift)

    lax.fori_loop(0, planes, one, (jnp.int32(0), jnp.int32(0)))
    weights = [velocity(sx_ref, sy_ref, fx_ref, fy_ref, v) for v in range(planes)]

    def out_copy(k, h):
        j = jnp.where(k < 2, k, row_tiles - 1)
        lanes = pl.ds(h * half, half)
        return pltpu.make_async_copy(
            out_buf.at[:, k, lanes], out_ref.at[:, j, lanes], sem_out.at[2 * k + h]
        )

    def step(k, _):
        for h in range(2):
            relax_tile(out_buf, out_buf, (s0, s1, s2, s3), core, factor_ref[0], weights, k, h, 3)
            out_copy(k, h).start()
        return 0

    lax.fori_loop(0, 3, step, 0)
    for k in range(3):
        for h in range(2):
            out_copy(k, h).wait()


def relax_edges(meta, small, factor, heights, planes_part, sums, packs, cuts, out):
    planes, _, lane_tiles = planes_part.shape[:3]
    planes_part = pltpu.with_memory_space_constraint(planes_part, pltpu.VMEM)
    operands = [meta, *small[:5], factor, heights, planes_part, *sums, *packs, out]
    return pl.pallas_call(
        functools.partial(relax_edges_kernel, cuts),
        out_shape=jax.ShapeDtypeStruct(out.shape, F32),
        in_specs=[SMEM_SPEC] * 7
        + [VMEM_SPEC] * 6
        + [ANY_SPEC] * len(cuts)
        + [HBM_SPEC],
        out_specs=HBM_SPEC,
        scratch_shapes=[
            pltpu.VMEM((planes, lane_tiles + 2, 48, LANE), F32),
            pltpu.VMEM((planes, 3, lane_tiles, ROW, LANE), F32),
            pltpu.VMEM((lane_tiles, planes * LOW_ROWS + 32, LANE), F32),
            pltpu.VMEM((lane_tiles, planes * HIGH_ROWS + 32, LANE), F32),
            pltpu.VMEM((lane_tiles, ROW, LANE), jnp.int32),
            pltpu.SemaphoreType.DMA((len(cuts),)),
            pltpu.SemaphoreType.DMA((6,)),
        ],
        input_output_aliases={len(operands) - 1: 0},
        compiler_params=params(20),
        name="relax_edges",
    )(*operands)


def per_device(populations, shift_x, shift_y, frac_x, frac_y, inflow, wall_state, heights,
               impact_frequency_factor):
    planes, row_count, col_count = populations.shape
    space_count, vel_count = lax.axis_size("space"), lax.axis_size("vel")
    row_tiles, lane_tiles = row_count // ROW, col_count // LANE
    space, vel = lax.axis_index("space"), lax.axis_index("vel")
    forward = [(i, i + 1) for i in range(space_count - 1)]
    backward = [(target, source) for source, target in forward]
    partner = [(i, i ^ 1) for i in range(vel_count)]
    across = [(i, i ^ 2) for i in range(vel_count)]

    meta = jnp.stack([space * row_count, space == 0, space == space_count - 1, vel % 2]).astype(jnp.int32)
    small = (shift_x, shift_y, frac_x, frac_y, inflow, wall_state)
    factor = impact_frequency_factor.reshape(1)
    bars = heights.reshape(lane_tiles, LANE)
    pop = populations.reshape(planes, row_tiles, ROW, lane_tiles, LANE).transpose(0, 1, 3, 2, 4)
    pop = pltpu.with_memory_space_constraint(pop, pltpu.HBM)
    low_sent, high_sent = min(LOW_SENT, planes * LOW_ROWS), min(HIGH_SENT, planes * HIGH_ROWS)
    cuts = [
        (0, 0, low_sent),
        (1, 0, high_sent),
        (0, low_sent, planes * LOW_ROWS),
        (1, high_sent, planes * HIGH_ROWS),
    ]

    up, down, *packs = outer_rows(meta, small, bars, pop, cuts)
    from_low = lax.ppermute(up, "space", forward)
    from_high = lax.ppermute(down, "space", backward)
    low_first = lax.ppermute(packs[0], "space", forward)
    high_first = lax.ppermute(packs[1], "space", backward)

    def total(own):
        from_core = lax.ppermute(own, "vel", partner)
        mine = lax.ppermute(fold(meta, own, from_core), "vel", across)
        return own, from_core, mine, lax.ppermute(mine, "vel", partner)

    middle = row_tiles // 2
    chunks = [list(range(2, middle)), list(range(middle, row_tiles - 1))]
    parts = []
    after = up
    for tiles in chunks:
        planes_part, own = advance(tiles, False, meta, small, bars, pop, after)
        parts.append((tiles[0], planes_part, total(own)))
        after = own
    edge_planes, own = advance([0, 1, row_tiles - 1], True, meta, small, bars, pop, after)
    edge_sums = total(join(own, from_low, from_high))

    out_shape = jax.ShapeDtypeStruct(pop.shape, F32)
    out = None
    for first_tile, planes_part, sums in parts:
        out = relax_inside(meta, small, factor, planes_part, sums, out, out_shape, first_tile)
    needed = overflow(shift_y, (low_sent, high_sent), (low_first, high_first, edge_sums[3]))

    def send_more(low, high):
        return lax.ppermute(low, "space", forward), lax.ppermute(high, "space", backward)

    more = lax.cond(needed > 0, send_more, lambda low, high: (low, high), packs[2], packs[3])
    halo = low_first, high_first, *more
    out = relax_edges(meta, small, factor, bars, edge_planes, edge_sums, halo, cuts, out)
    return out.transpose(0, 1, 3, 2, 4).reshape(planes, row_count, col_count)


def solution(mesh):
    return jax.shard_map(
        per_device,
        mesh=mesh,
        in_specs=(
            P("vel", "space", None),
            P("vel"),
            P("vel"),
            P("vel"),
            P("vel"),
            P("vel"),
            P("vel"),
            P(),
            P(),
        ),
        out_specs=P("vel", "space", None),
        check_vma=False,
    )
```

```python
import functools
import math

import jax
import jax.numpy as jnp
from jax import lax
from jax.experimental import pallas as pl
from jax.experimental.pallas import tpu as pltpu
from jax.sharding import PartitionSpec as P

SPEED_TALLY = 64
CFL = 8
LOW_ROWS = CFL + 1
HIGH_ROWS = CFL
ROW = 8
LANE = 128
PAD = 16
F32 = jnp.float32
LOW_SENT = 72
HIGH_SENT = 72

SMEM_SPEC = pl.BlockSpec(memory_space=pltpu.SMEM)
ANY_SPEC = pl.BlockSpec(memory_space=pl.ANY)
HBM_SPEC = pl.BlockSpec(memory_space=pltpu.HBM)
VMEM_SPEC = pl.BlockSpec(memory_space=pltpu.VMEM)


def params(mebibytes):
    return pltpu.CompilerParams(vmem_limit_bytes=mebibytes * 1024 * 1024)


def low_need(shift):
    return jnp.where(shift >= 0, shift + 1, 0)


def high_need(shift):
    return jnp.where(shift < 0, -shift, 0)


def fill_rows(padded, v, columns, start, count, value):
    block = jnp.full((ROW, LANE), value, F32)
    for t in columns:
        for r in range(start, start + count, ROW):
            padded[v, t, r : r + ROW, :] = block


def prepare_heights(heights_ref, bars):
    lane_tiles = heights_ref.shape[0]
    sublane = lax.broadcasted_iota(jnp.int32, (ROW, LANE), 0)
    for t in range(lane_tiles):
        bars[t] = jnp.broadcast_to(heights_ref[t : t + 1, :], (ROW, LANE)) - sublane


def advect(padded, v, scalars, tiles):
    sx, sy, fx, fy = scalars
    lane_tiles = padded.shape[1] - 2
    lane = lax.broadcasted_iota(jnp.int32, (ROW, LANE), 1)
    near_roll = jnp.where(sx < 0, sx + LANE, sx)
    far_roll = jnp.where(sx + 1 < 0, sx + 1 + LANE, sx + 1)

    def moved(start, t):
        nearer = padded[v, t + 1, pl.ds(start, ROW), :]
        further = padded[v, t + 1, pl.ds(start - 1, ROW), :]
        line = (1.0 - fy) * nearer + fy * further
        return pltpu.roll(line, near_roll, 1), pltpu.roll(line, far_roll, 1)

    def blend(put, t, near, far):
        put(t, (1.0 - fx) * near + fx * far)

    @pl.when(sx >= 0)
    def _():
        own_near, own_far = lane >= sx, lane >= sx + 1
        for begin, put in tiles:
            before = moved(begin - sy, -1)
            for t in range(lane_tiles):
                here = moved(begin - sy, t)
                near = jnp.where(own_near, here[0], before[0])
                blend(put, t, near, jnp.where(own_far, here[1], before[1]))
                before = here

    @pl.when(sx < 0)
    def _():
        own_near, own_far = lane < sx + LANE, lane < sx + 1 + LANE
        for begin, put in tiles:
            here = moved(begin - sy, 0)
            for t in range(lane_tiles):
                after = moved(begin - sy, t + 1)
                near = jnp.where(own_near, here[0], after[0])
                blend(put, t, near, jnp.where(own_far, here[1], after[1]))
                here = after


def store_masked(target, bars, first_row, solid_value):
    def put(t, value):
        target[t] = jnp.where(first_row < bars[t], solid_value, value)

    return put


def velocity(sx_ref, sy_ref, fx_ref, fy_ref, v):
    return sx_ref[v].astype(F32) + fx_ref[v], sy_ref[v].astype(F32) + fy_ref[v]


def sum_moments(planes_ref, k, weights, lane_tile_range):
    sums = [[None] * 4 for _ in lane_tile_range]
    for v, (along_x, along_y) in enumerate(weights):
        square = along_x * along_x + along_y * along_y
        for n, t in enumerate(lane_tile_range):
            f = planes_ref[v, k, t]
            terms = (f, f * along_x, f * along_y, f * square)
            sums[n] = [b if a is None else a + b for a, b in zip(sums[n], terms)]
    return sums


class Plan:
    def __init__(self, row_tiles, half):
        self.tile = 4 * half
        self.inside = list(range(2, row_tiles - 2))
        self.sizes = [self.tile + 4, self.tile, len(self.inside) * self.tile, 2 * self.tile, 2 * self.tile]
        self.starts = [sum(self.sizes[:n]) for n in range(len(self.sizes) + 1)]
        self.row_tiles = row_tiles

    def start(self, j):
        low = self.starts[3] + self.tile * j
        high = self.starts[4] + self.tile * (j - self.row_tiles + 2)
        inside = self.starts[2] + self.tile * (j - 2)
        return jnp.where(j < 2, low, jnp.where(j >= self.row_tiles - 2, high, inside))


def advance_kernel(plan, cuts, group, meta_ref, sx_ref, sy_ref, fx_ref, fy_ref, inflow_ref, wall_ref,
                   heights_ref, pop_ref, *refs):
    planes_ref, mine_ref, theirs_ref = refs[:3]
    packs = refs[3 : 3 + len(cuts)]
    (padded, planes_buf, outer, moments, low_pack, high_pack, bars, sem_in, sem_planes, sem_out) = refs[
        3 + len(cuts) :
    ]
    planes, row_tiles, lane_tiles = pop_ref.shape[:3]
    half = lane_tiles // 2
    rows = row_tiles * ROW
    row0, first, last, core = (meta_ref[i] for i in range(4))

    def loads(g):
        members = pl.ds(g * group, group)
        return [
            pltpu.make_async_copy(
                pop_ref.at[members, i],
                padded.at[members, 1 : 1 + lane_tiles, PAD + ROW * i : PAD + ROW * (i + 1), :],
                sem_in.at[g, i],
            )
            for i in range(row_tiles)
        ]

    def start(g, _):
        for load in loads(g):
            load.start()
        return 0

    lax.fori_loop(0, planes // group, start, 0)
    prepare_heights(heights_ref, bars)
    for slot in range(2):
        moments[slot, plan.tile : plan.tile + 4] = jnp.zeros((4, ROW, LANE), F32)

    def out_copy(v):
        return pltpu.make_async_copy(planes_buf.at[v], planes_ref.at[v], sem_planes.at[v])

    def one(v, offsets):
        low, high = offsets
        value = inflow_ref[v]
        shift = sy_ref[v]
        up = shift >= 0
        columns = range(lane_tiles + 2)
        fill_rows(padded, v, (0, lane_tiles + 1), PAD, rows, value)
        fill_rows(padded, v, columns, 0, PAD, jnp.where(first == 1, value, 0.0))
        fill_rows(padded, v, columns, PAD + rows, ROW, jnp.where(last == 1, value, 0.0))

        @pl.when(v % group == 0)
        def _():
            for load in loads(v // group):
                load.wait()

        scalars = sx_ref[v], shift, fx_ref[v], fy_ref[v]
        work = [
            (PAD + ROW * j, store_masked(planes_buf.at[v, j], bars, row0 + ROW * j, wall_ref[v]))
            for j in range(row_tiles)
        ]
        beyond = jnp.where(up, rows, -ROW)
        work.append((PAD + beyond, store_masked(outer.at[v], bars, row0 + beyond, 0.0)))
        advect(padded, v, scalars, work)
        out_copy(v).start()

        @pl.when(shift == CFL)
        def _():
            along_x, along_y = velocity(sx_ref, sy_ref, fx_ref, fy_ref, v)
            factors = 1.0, along_x, along_y, along_x * along_x + along_y * along_y

            def put(t, value):
                row = jnp.where(row0 + rows + ROW < bars[t], 0.0, value)
                slot, r = jnp.bitwise_xor(core, t // half), t % half
                for m in range(4):
                    n = plan.tile + m
                    total = moments[slot, n, r : r + 1, :] + (row * factors[m])[0:1, :]
                    moments[slot, n, r : r + 1, :] = total

            advect(padded, v, scalars, [(PAD + rows + ROW, put)])
            for t in range(lane_tiles):
                low_pack[t, pl.ds(low + 8, 1), :] = padded[v, t + 1, PAD + rows - 1 : PAD + rows, :]

        @pl.when(up)
        def _():
            for t in range(lane_tiles):
                source = pl.ds(PAD + rows - 1 - shift, 8)
                low_pack[t, pl.ds(low, 8), :] = padded[v, t + 1, source, :]

        @pl.when(shift == CFL)
        def _():
            for t in range(lane_tiles):
                low_pack[t, pl.ds(low + 8, 1), :] = padded[v, t + 1, PAD + rows - 1 : PAD + rows, :]

        @pl.when(jnp.logical_not(up))
        def _():
            for t in range(lane_tiles):
                high_pack[t, pl.ds(high, 8), :] = padded[v, t + 1, PAD : PAD + 8, :]

        return low + low_need(shift), high + high_need(shift)

    lax.fori_loop(0, planes, one, (jnp.int32(0), jnp.int32(0)))
    packing = []
    for n, (pack, begin, end) in enumerate(cuts):
        source = (low_pack, high_pack)[pack].at[:, begin:end, :]
        packing.append(pltpu.make_async_copy(source, packs[n], sem_out.at[2 + n]))
        packing[-1].start()

    for h in range(2):
        slot = jnp.bitwise_xor(core, h)
        for rising in (True, False):
            for part in range(2):
                tiles = range(h * half + part * half // 2, h * half + (part + 1) * half // 2)
                sums = [[None] * 4 for _ in tiles]
                for v in range(planes):
                    along_x, along_y = velocity(sx_ref, sy_ref, fx_ref, fy_ref, v)
                    goes = jnp.where((sy_ref[v] >= 0) == rising, 1.0, 0.0)
                    square = (along_x * along_x + along_y * along_y) * goes
                    factors = goes, along_x * goes, along_y * goes, square
                    for n, t in enumerate(tiles):
                        f = outer[v, t]
                        terms = [f * w for w in factors]
                        sums[n] = [b if a is None else a + b for a, b in zip(sums[n], terms)]
                begin = plan.starts[0 if rising else 1]
                for n, t in enumerate(tiles):
                    for m in range(4):
                        moments[slot, begin + m * half + t - h * half] = sums[n][m]
    weights = [velocity(sx_ref, sy_ref, fx_ref, fy_ref, v) for v in range(planes)]

    def step(j, _):
        begin = plan.start(j)
        for h in range(2):
            sums = sum_moments(planes_buf, j, weights, range(h * half, (h + 1) * half))
            slot = jnp.bitwise_xor(core, h)
            for t in range(half):
                for m in range(4):
                    moments[slot, begin + m * half + t] = sums[t][m]
        return 0

    lax.fori_loop(0, row_tiles, step, 0)
    copies = [
        pltpu.make_async_copy(moments.at[1], theirs_ref, sem_out.at[1]),
        pltpu.make_async_copy(moments.at[0], mine_ref, sem_out.at[0]),
    ]
    for copy in copies:
        copy.start()

    def finish(v, _):
        out_copy(v).wait()
        return 0

    lax.fori_loop(0, planes, finish, 0)
    for copy in packing + copies:
        copy.wait()


def advance(plan, meta, small, heights, pop, cuts):
    planes, row_tiles, lane_tiles = pop.shape[:3]
    group = math.gcd(planes, 4)
    blocks = plan.starts[-1]
    half_sums = jax.ShapeDtypeStruct((blocks, ROW, LANE), F32)
    return pl.pallas_call(
        functools.partial(advance_kernel, plan, cuts, group),
        out_shape=[jax.ShapeDtypeStruct(pop.shape, F32), half_sums, half_sums]
        + [jax.ShapeDtypeStruct((lane_tiles, end - begin, LANE), F32) for _, begin, end in cuts],
        in_specs=[SMEM_SPEC] * 7 + [VMEM_SPEC, ANY_SPEC],
        out_specs=[ANY_SPEC] * (3 + len(cuts)),
        scratch_shapes=[
            pltpu.VMEM((planes, lane_tiles + 2, PAD + row_tiles * ROW + ROW, LANE), F32),
            pltpu.VMEM((planes, row_tiles, lane_tiles, ROW, LANE), F32),
            pltpu.VMEM((planes, lane_tiles, ROW, LANE), F32),
            pltpu.VMEM((2, blocks, ROW, LANE), F32),
            pltpu.VMEM((lane_tiles, planes * LOW_ROWS + 16, LANE), F32),
            pltpu.VMEM((lane_tiles, planes * HIGH_ROWS + 16, LANE), F32),
            pltpu.VMEM((lane_tiles, ROW, LANE), jnp.int32),
            pltpu.SemaphoreType.DMA((planes // group, row_tiles)),
            pltpu.SemaphoreType.DMA((planes,)),
            pltpu.SemaphoreType.DMA((2 + len(cuts),)),
        ],
        compiler_params=params(58),
        name="advance",
    )(meta, *small, heights, pop)


def fold_kernel(mine_ref, received_ref, *out_refs):
    begin = 0
    for ref in out_refs:
        n = ref.shape[0]
        ref[...] = mine_ref[begin : begin + n] + received_ref[begin : begin + n]
        begin += n


def fold(mine, received, sizes):
    return pl.pallas_call(
        fold_kernel,
        out_shape=[jax.ShapeDtypeStruct((n, ROW, LANE), F32) for n in sizes],
        in_specs=[VMEM_SPEC] * 2,
        out_specs=[VMEM_SPEC] * len(sizes),
        compiler_params=params(8),
        name="fold",
    )(mine, received)


def join_low_kernel(own_ref, low_ref, out_ref):
    tile = own_ref.shape[0] // 2
    half = tile // 4
    out_ref[:tile] = own_ref[:tile] + low_ref[:tile]
    top = lax.broadcasted_iota(jnp.int32, (ROW, LANE), 0) == 0
    for m in range(4):
        for n in range(half):
            row = jnp.broadcast_to(low_ref[tile + m, n : n + 1, :], (ROW, LANE))
            index = tile + m * half + n
            out_ref[index] = own_ref[index] + jnp.where(top, row, 0.0)


def add_kernel(a_ref, b_ref, out_ref):
    out_ref[...] = a_ref[...] + b_ref[...]


def join_high_kernel(own_ref, high_ref, out_ref):
    tile = high_ref.shape[0]
    out_ref[:tile] = own_ref[:tile]
    out_ref[tile:] = own_ref[tile:] + high_ref[...]


def small_call(kernel, name, *operands):
    return pl.pallas_call(
        kernel,
        out_shape=jax.ShapeDtypeStruct(operands[0].shape, F32),
        in_specs=[VMEM_SPEC] * len(operands),
        out_specs=VMEM_SPEC,
        compiler_params=params(8),
        name=name,
    )(*operands)


def overflow_kernel(limits, sy_ref, *refs):
    low, high = low_need(sy_ref[0]), high_need(sy_ref[0])
    for v in range(1, sy_ref.shape[0]):
        low, high = low + low_need(sy_ref[v]), high + high_need(sy_ref[v])
    refs[-1][0] = jnp.where((low > limits[0]) | (high > limits[1]), 1, 0)


def overflow(shift_y, limits, after):
    return pl.pallas_call(
        functools.partial(overflow_kernel, limits),
        out_shape=jax.ShapeDtypeStruct((1,), jnp.int32),
        in_specs=[SMEM_SPEC] + [ANY_SPEC] * len(after),
        out_specs=SMEM_SPEC,
        compiler_params=params(8),
        name="overflow",
    )(shift_y, *after)[0]


def profile(density, flux_x, flux_y, energy, factor):
    inverse = 1.0 / density
    mean_x = flux_x * inverse
    mean_y = flux_y * inverse
    temperature = 0.5 * (energy * inverse - mean_x * mean_x - mean_y * mean_y)
    rate = 1.0 - jnp.exp(-factor * density / (SPEED_TALLY * jnp.sqrt(temperature)))
    height = rate * (density / (2.0 * math.pi * temperature))
    return mean_x, mean_y, -0.5 / temperature, height, 1.0 - rate


def relax_cells(get, put, values, factor, weights):
    mean_x, mean_y, scale, height, keep = profile(*values, factor)
    for v, (along_x, along_y) in enumerate(weights):
        gap_x = along_x - mean_x
        gap_y = along_y - mean_y
        state = height * jnp.exp((gap_x * gap_x + gap_y * gap_y) * scale)
        put(v, keep * get(v) + state)


def relax_tile(buf, sums, base, core, factor, weights, k, h):
    mine_ref, other_ref = sums
    half = buf.shape[2] // 2
    for n in range(half):
        t = h * half + n
        values = []
        for m in range(4):
            index = base + m * half + n
            values.append(jnp.where(core == h, mine_ref[index], other_ref[index]))

        def put(v, value):
            buf[v, k, t] = value

        relax_cells(lambda v: buf[v, k, t], put, values, factor, weights)


def relax_kernel(tiles, meta_ref, sx_ref, sy_ref, fx_ref, fy_ref, factor_ref, mine_ref, other_ref,
                 planes_ref, out_ref, done_ref, buf, sem_in, sem_out):
    planes, _, lane_tiles = planes_ref.shape[:3]
    half = lane_tiles // 2
    done_ref[0] = 1
    first_tile, count = tiles[0], len(tiles)

    def copy(k, h, out):
        lanes = pl.ds(h * half, half)
        here = buf.at[:, k, lanes]
        if out:
            return pltpu.make_async_copy(here, out_ref.at[:, first_tile + k, lanes], sem_out.at[2 * k + h])
        return pltpu.make_async_copy(planes_ref.at[:, first_tile + k, lanes], here, sem_in.at[2 * k + h])

    for k in range(count):
        for h in range(2):
            copy(k, h, False).start()
    weights = [velocity(sx_ref, sy_ref, fx_ref, fy_ref, v) for v in range(planes)]

    def step(k, _):
        for h in range(2):
            copy(k, h, False).wait()
            sums = mine_ref, other_ref
            relax_tile(buf, sums, k * 4 * half, meta_ref[3], factor_ref[0], weights, k, h)
            copy(k, h, True).start()
        return 0

    lax.fori_loop(0, count, step, 0)
    for k in range(count):
        for h in range(2):
            copy(k, h, True).wait()


def relax_inside(tiles, meta, small, factor, sums, moved):
    planes, _, lane_tiles = moved.shape[:3]
    count = len(tiles)
    return pl.pallas_call(
        functools.partial(relax_kernel, tiles),
        out_shape=[jax.ShapeDtypeStruct(moved.shape, F32), jax.ShapeDtypeStruct((1,), jnp.int32)],
        in_specs=[SMEM_SPEC] * 6 + [VMEM_SPEC] * 2 + [ANY_SPEC],
        out_specs=[ANY_SPEC, SMEM_SPEC],
        scratch_shapes=[
            pltpu.VMEM((planes, count, lane_tiles, ROW, LANE), F32),
            pltpu.SemaphoreType.DMA((2 * count,)),
            pltpu.SemaphoreType.DMA((2 * count,)),
        ],
        compiler_params=params(58),
        name="relax_inside",
    )(meta, *small[:4], factor, *sums, moved)


def relax_edges_kernel(cuts, meta_ref, sx_ref, sy_ref, fx_ref, fy_ref, inflow_ref, factor_ref,
                       heights_ref, m_low, o_low, m_high, o_high, planes_ref, *refs):
    pack_refs = refs[: len(cuts)]
    _, out_ref, frames, buf, low_buf, high_buf, bars, sem_in, sem_planes, sem_out = refs[len(cuts) :]
    planes, row_tiles, lane_tiles = planes_ref.shape[:3]
    half = lane_tiles // 2
    row0, first, last, core = (meta_ref[i] for i in range(4))
    places = 0, 1, row_tiles - 2, row_tiles - 1
    needs = [low_need(sy_ref[0]), high_need(sy_ref[0])]
    for v in range(1, planes):
        needs = [needs[0] + low_need(sy_ref[v]), needs[1] + high_need(sy_ref[v])]

    def pack_copy(n):
        pack, begin, end = cuts[n]
        target = (low_buf, high_buf)[pack].at[:, 16 + begin : 16 + end, :]
        return pltpu.make_async_copy(pack_refs[n], target, sem_in.at[n])

    def in_copy(k):
        return pltpu.make_async_copy(planes_ref.at[:, places[k]], buf.at[:, k], sem_planes.at[k])

    for n in range(len(cuts)):
        pl.when(needs[cuts[n][0]] > cuts[n][1])(lambda n=n: pack_copy(n).start())
    for k in range(4):
        in_copy(k).start()
    prepare_heights(heights_ref, bars)
    for n in range(len(cuts)):
        pl.when(needs[cuts[n][0]] > cuts[n][1])(lambda n=n: pack_copy(n).wait())
    for k in range(4):
        in_copy(k).wait()

    def add_masked(v, k, first_row):
        def put(t, value):
            buf[v, k, t] = buf[v, k, t] + jnp.where(first_row < bars[t], 0.0, value)

        return put

    def one(v, offsets):
        low, high = offsets
        value = inflow_ref[v]
        shift = sy_ref[v]
        up = shift >= 0
        scalars = sx_ref[v], shift, fx_ref[v], fy_ref[v]
        borders = (0, lane_tiles + 1)
        columns = range(lane_tiles + 2)

        @pl.when(up & (first == 0))
        def _():
            fill_rows(frames, v, borders, 8, 16, value)
            fill_rows(frames, v, columns, 24, 16, 0.0)
            for t in range(lane_tiles):
                for r in range(0, 16, ROW):
                    piece = low_buf[t, pl.ds(low + shift + 1 + r, ROW), :]
                    frames[v, t + 1, 8 + r : 8 + r + ROW, :] = piece
            advect(frames, v, scalars, [(24, add_masked(v, 0, row0))])

            @pl.when(shift == CFL)
            def _():
                advect(frames, v, scalars, [(32, add_masked(v, 1, row0 + ROW))])

        @pl.when(jnp.logical_not(up) & (last == 0))
        def _():
            fill_rows(frames, v, borders, 32, 8, value)
            fill_rows(frames, v, columns, 16, 16, 0.0)
            for t in range(lane_tiles):
                frames[v, t + 1, 32:40, :] = high_buf[t, pl.ds(16 + high, ROW), :]
            advect(frames, v, scalars, [(24, add_masked(v, 3, row0 + ROW * (row_tiles - 1)))])

        return low + low_need(shift), high + high_need(shift)

    lax.fori_loop(0, planes, one, (jnp.int32(0), jnp.int32(0)))
    weights = [velocity(sx_ref, sy_ref, fx_ref, fy_ref, v) for v in range(planes)]

    def out_copy(k, h):
        j = jnp.where(k < 2, k, row_tiles - 4 + k)
        lanes = pl.ds(h * half, half)
        return pltpu.make_async_copy(buf.at[:, k, lanes], out_ref.at[:, j, lanes], sem_out.at[2 * k + h])

    for sums, begin in (((m_low, o_low), 0), ((m_high, o_high), 2)):

        def step(k, _, sums=sums, begin=begin):
            for h in range(2):
                relax_tile(buf, sums, (k - begin) * 4 * half, core, factor_ref[0], weights, k, h)
                out_copy(k, h).start()
            return 0

        lax.fori_loop(begin, begin + 2, step, 0)
    for k in range(4):
        for h in range(2):
            out_copy(k, h).wait()


def relax_edges(meta, small, factor, heights, sums, moved, packs, cuts, out):
    planes, _, lane_tiles = moved.shape[:3]
    operands = [meta, *small[:5], factor, heights, *sums, moved, *packs, out]
    return pl.pallas_call(
        functools.partial(relax_edges_kernel, cuts),
        out_shape=jax.ShapeDtypeStruct(out.shape, F32),
        in_specs=[SMEM_SPEC] * 7 + [VMEM_SPEC] * 5 + [ANY_SPEC] * (len(cuts) + 2),
        out_specs=ANY_SPEC,
        scratch_shapes=[
            pltpu.VMEM((planes, lane_tiles + 2, 48, LANE), F32),
            pltpu.VMEM((planes, 4, lane_tiles, ROW, LANE), F32),
            pltpu.VMEM((lane_tiles, planes * LOW_ROWS + 32, LANE), F32),
            pltpu.VMEM((lane_tiles, planes * HIGH_ROWS + 32, LANE), F32),
            pltpu.VMEM((lane_tiles, ROW, LANE), jnp.int32),
            pltpu.SemaphoreType.DMA((len(cuts),)),
            pltpu.SemaphoreType.DMA((4,)),
            pltpu.SemaphoreType.DMA((8,)),
        ],
        input_output_aliases={len(operands) - 1: 0},
        compiler_params=params(58),
        name="relax_edges",
    )(*operands)


def per_device(populations, shift_x, shift_y, frac_x, frac_y, inflow, wall_state, heights,
               impact_frequency_factor):
    planes, row_count, col_count = populations.shape
    space_count, vel_count = lax.axis_size("space"), lax.axis_size("vel")
    row_tiles, lane_tiles = row_count // ROW, col_count // LANE
    space, vel = lax.axis_index("space"), lax.axis_index("vel")
    forward = [(i, i + 1) for i in range(space_count - 1)]
    backward = [(target, source) for source, target in forward]
    partner = [(i, i ^ 1) for i in range(vel_count)]
    across = [(i, i ^ 2) for i in range(vel_count)]

    meta = jnp.stack([space * row_count, space == 0, space == space_count - 1, vel % 2]).astype(jnp.int32)
    small = (shift_x, shift_y, frac_x, frac_y, inflow, wall_state)
    factor = impact_frequency_factor.reshape(1)
    bars = heights.reshape(lane_tiles, LANE)
    pop = populations.reshape(planes, row_tiles, ROW, lane_tiles, LANE).transpose(0, 1, 3, 2, 4)
    low_sent, high_sent = min(LOW_SENT, planes * LOW_ROWS), min(HIGH_SENT, planes * HIGH_ROWS)
    cuts = [
        (0, 0, low_sent),
        (1, 0, high_sent),
        (0, low_sent, planes * LOW_ROWS),
        (1, high_sent, planes * HIGH_ROWS),
    ]
    plan = Plan(row_tiles, lane_tiles // 2)

    moved, mine, theirs, *packs = advance(plan, meta, small, bars, pop, cuts)
    received = lax.ppermute(theirs, "vel", partner)
    up, down, inside, edge_low, edge_high = fold(mine, received, plan.sizes)
    from_low = lax.ppermute(up, "space", forward)
    from_high = lax.ppermute(down, "space", backward)
    low_first = lax.ppermute(packs[0], "space", forward)
    high_first = lax.ppermute(packs[1], "space", backward)

    def total(sums):
        whole = small_call(add_kernel, "add", sums, lax.ppermute(sums, "vel", across))
        return whole, lax.ppermute(whole, "vel", partner)

    sums_inside = total(inside)
    sums_low = total(small_call(join_low_kernel, "join_low", edge_low, from_low))
    sums_high = total(small_call(join_high_kernel, "join_high", edge_high, from_high))

    out, done = relax_inside(plan.inside, meta, small, factor, sums_inside, moved)
    after = low_first, high_first, sums_low[1], sums_high[1], done
    needed = overflow(shift_y, (low_sent, high_sent), after)

    def send_more(low, high):
        return lax.ppermute(low, "space", forward), lax.ppermute(high, "space", backward)

    more = lax.cond(needed > 0, send_more, lambda low, high: (low, high), packs[2], packs[3])
    halo = low_first, high_first, *more
    out = relax_edges(meta, small, factor, bars, sums_low + sums_high, moved, halo, cuts, out)
    return out.transpose(0, 1, 3, 2, 4).reshape(planes, row_count, col_count)


def solution(mesh):
    return jax.shard_map(
        per_device,
        mesh=mesh,
        in_specs=(
            P("vel", "space", None),
            P("vel"),
            P("vel"),
            P("vel"),
            P("vel"),
            P("vel"),
            P("vel"),
            P(),
            P(),
        ),
        out_specs=P("vel", "space", None),
        check_vma=False,
    )
```

```python
import functools
import math

import jax
import jax.numpy as jnp
from jax import lax
from jax.experimental import pallas as pl
from jax.experimental.pallas import tpu as pltpu
from jax.sharding import PartitionSpec as P

SPEED_TALLY = 64
CFL = 8
LOW_ROWS = CFL + 1
HIGH_ROWS = CFL
ROW = 8
LANE = 128
PAD = 16
F32 = jnp.float32
LOW_SENT = 72
HIGH_SENT = 72

SMEM_SPEC = pl.BlockSpec(memory_space=pltpu.SMEM)
ANY_SPEC = pl.BlockSpec(memory_space=pl.ANY)
HBM_SPEC = pl.BlockSpec(memory_space=pltpu.HBM)
VMEM_SPEC = pl.BlockSpec(memory_space=pltpu.VMEM)


def params(mebibytes):
    return pltpu.CompilerParams(vmem_limit_bytes=mebibytes * 1024 * 1024)


def low_need(shift):
    return jnp.where(shift >= 0, shift + 1, 0)


def high_need(shift):
    return jnp.where(shift < 0, -shift, 0)


def fill_rows(padded, v, columns, start, count, value):
    block = jnp.full((ROW, LANE), value, F32)
    for t in columns:
        for r in range(start, start + count, ROW):
            padded[v, t, r : r + ROW, :] = block


def prepare_heights(heights_ref, bars):
    lane_tiles = heights_ref.shape[0]
    sublane = lax.broadcasted_iota(jnp.int32, (ROW, LANE), 0)
    for t in range(lane_tiles):
        bars[t] = jnp.broadcast_to(heights_ref[t : t + 1, :], (ROW, LANE)) - sublane


def advect(padded, v, scalars, tiles):
    sx, sy, fx, fy = scalars
    lane_tiles = padded.shape[1] - 2
    lane = lax.broadcasted_iota(jnp.int32, (ROW, LANE), 1)
    near_roll = jnp.where(sx < 0, sx + LANE, sx)
    far_roll = jnp.where(sx + 1 < 0, sx + 1 + LANE, sx + 1)

    def moved(start, t):
        nearer = padded[v, t + 1, pl.ds(start, ROW), :]
        further = padded[v, t + 1, pl.ds(start - 1, ROW), :]
        line = (1.0 - fy) * nearer + fy * further
        return pltpu.roll(line, near_roll, 1), pltpu.roll(line, far_roll, 1)

    def blend(put, t, near, far):
        put(t, (1.0 - fx) * near + fx * far)

    @pl.when(sx >= 0)
    def _():
        own_near, own_far = lane >= sx, lane >= sx + 1
        for begin, put in tiles:
            before = moved(begin - sy, -1)
            for t in range(lane_tiles):
                here = moved(begin - sy, t)
                near = jnp.where(own_near, here[0], before[0])
                blend(put, t, near, jnp.where(own_far, here[1], before[1]))
                before = here

    @pl.when(sx < 0)
    def _():
        own_near, own_far = lane < sx + LANE, lane < sx + 1 + LANE
        for begin, put in tiles:
            here = moved(begin - sy, 0)
            for t in range(lane_tiles):
                after = moved(begin - sy, t + 1)
                near = jnp.where(own_near, here[0], after[0])
                blend(put, t, near, jnp.where(own_far, here[1], after[1]))
                here = after


def store_masked(target, bars, first_row, solid_value):
    def put(t, value):
        target[t] = jnp.where(first_row < bars[t], solid_value, value)

    return put


def velocity(sx_ref, sy_ref, fx_ref, fy_ref, v):
    return sx_ref[v].astype(F32) + fx_ref[v], sy_ref[v].astype(F32) + fy_ref[v]


def sum_moments(planes_ref, k, weights, lane_tile_range):
    sums = [[None] * 4 for _ in lane_tile_range]
    for v, (along_x, along_y) in enumerate(weights):
        square = along_x * along_x + along_y * along_y
        for n, t in enumerate(lane_tile_range):
            f = planes_ref[v, k, t]
            terms = (f, f * along_x, f * along_y, f * square)
            sums[n] = [b if a is None else a + b for a, b in zip(sums[n], terms)]
    return sums


class Plan:
    def __init__(self, row_tiles, half):
        self.tile = 4 * half
        self.inside = list(range(2, row_tiles - 2))
        self.sizes = [self.tile + 4, self.tile, len(self.inside) * self.tile, 2 * self.tile, 2 * self.tile]
        self.starts = [sum(self.sizes[:n]) for n in range(len(self.sizes) + 1)]
        self.row_tiles = row_tiles

    def start(self, j):
        low = self.starts[3] + self.tile * j
        high = self.starts[4] + self.tile * (j - self.row_tiles + 2)
        inside = self.starts[2] + self.tile * (j - 2)
        return jnp.where(j < 2, low, jnp.where(j >= self.row_tiles - 2, high, inside))


def advance_kernel(plan, cuts, group, meta_ref, sx_ref, sy_ref, fx_ref, fy_ref, inflow_ref, wall_ref,
                   heights_ref, pop_ref, *refs):
    planes_ref, mine_ref, theirs_ref, more_ref = refs[:4]
    packs = refs[4 : 4 + len(cuts)]
    (padded, planes_buf, outer, last_row, low_pack, high_pack, bars, sem_in, sem_planes, sem_out) = refs[
        4 + len(cuts) :
    ]
    planes, row_tiles, lane_tiles = pop_ref.shape[:3]
    half = lane_tiles // 2
    rows = row_tiles * ROW
    row0, first, last, core = (meta_ref[i] for i in range(4))

    def loads(g):
        members = pl.ds(g * group, group)
        return [
            pltpu.make_async_copy(
                pop_ref.at[members, i],
                padded.at[members, 1 : 1 + lane_tiles, PAD + ROW * i : PAD + ROW * (i + 1), :],
                sem_in.at[g, i],
            )
            for i in range(row_tiles)
        ]

    def start(g, _):
        for load in loads(g):
            load.start()
        return 0

    lax.fori_loop(0, planes // group, start, 0)
    prepare_heights(heights_ref, bars)
    last_row[...] = jnp.zeros_like(last_row)

    def put_sums(h, first_block, sums):
        for is_mine, ref in ((True, mine_ref), (False, theirs_ref)):

            @pl.when((core == h) == is_mine)
            def _():
                for n, value in enumerate(sums):
                    ref[first_block + n] = value


    def out_copy(v):
        return pltpu.make_async_copy(planes_buf.at[v], planes_ref.at[v], sem_planes.at[v])

    def one(v, offsets):
        low, high = offsets
        value = inflow_ref[v]
        shift = sy_ref[v]
        up = shift >= 0
        columns = range(lane_tiles + 2)
        fill_rows(padded, v, (0, lane_tiles + 1), PAD, rows, value)
        fill_rows(padded, v, columns, 0, PAD, jnp.where(first == 1, value, 0.0))
        fill_rows(padded, v, columns, PAD + rows, ROW, jnp.where(last == 1, value, 0.0))

        @pl.when(v % group == 0)
        def _():
            for load in loads(v // group):
                load.wait()

        scalars = sx_ref[v], shift, fx_ref[v], fy_ref[v]
        work = [
            (PAD + ROW * j, store_masked(planes_buf.at[v, j], bars, row0 + ROW * j, wall_ref[v]))
            for j in range(row_tiles)
        ]
        beyond = jnp.where(up, rows, -ROW)
        work.append((PAD + beyond, store_masked(outer.at[v], bars, row0 + beyond, 0.0)))
        advect(padded, v, scalars, work)
        out_copy(v).start()

        @pl.when(shift == CFL)
        def _():
            along_x, along_y = velocity(sx_ref, sy_ref, fx_ref, fy_ref, v)
            factors = 1.0, along_x, along_y, along_x * along_x + along_y * along_y

            def put(t, value):
                row = jnp.where(row0 + rows + ROW < bars[t], 0.0, value)
                h, r = divmod(t, half)
                for m in range(4):
                    total = last_row[h, m, r : r + 1, :] + (row * factors[m])[0:1, :]
                    last_row[h, m, r : r + 1, :] = total

            advect(padded, v, scalars, [(PAD + rows + ROW, put)])

        @pl.when(up)
        def _():
            for t in range(lane_tiles):
                source = pl.ds(PAD + rows - 1 - shift, 8)
                low_pack[t, pl.ds(low, 8), :] = padded[v, t + 1, source, :]

        @pl.when(shift == CFL)
        def _():
            for t in range(lane_tiles):
                low_pack[t, pl.ds(low + 8, 1), :] = padded[v, t + 1, PAD + rows - 1 : PAD + rows, :]

        @pl.when(jnp.logical_not(up))
        def _():
            for t in range(lane_tiles):
                high_pack[t, pl.ds(high, 8), :] = padded[v, t + 1, PAD : PAD + 8, :]

        return low + low_need(shift), high + high_need(shift)

    needs = lax.fori_loop(0, planes, one, (jnp.int32(0), jnp.int32(0)))
    sent = [end for _, begin, end in cuts if begin == 0]
    overflows = (needs[0] > sent[0]) | (needs[1] > sent[1])
    more_ref[0] = jnp.where(overflows, 1, 0)

    def pack_copy(n):
        pack, begin, end = cuts[n]
        source = (low_pack, high_pack)[pack].at[:, begin:end, :]
        return pltpu.make_async_copy(source, packs[n], sem_out.at[n])

    def each_pack(act):
        for n, (_, begin, _) in enumerate(cuts):
            if begin == 0:
                act(pack_copy(n))
            else:
                pl.when(overflows)(lambda n=n: act(pack_copy(n)))

    each_pack(lambda copy: copy.start())
    for h in range(2):
        put_sums(h, plan.tile, [last_row[h, m] for m in range(4)])
        for rising in (True, False):
            for part in range(2):
                tiles = range(h * half + part * half // 2, h * half + (part + 1) * half // 2)
                sums = [[None] * 4 for _ in tiles]
                for v in range(planes):
                    along_x, along_y = velocity(sx_ref, sy_ref, fx_ref, fy_ref, v)
                    goes = jnp.where((sy_ref[v] >= 0) == rising, 1.0, 0.0)
                    square = (along_x * along_x + along_y * along_y) * goes
                    factors = goes, along_x * goes, along_y * goes, square
                    for n, t in enumerate(tiles):
                        f = outer[v, t]
                        terms = [f * w for w in factors]
                        sums[n] = [b if a is None else a + b for a, b in zip(sums[n], terms)]
                begin = plan.starts[0 if rising else 1] + part * half // 2
                for m in range(4):
                    put_sums(h, begin + m * half, [sums[n][m] for n in range(len(tiles))])
    weights = [velocity(sx_ref, sy_ref, fx_ref, fy_ref, v) for v in range(planes)]

    def step(j, _):
        begin = plan.start(j)
        for h in range(2):
            sums = sum_moments(planes_buf, j, weights, range(h * half, (h + 1) * half))
            put_sums(h, begin, [sums[t][m] for m in range(4) for t in range(half)])
        return 0

    lax.fori_loop(0, row_tiles, step, 0)

    def finish(v, _):
        out_copy(v).wait()
        return 0

    lax.fori_loop(0, planes, finish, 0)
    each_pack(lambda copy: copy.wait())


def advance(plan, meta, small, heights, pop, cuts):
    planes, row_tiles, lane_tiles = pop.shape[:3]
    group = math.gcd(planes, 4)
    blocks = plan.starts[-1]
    half_sums = jax.ShapeDtypeStruct((blocks, ROW, LANE), F32)
    return pl.pallas_call(
        functools.partial(advance_kernel, plan, cuts, group),
        out_shape=[pltpu.HBM(pop.shape, F32), half_sums, half_sums, jax.ShapeDtypeStruct((1,), jnp.int32)]
        + [pltpu.HBM((lane_tiles, end - begin, LANE), F32) for _, begin, end in cuts],
        in_specs=[SMEM_SPEC] * 7 + [VMEM_SPEC, HBM_SPEC],
        out_specs=[HBM_SPEC, VMEM_SPEC, VMEM_SPEC, SMEM_SPEC] + [HBM_SPEC] * len(cuts),
        scratch_shapes=[
            pltpu.VMEM((planes, lane_tiles + 2, PAD + row_tiles * ROW + ROW, LANE), F32),
            pltpu.VMEM((planes, row_tiles, lane_tiles, ROW, LANE), F32),
            pltpu.VMEM((planes, lane_tiles, ROW, LANE), F32),
            pltpu.VMEM((2, 4, ROW, LANE), F32),
            pltpu.VMEM((lane_tiles, planes * LOW_ROWS + 16, LANE), F32),
            pltpu.VMEM((lane_tiles, planes * HIGH_ROWS + 16, LANE), F32),
            pltpu.VMEM((lane_tiles, ROW, LANE), jnp.int32),
            pltpu.SemaphoreType.DMA((planes // group, row_tiles)),
            pltpu.SemaphoreType.DMA((planes,)),
            pltpu.SemaphoreType.DMA((len(cuts),)),
        ],
        compiler_params=params(58),
        name="advance",
    )(meta, *small, heights, pop)


def fold_kernel(mine_ref, received_ref, *out_refs):
    begin = 0
    for ref in out_refs:
        n = ref.shape[0]
        ref[...] = mine_ref[begin : begin + n] + received_ref[begin : begin + n]
        begin += n


def fold(mine, received, sizes):
    return pl.pallas_call(
        fold_kernel,
        out_shape=[jax.ShapeDtypeStruct((n, ROW, LANE), F32) for n in sizes],
        in_specs=[VMEM_SPEC] * 2,
        out_specs=[VMEM_SPEC] * len(sizes),
        compiler_params=params(8),
        name="fold",
    )(mine, received)


def join_low_kernel(own_ref, low_ref, *refs):
    out_ref = refs[-1]
    tile = own_ref.shape[0] // 2
    half = tile // 4
    out_ref[2 * tile :] = jnp.zeros((out_ref.shape[0] - 2 * tile, ROW, LANE), F32)
    out_ref[:tile] = own_ref[:tile] + low_ref[:tile]
    top = lax.broadcasted_iota(jnp.int32, (ROW, LANE), 0) == 0
    for m in range(4):
        for n in range(half):
            row = jnp.broadcast_to(low_ref[tile + m, n : n + 1, :], (ROW, LANE))
            index = tile + m * half + n
            out_ref[index] = own_ref[index] + jnp.where(top, row, 0.0)


def add_kernel(a_ref, b_ref, *refs):
    refs[-1][...] = a_ref[...] + b_ref[...]


def join_high_kernel(own_ref, high_ref, *refs):
    out_ref = refs[-1]
    tile = high_ref.shape[0]
    out_ref[2 * tile :] = jnp.zeros((out_ref.shape[0] - 2 * tile, ROW, LANE), F32)
    out_ref[:tile] = own_ref[:tile]
    out_ref[tile : 2 * tile] = own_ref[tile:] + high_ref[...]


def small_call(kernel, name, a, b, after=(), extra=0):
    operands = a, b, *after
    shape = (a.shape[0] + extra, *a.shape[1:])
    return pl.pallas_call(
        kernel,
        out_shape=jax.ShapeDtypeStruct(shape, F32),
        in_specs=[VMEM_SPEC] * 2 + [ANY_SPEC] * len(after),
        out_specs=VMEM_SPEC,
        compiler_params=params(8),
        name=name,
    )(*operands)


def profile(density, flux_x, flux_y, energy, factor):
    inverse = 1.0 / density
    mean_x = flux_x * inverse
    mean_y = flux_y * inverse
    temperature = 0.5 * (energy * inverse - mean_x * mean_x - mean_y * mean_y)
    rate = 1.0 - jnp.exp(-factor * density / (SPEED_TALLY * jnp.sqrt(temperature)))
    height = rate * (density / (2.0 * math.pi * temperature))
    return mean_x, mean_y, -0.5 / temperature, height, 1.0 - rate


def relax_cells(get, put, values, factor, weights):
    mean_x, mean_y, scale, height, keep = profile(*values, factor)
    for v, (along_x, along_y) in enumerate(weights):
        gap_x = along_x - mean_x
        gap_y = along_y - mean_y
        state = height * jnp.exp((gap_x * gap_x + gap_y * gap_y) * scale)
        put(v, keep * get(v) + state)


def relax_tile(buf, sums, base, core, factor, weights, k, h):
    mine_ref, other_ref = sums
    half = buf.shape[2] // 2
    for n in range(half):
        t = h * half + n
        values = []
        for m in range(4):
            index = base + m * half + n
            values.append(jnp.where(core == h, mine_ref[index], other_ref[index]))

        def put(v, value):
            buf[v, k, t] = value

        relax_cells(lambda v: buf[v, k, t], put, values, factor, weights)


def relax_kernel(tiles, meta_ref, sx_ref, sy_ref, fx_ref, fy_ref, factor_ref, mine_ref, other_ref,
                 planes_ref, out_ref, done_ref, buf, sem_in, sem_out):
    planes, _, lane_tiles = planes_ref.shape[:3]
    half = lane_tiles // 2
    done_ref[0] = 1
    first_tile, count = tiles[0], len(tiles)

    def copy(k, h, out):
        lanes = pl.ds(h * half, half)
        here = buf.at[:, k, lanes]
        if out:
            return pltpu.make_async_copy(here, out_ref.at[:, first_tile + k, lanes], sem_out.at[2 * k + h])
        return pltpu.make_async_copy(planes_ref.at[:, first_tile + k, lanes], here, sem_in.at[2 * k + h])

    for k in range(count):
        for h in range(2):
            copy(k, h, False).start()
    weights = [velocity(sx_ref, sy_ref, fx_ref, fy_ref, v) for v in range(planes)]

    def step(k, _):
        for h in range(2):
            copy(k, h, False).wait()
            sums = mine_ref, other_ref
            relax_tile(buf, sums, k * 4 * half, meta_ref[3], factor_ref[0], weights, k, h)
            copy(k, h, True).start()
        return 0

    lax.fori_loop(0, count, step, 0)
    for k in range(count):
        for h in range(2):
            copy(k, h, True).wait()


def relax_inside(tiles, meta, small, factor, sums, moved):
    planes, _, lane_tiles = moved.shape[:3]
    count = len(tiles)
    return pl.pallas_call(
        functools.partial(relax_kernel, tiles),
        out_shape=[jax.ShapeDtypeStruct(moved.shape, F32), jax.ShapeDtypeStruct((1,), jnp.int32)],
        in_specs=[SMEM_SPEC] * 6 + [VMEM_SPEC] * 2 + [ANY_SPEC],
        out_specs=[ANY_SPEC, SMEM_SPEC],
        scratch_shapes=[
            pltpu.VMEM((planes, count, lane_tiles, ROW, LANE), F32),
            pltpu.SemaphoreType.DMA((2 * count,)),
            pltpu.SemaphoreType.DMA((2 * count,)),
        ],
        compiler_params=params(58),
        name="relax_inside",
    )(meta, *small[:4], factor, *sums, moved)


def relax_edges_kernel(cuts, meta_ref, sx_ref, sy_ref, fx_ref, fy_ref, inflow_ref, factor_ref,
                       heights_ref, m_low, o_low, m_high, o_high, planes_ref, *refs):
    pack_refs = refs[: len(cuts)]
    _, out_ref, frames, buf, low_buf, high_buf, bars, sem_in, sem_planes, sem_out = refs[len(cuts) :]
    planes, row_tiles, lane_tiles = planes_ref.shape[:3]
    half = lane_tiles // 2
    row0, first, last, core = (meta_ref[i] for i in range(4))
    places = 0, 1, row_tiles - 2, row_tiles - 1
    needs = [low_need(sy_ref[0]), high_need(sy_ref[0])]
    for v in range(1, planes):
        needs = [needs[0] + low_need(sy_ref[v]), needs[1] + high_need(sy_ref[v])]

    def pack_copy(n):
        pack, begin, end = cuts[n]
        target = (low_buf, high_buf)[pack].at[:, 16 + begin : 16 + end, :]
        return pltpu.make_async_copy(pack_refs[n], target, sem_in.at[n])

    def in_copy(k):
        return pltpu.make_async_copy(planes_ref.at[:, places[k]], buf.at[:, k], sem_planes.at[k])

    for n in range(len(cuts)):
        pl.when(needs[cuts[n][0]] > cuts[n][1])(lambda n=n: pack_copy(n).start())
    for k in range(4):
        in_copy(k).start()
    prepare_heights(heights_ref, bars)
    for n in range(len(cuts)):
        pl.when(needs[cuts[n][0]] > cuts[n][1])(lambda n=n: pack_copy(n).wait())
    for k in range(4):
        in_copy(k).wait()

    def add_masked(v, k, first_row):
        def put(t, value):
            buf[v, k, t] = buf[v, k, t] + jnp.where(first_row < bars[t], 0.0, value)

        return put

    def one(v, offsets):
        low, high = offsets
        value = inflow_ref[v]
        shift = sy_ref[v]
        up = shift >= 0
        scalars = sx_ref[v], shift, fx_ref[v], fy_ref[v]
        borders = (0, lane_tiles + 1)
        columns = range(lane_tiles + 2)

        @pl.when(up & (first == 0))
        def _():
            fill_rows(frames, v, borders, 8, 16, value)
            fill_rows(frames, v, columns, 24, 16, 0.0)
            for t in range(lane_tiles):
                for r in range(0, 16, ROW):
                    piece = low_buf[t, pl.ds(low + shift + 1 + r, ROW), :]
                    frames[v, t + 1, 8 + r : 8 + r + ROW, :] = piece
            advect(frames, v, scalars, [(24, add_masked(v, 0, row0))])

            @pl.when(shift == CFL)
            def _():
                advect(frames, v, scalars, [(32, add_masked(v, 1, row0 + ROW))])

        @pl.when(jnp.logical_not(up) & (last == 0))
        def _():
            fill_rows(frames, v, borders, 32, 8, value)
            fill_rows(frames, v, columns, 16, 16, 0.0)
            for t in range(lane_tiles):
                frames[v, t + 1, 32:40, :] = high_buf[t, pl.ds(16 + high, ROW), :]
            advect(frames, v, scalars, [(24, add_masked(v, 3, row0 + ROW * (row_tiles - 1)))])

        return low + low_need(shift), high + high_need(shift)

    lax.fori_loop(0, planes, one, (jnp.int32(0), jnp.int32(0)))
    weights = [velocity(sx_ref, sy_ref, fx_ref, fy_ref, v) for v in range(planes)]

    def out_copy(k, h):
        j = jnp.where(k < 2, k, row_tiles - 4 + k)
        lanes = pl.ds(h * half, half)
        return pltpu.make_async_copy(buf.at[:, k, lanes], out_ref.at[:, j, lanes], sem_out.at[2 * k + h])

    for sums, begin in (((m_low, o_low), 0), ((m_high, o_high), 2)):

        def step(k, _, sums=sums, begin=begin):
            for h in range(2):
                relax_tile(buf, sums, (k - begin) * 4 * half, core, factor_ref[0], weights, k, h)
                out_copy(k, h).start()
            return 0

        lax.fori_loop(begin, begin + 2, step, 0)
    for k in range(4):
        for h in range(2):
            out_copy(k, h).wait()


def relax_edges(meta, small, factor, heights, sums, moved, packs, cuts, out):
    planes, _, lane_tiles = moved.shape[:3]
    operands = [meta, *small[:5], factor, heights, *sums, moved, *packs, out]
    return pl.pallas_call(
        functools.partial(relax_edges_kernel, cuts),
        out_shape=jax.ShapeDtypeStruct(out.shape, F32),
        in_specs=[SMEM_SPEC] * 7 + [VMEM_SPEC] * 5 + [ANY_SPEC] * (len(cuts) + 2),
        out_specs=ANY_SPEC,
        scratch_shapes=[
            pltpu.VMEM((planes, lane_tiles + 2, 48, LANE), F32),
            pltpu.VMEM((planes, 4, lane_tiles, ROW, LANE), F32),
            pltpu.VMEM((lane_tiles, planes * LOW_ROWS + 32, LANE), F32),
            pltpu.VMEM((lane_tiles, planes * HIGH_ROWS + 32, LANE), F32),
            pltpu.VMEM((lane_tiles, ROW, LANE), jnp.int32),
            pltpu.SemaphoreType.DMA((len(cuts),)),
            pltpu.SemaphoreType.DMA((4,)),
            pltpu.SemaphoreType.DMA((8,)),
        ],
        input_output_aliases={len(operands) - 1: 0},
        compiler_params=params(58),
        name="relax_edges",
    )(*operands)


def per_device(populations, shift_x, shift_y, frac_x, frac_y, inflow, wall_state, heights,
               impact_frequency_factor):
    planes, row_count, col_count = populations.shape
    space_count, vel_count = lax.axis_size("space"), lax.axis_size("vel")
    row_tiles, lane_tiles = row_count // ROW, col_count // LANE
    space, vel = lax.axis_index("space"), lax.axis_index("vel")
    forward = [(i, i + 1) for i in range(space_count - 1)]
    backward = [(target, source) for source, target in forward]
    partner = [(i, i ^ 1) for i in range(vel_count)]
    across = [(i, i ^ 2) for i in range(vel_count)]

    meta = jnp.stack([space * row_count, space == 0, space == space_count - 1, vel % 2]).astype(jnp.int32)
    small = (shift_x, shift_y, frac_x, frac_y, inflow, wall_state)
    factor = impact_frequency_factor.reshape(1)
    bars = heights.reshape(lane_tiles, LANE)
    pop = populations.reshape(planes, row_tiles, ROW, lane_tiles, LANE).transpose(0, 1, 3, 2, 4)
    pop = pltpu.with_memory_space_constraint(pop, pltpu.HBM)
    low_sent, high_sent = min(LOW_SENT, planes * LOW_ROWS), min(HIGH_SENT, planes * HIGH_ROWS)
    cuts = [
        (0, 0, low_sent),
        (1, 0, high_sent),
        (0, low_sent, planes * LOW_ROWS),
        (1, high_sent, planes * HIGH_ROWS),
    ]
    plan = Plan(row_tiles, lane_tiles // 2)

    moved, mine, theirs, more_needed, *packs = advance(plan, meta, small, bars, pop, cuts)
    received = lax.ppermute(theirs, "vel", partner)
    up, down, inside, edge_low, edge_high = fold(mine, received, plan.sizes)
    from_low = lax.ppermute(up, "space", forward)
    from_high = lax.ppermute(down, "space", backward)
    low_first = lax.ppermute(packs[0], "space", forward)
    high_first = lax.ppermute(packs[1], "space", backward)

    def total(sums, after=()):
        whole = small_call(add_kernel, "add", sums, lax.ppermute(sums, "vel", across), after)
        return whole, lax.ppermute(whole, "vel", partner)

    def send_more(low, high):
        return lax.ppermute(low, "space", forward), lax.ppermute(high, "space", backward)

    more = lax.cond(more_needed[0] > 0, send_more, lambda low, high: (low, high), packs[2], packs[3])
    sums_inside = total(inside)
    out, done = relax_inside(plan.inside, meta, small, factor, sums_inside, moved)
    sums_low = total(small_call(join_low_kernel, "join_low", edge_low, from_low, (), 1))
    sums_high = total(small_call(join_high_kernel, "join_high", edge_high, from_high, (), 1))

    halo = low_first, high_first, *more
    out = relax_edges(meta, small, factor, bars, sums_low + sums_high, moved, halo, cuts, out)
    return out.transpose(0, 1, 3, 2, 4).reshape(planes, row_count, col_count)


def solution(mesh):
    return jax.shard_map(
        per_device,
        mesh=mesh,
        in_specs=(
            P("vel", "space", None),
            P("vel"),
            P("vel"),
            P("vel"),
            P("vel"),
            P("vel"),
            P("vel"),
            P(),
            P(),
        ),
        out_specs=P("vel", "space", None),
        check_vma=False,
    )
```

```python
import functools
import math

import jax
import jax.numpy as jnp
from jax import lax
from jax.experimental import pallas as pl
from jax.experimental.pallas import tpu as pltpu
from jax.sharding import PartitionSpec as P

SPEED_TALLY = 64
CFL = 8
LOW_ROWS = CFL + 1
HIGH_ROWS = CFL
ROW = 8
LANE = 128
PAD = 16
F32 = jnp.float32
LOW_SENT = 72
HIGH_SENT = 72

SMEM_SPEC = pl.BlockSpec(memory_space=pltpu.SMEM)
ANY_SPEC = pl.BlockSpec(memory_space=pl.ANY)
HBM_SPEC = pl.BlockSpec(memory_space=pltpu.HBM)
VMEM_SPEC = pl.BlockSpec(memory_space=pltpu.VMEM)


def params(mebibytes):
    return pltpu.CompilerParams(vmem_limit_bytes=mebibytes * 1024 * 1024)


def in_hbm(*arrays):
    return [pltpu.with_memory_space_constraint(x, pltpu.HBM) for x in arrays]


def low_need(shift):
    return jnp.where(shift >= 0, shift + 1, 0)


def high_need(shift):
    return jnp.where(shift < 0, -shift, 0)


def fill_rows(padded, v, columns, start, count, value):
    block = jnp.full((ROW, LANE), value, F32)
    for t in columns:
        for r in range(start, start + count, ROW):
            padded[v, t, r : r + ROW, :] = block


def prepare_heights(heights_ref, bars):
    lane_tiles = heights_ref.shape[0]
    sublane = lax.broadcasted_iota(jnp.int32, (ROW, LANE), 0)
    for t in range(lane_tiles):
        bars[t] = jnp.broadcast_to(heights_ref[t : t + 1, :], (ROW, LANE)) - sublane


def advect(padded, v, scalars, tiles):
    sx, sy, fx, fy = scalars
    lane_tiles = padded.shape[1] - 2
    lane = lax.broadcasted_iota(jnp.int32, (ROW, LANE), 1)
    near_roll = jnp.where(sx < 0, sx + LANE, sx)
    far_roll = jnp.where(sx + 1 < 0, sx + 1 + LANE, sx + 1)

    def moved(start, t):
        nearer = padded[v, t + 1, pl.ds(start, ROW), :]
        further = padded[v, t + 1, pl.ds(start - 1, ROW), :]
        line = (1.0 - fy) * nearer + fy * further
        return pltpu.roll(line, near_roll, 1), pltpu.roll(line, far_roll, 1)

    def blend(put, t, near, far):
        put(t, (1.0 - fx) * near + fx * far)

    @pl.when(sx >= 0)
    def _():
        own_near, own_far = lane >= sx, lane >= sx + 1
        for begin, put in tiles:
            before = moved(begin - sy, -1)
            for t in range(lane_tiles):
                here = moved(begin - sy, t)
                near = jnp.where(own_near, here[0], before[0])
                blend(put, t, near, jnp.where(own_far, here[1], before[1]))
                before = here

    @pl.when(sx < 0)
    def _():
        own_near, own_far = lane < sx + LANE, lane < sx + 1 + LANE
        for begin, put in tiles:
            here = moved(begin - sy, 0)
            for t in range(lane_tiles):
                after = moved(begin - sy, t + 1)
                near = jnp.where(own_near, here[0], after[0])
                blend(put, t, near, jnp.where(own_far, here[1], after[1]))
                here = after


def store_masked(target, bars, first_row, solid_value):
    def put(t, value):
        target[t] = jnp.where(first_row < bars[t], solid_value, value)

    return put


def velocity(sx_ref, sy_ref, fx_ref, fy_ref, v):
    return sx_ref[v].astype(F32) + fx_ref[v], sy_ref[v].astype(F32) + fy_ref[v]


def sum_moments(planes_ref, k, weights, lane_tile_range):
    sums = [[None] * 4 for _ in lane_tile_range]
    for v, (along_x, along_y) in enumerate(weights):
        square = along_x * along_x + along_y * along_y
        for n, t in enumerate(lane_tile_range):
            f = planes_ref[v, k, t]
            terms = (f, f * along_x, f * along_y, f * square)
            sums[n] = [b if a is None else a + b for a, b in zip(sums[n], terms)]
    return sums


class Plan:
    def __init__(self, row_tiles, half):
        self.tile = 4 * half
        self.inside = list(range(2, row_tiles - 2))
        self.sizes = [self.tile + 4, self.tile, len(self.inside) * self.tile, 2 * self.tile, 2 * self.tile]
        self.starts = [sum(self.sizes[:n]) for n in range(len(self.sizes) + 1)]
        self.row_tiles = row_tiles

    def start(self, j):
        low = self.starts[3] + self.tile * j
        high = self.starts[4] + self.tile * (j - self.row_tiles + 2)
        inside = self.starts[2] + self.tile * (j - 2)
        return jnp.where(j < 2, low, jnp.where(j >= self.row_tiles - 2, high, inside))


def advance_kernel(plan, cuts, group, meta_ref, sx_ref, sy_ref, fx_ref, fy_ref, inflow_ref, wall_ref,
                   heights_ref, pop_ref, *refs):
    planes_ref, mine_ref, theirs_ref, more_ref = refs[:4]
    packs = refs[4 : 4 + len(cuts)]
    (padded, planes_buf, outer, last_row, low_pack, high_pack, bars, sem_in, sem_planes, sem_out) = refs[
        4 + len(cuts) :
    ]
    planes, row_tiles, lane_tiles = pop_ref.shape[:3]
    half = lane_tiles // 2
    rows = row_tiles * ROW
    row0, first, last, core = (meta_ref[i] for i in range(4))

    def loads(g):
        members = pl.ds(g * group, group)
        return [
            pltpu.make_async_copy(
                pop_ref.at[members, i],
                padded.at[members, 1 : 1 + lane_tiles, PAD + ROW * i : PAD + ROW * (i + 1), :],
                sem_in.at[g, i],
            )
            for i in range(row_tiles)
        ]

    def start(g, _):
        for load in loads(g):
            load.start()
        return 0

    lax.fori_loop(0, planes // group, start, 0)
    prepare_heights(heights_ref, bars)
    last_row[...] = jnp.zeros_like(last_row)

    def put_sums(h, first_block, sums):
        for is_mine, ref in ((True, mine_ref), (False, theirs_ref)):

            @pl.when((core == h) == is_mine)
            def _():
                for n, value in enumerate(sums):
                    ref[first_block + n] = value


    def out_copy(v):
        return pltpu.make_async_copy(planes_buf.at[v], planes_ref.at[v], sem_planes.at[v])

    def one(v, offsets):
        low, high = offsets
        value = inflow_ref[v]
        shift = sy_ref[v]
        up = shift >= 0
        columns = range(lane_tiles + 2)
        fill_rows(padded, v, (0, lane_tiles + 1), PAD, rows, value)
        fill_rows(padded, v, columns, 0, PAD, jnp.where(first == 1, value, 0.0))
        fill_rows(padded, v, columns, PAD + rows, ROW, jnp.where(last == 1, value, 0.0))

        @pl.when(v % group == 0)
        def _():
            for load in loads(v // group):
                load.wait()

        scalars = sx_ref[v], shift, fx_ref[v], fy_ref[v]
        work = [
            (PAD + ROW * j, store_masked(planes_buf.at[v, j], bars, row0 + ROW * j, wall_ref[v]))
            for j in range(row_tiles)
        ]
        beyond = jnp.where(up, rows, -ROW)
        work.append((PAD + beyond, store_masked(outer.at[v], bars, row0 + beyond, 0.0)))
        advect(padded, v, scalars, work)
        out_copy(v).start()

        @pl.when(shift == CFL)
        def _():
            along_x, along_y = velocity(sx_ref, sy_ref, fx_ref, fy_ref, v)
            factors = 1.0, along_x, along_y, along_x * along_x + along_y * along_y

            def put(t, value):
                row = jnp.where(row0 + rows + ROW < bars[t], 0.0, value)
                h, r = divmod(t, half)
                for m in range(4):
                    total = last_row[h, m, r : r + 1, :] + (row * factors[m])[0:1, :]
                    last_row[h, m, r : r + 1, :] = total

            advect(padded, v, scalars, [(PAD + rows + ROW, put)])

        @pl.when(up)
        def _():
            for t in range(lane_tiles):
                source = pl.ds(PAD + rows - 1 - shift, 8)
                low_pack[t, pl.ds(low, 8), :] = padded[v, t + 1, source, :]

        @pl.when(shift == CFL)
        def _():
            for t in range(lane_tiles):
                low_pack[t, pl.ds(low + 8, 1), :] = padded[v, t + 1, PAD + rows - 1 : PAD + rows, :]

        @pl.when(jnp.logical_not(up))
        def _():
            for t in range(lane_tiles):
                high_pack[t, pl.ds(high, 8), :] = padded[v, t + 1, PAD : PAD + 8, :]

        return low + low_need(shift), high + high_need(shift)

    needs = lax.fori_loop(0, planes, one, (jnp.int32(0), jnp.int32(0)))
    sent = [end for _, begin, end in cuts if begin == 0]
    overflows = (needs[0] > sent[0]) | (needs[1] > sent[1])
    more_ref[0] = jnp.where(overflows, 1, 0)

    def pack_copy(n):
        pack, begin, end = cuts[n]
        source = (low_pack, high_pack)[pack].at[:, begin:end, :]
        return pltpu.make_async_copy(source, packs[n], sem_out.at[n])

    def each_pack(act):
        for n, (_, begin, _) in enumerate(cuts):
            if begin == 0:
                act(pack_copy(n))
            else:
                pl.when(overflows)(lambda n=n: act(pack_copy(n)))

    each_pack(lambda copy: copy.start())
    for h in range(2):
        put_sums(h, plan.tile, [last_row[h, m] for m in range(4)])
        for rising in (True, False):
            for part in range(2):
                tiles = range(h * half + part * half // 2, h * half + (part + 1) * half // 2)
                sums = [[None] * 4 for _ in tiles]
                for v in range(planes):
                    along_x, along_y = velocity(sx_ref, sy_ref, fx_ref, fy_ref, v)
                    goes = jnp.where((sy_ref[v] >= 0) == rising, 1.0, 0.0)
                    square = (along_x * along_x + along_y * along_y) * goes
                    factors = goes, along_x * goes, along_y * goes, square
                    for n, t in enumerate(tiles):
                        f = outer[v, t]
                        terms = [f * w for w in factors]
                        sums[n] = [b if a is None else a + b for a, b in zip(sums[n], terms)]
                begin = plan.starts[0 if rising else 1] + part * half // 2
                for m in range(4):
                    put_sums(h, begin + m * half, [sums[n][m] for n in range(len(tiles))])
    weights = [velocity(sx_ref, sy_ref, fx_ref, fy_ref, v) for v in range(planes)]

    def step(j, _):
        begin = plan.start(j)
        for h in range(2):
            sums = sum_moments(planes_buf, j, weights, range(h * half, (h + 1) * half))
            put_sums(h, begin, [sums[t][m] for m in range(4) for t in range(half)])
        return 0

    lax.fori_loop(0, row_tiles, step, 0)

    def finish(v, _):
        out_copy(v).wait()
        return 0

    lax.fori_loop(0, planes, finish, 0)
    each_pack(lambda copy: copy.wait())


def advance(plan, meta, small, heights, pop, cuts):
    planes, row_tiles, lane_tiles = pop.shape[:3]
    group = math.gcd(planes, 4)
    blocks = plan.starts[-1]
    half_sums = jax.ShapeDtypeStruct((blocks, ROW, LANE), F32)
    return pl.pallas_call(
        functools.partial(advance_kernel, plan, cuts, group),
        out_shape=[pltpu.HBM(pop.shape, F32), half_sums, half_sums, jax.ShapeDtypeStruct((1,), jnp.int32)]
        + [pltpu.HBM((lane_tiles, end - begin, LANE), F32) for _, begin, end in cuts],
        in_specs=[SMEM_SPEC] * 7 + [VMEM_SPEC, HBM_SPEC],
        out_specs=[HBM_SPEC, VMEM_SPEC, VMEM_SPEC, SMEM_SPEC] + [HBM_SPEC] * len(cuts),
        scratch_shapes=[
            pltpu.VMEM((planes, lane_tiles + 2, PAD + row_tiles * ROW + ROW, LANE), F32),
            pltpu.VMEM((planes, row_tiles, lane_tiles, ROW, LANE), F32),
            pltpu.VMEM((planes, lane_tiles, ROW, LANE), F32),
            pltpu.VMEM((2, 4, ROW, LANE), F32),
            pltpu.VMEM((lane_tiles, planes * LOW_ROWS + 16, LANE), F32),
            pltpu.VMEM((lane_tiles, planes * HIGH_ROWS + 16, LANE), F32),
            pltpu.VMEM((lane_tiles, ROW, LANE), jnp.int32),
            pltpu.SemaphoreType.DMA((planes // group, row_tiles)),
            pltpu.SemaphoreType.DMA((planes,)),
            pltpu.SemaphoreType.DMA((len(cuts),)),
        ],
        compiler_params=params(36),
        name="advance",
    )(*in_hbm(meta, *small, heights, pop))


def fold_kernel(mine_ref, received_ref, *out_refs):
    begin = 0
    for ref in out_refs:
        n = ref.shape[0]
        ref[...] = mine_ref[begin : begin + n] + received_ref[begin : begin + n]
        begin += n


def fold(mine, received, sizes):
    return pl.pallas_call(
        fold_kernel,
        out_shape=[jax.ShapeDtypeStruct((n, ROW, LANE), F32) for n in sizes],
        in_specs=[VMEM_SPEC] * 2,
        out_specs=[VMEM_SPEC] * len(sizes),
        compiler_params=params(8),
        name="fold",
    )(mine, received)


def join_low_kernel(own_ref, low_ref, *refs):
    out_ref = refs[-1]
    tile = own_ref.shape[0] // 2
    half = tile // 4
    out_ref[2 * tile :] = jnp.zeros((out_ref.shape[0] - 2 * tile, ROW, LANE), F32)
    out_ref[:tile] = own_ref[:tile] + low_ref[:tile]
    top = lax.broadcasted_iota(jnp.int32, (ROW, LANE), 0) == 0
    for m in range(4):
        for n in range(half):
            row = jnp.broadcast_to(low_ref[tile + m, n : n + 1, :], (ROW, LANE))
            index = tile + m * half + n
            out_ref[index] = own_ref[index] + jnp.where(top, row, 0.0)


def add_kernel(a_ref, b_ref, *refs):
    refs[-1][...] = a_ref[...] + b_ref[...]


def join_high_kernel(own_ref, high_ref, *refs):
    out_ref = refs[-1]
    tile = high_ref.shape[0]
    out_ref[2 * tile :] = jnp.zeros((out_ref.shape[0] - 2 * tile, ROW, LANE), F32)
    out_ref[:tile] = own_ref[:tile]
    out_ref[tile : 2 * tile] = own_ref[tile:] + high_ref[...]


def small_call(kernel, name, a, b, after=(), extra=0):
    operands = a, b, *after
    shape = (a.shape[0] + extra, *a.shape[1:])
    return pl.pallas_call(
        kernel,
        out_shape=jax.ShapeDtypeStruct(shape, F32),
        in_specs=[VMEM_SPEC] * 2 + [ANY_SPEC] * len(after),
        out_specs=VMEM_SPEC,
        compiler_params=params(8),
        name=name,
    )(*operands)


def profile(density, flux_x, flux_y, energy, factor):
    inverse = 1.0 / density
    mean_x = flux_x * inverse
    mean_y = flux_y * inverse
    temperature = 0.5 * (energy * inverse - mean_x * mean_x - mean_y * mean_y)
    rate = 1.0 - jnp.exp(-factor * density / (SPEED_TALLY * jnp.sqrt(temperature)))
    height = rate * (density / (2.0 * math.pi * temperature))
    return mean_x, mean_y, -0.5 / temperature, height, 1.0 - rate


def relax_cells(get, put, values, factor, weights):
    mean_x, mean_y, scale, height, keep = profile(*values, factor)
    for v, (along_x, along_y) in enumerate(weights):
        gap_x = along_x - mean_x
        gap_y = along_y - mean_y
        state = height * jnp.exp((gap_x * gap_x + gap_y * gap_y) * scale)
        put(v, keep * get(v) + state)


def relax_tile(buf, sums, base, core, factor, weights, k, h):
    mine_ref, other_ref = sums
    half = buf.shape[2] // 2
    for n in range(half):
        t = h * half + n
        values = []
        for m in range(4):
            index = base + m * half + n
            values.append(jnp.where(core == h, mine_ref[index], other_ref[index]))

        def put(v, value):
            buf[v, k, t] = value

        relax_cells(lambda v: buf[v, k, t], put, values, factor, weights)


def relax_kernel(tiles, meta_ref, sx_ref, sy_ref, fx_ref, fy_ref, factor_ref, mine_ref, other_ref,
                 planes_ref, *refs):
    out_ref, buf, sem_in, sem_out = refs[-4:]
    planes, _, lane_tiles = planes_ref.shape[:3]
    half = lane_tiles // 2
    first_tile, count = tiles[0], len(tiles)

    def copy(k, h, out):
        lanes = pl.ds(h * half, half)
        here = buf.at[:, k, lanes]
        if out:
            return pltpu.make_async_copy(here, out_ref.at[:, first_tile + k, lanes], sem_out.at[2 * k + h])
        return pltpu.make_async_copy(planes_ref.at[:, first_tile + k, lanes], here, sem_in.at[2 * k + h])

    for k in range(count):
        for h in range(2):
            copy(k, h, False).start()
    weights = [velocity(sx_ref, sy_ref, fx_ref, fy_ref, v) for v in range(planes)]

    def step(k, _):
        for h in range(2):
            copy(k, h, False).wait()
            sums = mine_ref, other_ref
            relax_tile(buf, sums, k * 4 * half, meta_ref[3], factor_ref[0], weights, k, h)
            copy(k, h, True).start()
        return 0

    lax.fori_loop(0, count, step, 0)
    for k in range(count):
        for h in range(2):
            copy(k, h, True).wait()


def relax_tiles(tiles, meta, small, factor, sums, moved, out=None):
    planes, _, lane_tiles = moved.shape[:3]
    count = len(tiles)
    operands = [*in_hbm(meta, *small[:4]), factor, *sums, *in_hbm(moved)]
    in_specs = [SMEM_SPEC] * 6 + [VMEM_SPEC] * 2 + [HBM_SPEC]
    aliases = {}
    if out is not None:
        aliases = {len(operands): 0}
        operands.extend(in_hbm(out))
        in_specs.append(HBM_SPEC)
    return pl.pallas_call(
        functools.partial(relax_kernel, tiles),
        out_shape=pltpu.HBM(moved.shape, F32),
        in_specs=in_specs,
        out_specs=HBM_SPEC,
        scratch_shapes=[
            pltpu.VMEM((planes, count, lane_tiles, ROW, LANE), F32),
            pltpu.SemaphoreType.DMA((2 * count,)),
            pltpu.SemaphoreType.DMA((2 * count,)),
        ],
        input_output_aliases=aliases,
        compiler_params=params(24),
        name="relax_tiles",
    )(*operands)


def relax_edges_kernel(cuts, meta_ref, sx_ref, sy_ref, fx_ref, fy_ref, inflow_ref, factor_ref,
                       heights_ref, m_low, o_low, m_high, o_high, planes_ref, *refs):
    pack_refs = refs[: len(cuts)]
    _, out_ref, frames, buf, low_buf, high_buf, bars, sem_in, sem_planes, sem_out = refs[len(cuts) :]
    planes, row_tiles, lane_tiles = planes_ref.shape[:3]
    half = lane_tiles // 2
    row0, first, last, core = (meta_ref[i] for i in range(4))
    places = 0, 1, row_tiles - 1
    needs = [low_need(sy_ref[0]), high_need(sy_ref[0])]
    for v in range(1, planes):
        needs = [needs[0] + low_need(sy_ref[v]), needs[1] + high_need(sy_ref[v])]

    def pack_copy(n):
        pack, begin, end = cuts[n]
        target = (low_buf, high_buf)[pack].at[:, 16 + begin : 16 + end, :]
        return pltpu.make_async_copy(pack_refs[n], target, sem_in.at[n])

    def in_copy(k):
        return pltpu.make_async_copy(planes_ref.at[:, places[k]], buf.at[:, k], sem_planes.at[k])

    for n in range(len(cuts)):
        pl.when(needs[cuts[n][0]] > cuts[n][1])(lambda n=n: pack_copy(n).start())
    for k in (0, 2, 1):
        in_copy(k).start()
    prepare_heights(heights_ref, bars)
    for t in range(lane_tiles + 2):
        for r in (24, 32):
            frames[0, t, r : r + ROW, :] = jnp.zeros((ROW, LANE), F32)
        for r in (16, 24):
            frames[1, t, r : r + ROW, :] = jnp.zeros((ROW, LANE), F32)
    for n in range(len(cuts)):
        pl.when(needs[cuts[n][0]] > cuts[n][1])(lambda n=n: pack_copy(n).wait())
    for k in (0, 2, 1):
        in_copy(k).wait()

    def add_masked(v, k, first_row):
        def put(t, value):
            buf[v, k, t] = buf[v, k, t] + jnp.where(first_row < bars[t], 0.0, value)

        return put

    def one(v, offsets):
        low, high = offsets
        value = inflow_ref[v]
        shift = sy_ref[v]
        up = shift >= 0
        scalars = sx_ref[v], shift, fx_ref[v], fy_ref[v]
        borders = (0, lane_tiles + 1)

        @pl.when(up & (first == 0))
        def _():
            fill_rows(frames, 0, borders, 8, 16, value)
            for t in range(lane_tiles):
                for r in range(0, 16, ROW):
                    piece = low_buf[t, pl.ds(low + shift + 1 + r, ROW), :]
                    frames[0, t + 1, 8 + r : 8 + r + ROW, :] = piece
            advect(frames, 0, scalars, [(24, add_masked(v, 0, row0))])

            @pl.when(shift == CFL)
            def _():
                advect(frames, 0, scalars, [(32, add_masked(v, 1, row0 + ROW))])

        @pl.when(jnp.logical_not(up) & (last == 0))
        def _():
            fill_rows(frames, 1, borders, 32, 8, value)
            for t in range(lane_tiles):
                frames[1, t + 1, 32:40, :] = high_buf[t, pl.ds(16 + high, ROW), :]
            advect(frames, 1, scalars, [(24, add_masked(v, 2, row0 + ROW * (row_tiles - 1)))])

        return low + low_need(shift), high + high_need(shift)

    lax.fori_loop(0, planes, one, (jnp.int32(0), jnp.int32(0)))
    weights = [velocity(sx_ref, sy_ref, fx_ref, fy_ref, v) for v in range(planes)]

    def out_copy(k, h):
        j = jnp.where(k < 2, k, row_tiles - 1)
        lanes = pl.ds(h * half, half)
        return pltpu.make_async_copy(buf.at[:, k, lanes], out_ref.at[:, j, lanes], sem_out.at[2 * k + h])

    def finish(k, h, sums, base):
        relax_tile(buf, sums, base, core, factor_ref[0], weights, k, h)
        out_copy(k, h).start()

    def step(k, _):
        for h in range(2):
            finish(k, h, (m_low, o_low), k * 4 * half)
        return 0

    for h in range(2):
        finish(2, h, (m_high, o_high), 4 * half)
    lax.fori_loop(0, 2, step, 0)
    for k in range(3):
        for h in range(2):
            out_copy(k, h).wait()


def relax_edges(meta, small, factor, heights, sums, moved, packs, cuts, out):
    planes, _, lane_tiles = moved.shape[:3]
    fixed = [*in_hbm(meta, *small[:5]), factor, *in_hbm(heights)]
    operands = [*fixed, *sums, *in_hbm(moved), *packs, *in_hbm(out)]
    return pl.pallas_call(
        functools.partial(relax_edges_kernel, cuts),
        out_shape=pltpu.HBM(out.shape, F32),
        in_specs=[SMEM_SPEC] * 7
        + [VMEM_SPEC] * 5
        + [HBM_SPEC]
        + [ANY_SPEC] * len(cuts)
        + [HBM_SPEC],
        out_specs=HBM_SPEC,
        scratch_shapes=[
            pltpu.VMEM((2, lane_tiles + 2, 48, LANE), F32),
            pltpu.VMEM((planes, 3, lane_tiles, ROW, LANE), F32),
            pltpu.VMEM((lane_tiles, planes * LOW_ROWS + 32, LANE), F32),
            pltpu.VMEM((lane_tiles, planes * HIGH_ROWS + 32, LANE), F32),
            pltpu.VMEM((lane_tiles, ROW, LANE), jnp.int32),
            pltpu.SemaphoreType.DMA((len(cuts),)),
            pltpu.SemaphoreType.DMA((3,)),
            pltpu.SemaphoreType.DMA((6,)),
        ],
        input_output_aliases={len(operands) - 1: 0},
        compiler_params=params(24),
        name="relax_edges",
    )(*operands)


def per_device(populations, shift_x, shift_y, frac_x, frac_y, inflow, wall_state, heights,
               impact_frequency_factor):
    planes, row_count, col_count = populations.shape
    space_count, vel_count = lax.axis_size("space"), lax.axis_size("vel")
    row_tiles, lane_tiles = row_count // ROW, col_count // LANE
    space, vel = lax.axis_index("space"), lax.axis_index("vel")
    forward = [(i, i + 1) for i in range(space_count - 1)]
    backward = [(target, source) for source, target in forward]
    partner = [(i, i ^ 1) for i in range(vel_count)]
    across = [(i, i ^ 2) for i in range(vel_count)]

    meta = jnp.stack([space * row_count, space == 0, space == space_count - 1, vel % 2]).astype(jnp.int32)
    small = (shift_x, shift_y, frac_x, frac_y, inflow, wall_state)
    factor = impact_frequency_factor.reshape(1)
    bars = heights.reshape(lane_tiles, LANE)
    pop = populations.reshape(planes, row_tiles, ROW, lane_tiles, LANE).transpose(0, 1, 3, 2, 4)
    low_sent, high_sent = min(LOW_SENT, planes * LOW_ROWS), min(HIGH_SENT, planes * HIGH_ROWS)
    cuts = [
        (0, 0, low_sent),
        (1, 0, high_sent),
        (0, low_sent, planes * LOW_ROWS),
        (1, high_sent, planes * HIGH_ROWS),
    ]
    plan = Plan(row_tiles, lane_tiles // 2)

    moved, mine, theirs, more_needed, *packs = advance(plan, meta, small, bars, pop, cuts)
    received = lax.ppermute(theirs, "vel", partner)
    up, down, inside, edge_low, edge_high = fold(mine, received, plan.sizes)
    from_low = lax.ppermute(up, "space", forward)
    from_high = lax.ppermute(down, "space", backward)
    low_first = lax.ppermute(packs[0], "space", forward)
    high_first = lax.ppermute(packs[1], "space", backward)

    def total(sums, after=()):
        whole = small_call(add_kernel, "add", sums, lax.ppermute(sums, "vel", across), after)
        return whole, lax.ppermute(whole, "vel", partner)

    def send_more(low, high):
        return lax.ppermute(low, "space", forward), lax.ppermute(high, "space", backward)

    more = lax.cond(more_needed[0] > 0, send_more, lambda low, high: (low, high), packs[2], packs[3])
    sums_inside = total(inside)
    out = relax_tiles(plan.inside, meta, small, factor, sums_inside, moved)
    sums_low = total(small_call(join_low_kernel, "join_low", edge_low, from_low, (), 1))
    sums_high = total(small_call(join_high_kernel, "join_high", edge_high, from_high, (), 1))

    out = relax_tiles([row_tiles - 2], meta, small, factor, sums_high, moved, out)
    halo = low_first, high_first, *more
    out = relax_edges(meta, small, factor, bars, sums_low + sums_high, moved, halo, cuts, out)
    return out.transpose(0, 1, 3, 2, 4).reshape(planes, row_count, col_count)


def solution(mesh):
    return jax.shard_map(
        per_device,
        mesh=mesh,
        in_specs=(
            P("vel", "space", None),
            P("vel"),
            P("vel"),
            P("vel"),
            P("vel"),
            P("vel"),
            P("vel"),
            P(),
            P(),
        ),
        out_specs=P("vel", "space", None),
        check_vma=False,
    )
```

```python
import functools
import math

import jax
import jax.numpy as jnp
from jax import lax
from jax.experimental import pallas as pl
from jax.experimental.pallas import tpu as pltpu
from jax.sharding import PartitionSpec as P

SPEED_TALLY = 64
CFL = 8
LOW_ROWS = CFL + 1
HIGH_ROWS = CFL
ROW = 8
LANE = 128
PAD = 16
F32 = jnp.float32
LOW_SENT = 72
HIGH_SENT = 72

SMEM_SPEC = pl.BlockSpec(memory_space=pltpu.SMEM)
ANY_SPEC = pl.BlockSpec(memory_space=pl.ANY)
HBM_SPEC = pl.BlockSpec(memory_space=pltpu.HBM)
VMEM_SPEC = pl.BlockSpec(memory_space=pltpu.VMEM)


def params(mebibytes):
    return pltpu.CompilerParams(vmem_limit_bytes=mebibytes * 1024 * 1024)


def in_hbm(*arrays):
    return [pltpu.with_memory_space_constraint(x, pltpu.HBM) for x in arrays]


def low_need(shift):
    return jnp.where(shift >= 0, shift + 1, 0)


def high_need(shift):
    return jnp.where(shift < 0, -shift, 0)


def fill_rows(padded, v, columns, start, count, value):
    block = jnp.full((ROW, LANE), value, F32)
    for t in columns:
        for r in range(start, start + count, ROW):
            padded[v, t, r : r + ROW, :] = block


def prepare_heights(heights_ref, bars):
    lane_tiles = heights_ref.shape[0]
    sublane = lax.broadcasted_iota(jnp.int32, (ROW, LANE), 0)
    for t in range(lane_tiles):
        bars[t] = jnp.broadcast_to(heights_ref[t : t + 1, :], (ROW, LANE)) - sublane


def advect(padded, v, scalars, tiles):
    sx, sy, fx, fy = scalars
    lane_tiles = padded.shape[1] - 2
    lane = lax.broadcasted_iota(jnp.int32, (ROW, LANE), 1)
    near_roll = jnp.where(sx < 0, sx + LANE, sx)
    far_roll = jnp.where(sx + 1 < 0, sx + 1 + LANE, sx + 1)

    def moved(start, t):
        nearer = padded[v, t + 1, pl.ds(start, ROW), :]
        further = padded[v, t + 1, pl.ds(start - 1, ROW), :]
        line = (1.0 - fy) * nearer + fy * further
        if t < 0 or t == lane_tiles:
            return line, line
        return pltpu.roll(line, near_roll, 1), pltpu.roll(line, far_roll, 1)

    def blend(put, t, near, far):
        put(t, (1.0 - fx) * near + fx * far)

    @pl.when(sx >= 0)
    def _():
        own_near, own_far = lane >= sx, lane >= sx + 1
        for begin, put in tiles:
            before = moved(begin - sy, -1)
            for t in range(lane_tiles):
                here = moved(begin - sy, t)
                near = jnp.where(own_near, here[0], before[0])
                blend(put, t, near, jnp.where(own_far, here[1], before[1]))
                before = here

    @pl.when(sx < 0)
    def _():
        own_near, own_far = lane < sx + LANE, lane < sx + 1 + LANE
        for begin, put in tiles:
            here = moved(begin - sy, 0)
            for t in range(lane_tiles):
                after = moved(begin - sy, t + 1)
                near = jnp.where(own_near, here[0], after[0])
                blend(put, t, near, jnp.where(own_far, here[1], after[1]))
                here = after


def store_masked(target, bars, first_row, solid_value):
    def put(t, value):
        target[t] = jnp.where(first_row < bars[t], solid_value, value)

    return put


def velocity(sx_ref, sy_ref, fx_ref, fy_ref, v):
    return sx_ref[v].astype(F32) + fx_ref[v], sy_ref[v].astype(F32) + fy_ref[v]


def sum_moments(planes_ref, k, weights, lane_tile_range):
    sums = [[None] * 4 for _ in lane_tile_range]
    for v, (along_x, along_y) in enumerate(weights):
        square = along_x * along_x + along_y * along_y
        for n, t in enumerate(lane_tile_range):
            f = planes_ref[v, k, t]
            terms = (f, f * along_x, f * along_y, f * square)
            sums[n] = [b if a is None else a + b for a, b in zip(sums[n], terms)]
    return sums


class Plan:
    def __init__(self, row_tiles, half):
        self.tile = 4 * half
        self.inside = list(range(2, row_tiles - 2))
        self.sizes = [self.tile + 4, self.tile, len(self.inside) * self.tile, 2 * self.tile, 2 * self.tile]
        self.starts = [sum(self.sizes[:n]) for n in range(len(self.sizes) + 1)]
        self.row_tiles = row_tiles

    def start(self, j):
        low = self.starts[3] + self.tile * j
        high = self.starts[4] + self.tile * (j - self.row_tiles + 2)
        inside = self.starts[2] + self.tile * (j - 2)
        return jnp.where(j < 2, low, jnp.where(j >= self.row_tiles - 2, high, inside))


def advance_kernel(plan, cuts, group, meta_ref, sx_ref, sy_ref, fx_ref, fy_ref, inflow_ref, wall_ref,
                   heights_ref, pop_ref, *refs):
    planes_ref, mine_ref, theirs_ref, more_ref = refs[:4]
    packs = refs[4 : 4 + len(cuts)]
    (padded, planes_buf, outer, last_row, low_pack, high_pack, bars, sem_in, sem_planes, sem_out) = refs[
        4 + len(cuts) :
    ]
    planes, row_tiles, lane_tiles = pop_ref.shape[:3]
    half = lane_tiles // 2
    rows = row_tiles * ROW
    row0, first, last, core = (meta_ref[i] for i in range(4))

    def loads(g):
        members = pl.ds(g * group, group)
        return [
            pltpu.make_async_copy(
                pop_ref.at[members, i],
                padded.at[members, 1 : 1 + lane_tiles, PAD + ROW * i : PAD + ROW * (i + 1), :],
                sem_in.at[g, i],
            )
            for i in range(row_tiles)
        ]

    def start(g, _):
        for load in loads(g):
            load.start()
        return 0

    lax.fori_loop(0, planes // group, start, 0)
    prepare_heights(heights_ref, bars)
    last_row[...] = jnp.zeros_like(last_row)

    def put_sums(h, first_block, sums):
        for is_mine, ref in ((True, mine_ref), (False, theirs_ref)):

            @pl.when((core == h) == is_mine)
            def _():
                for n, value in enumerate(sums):
                    ref[first_block + n] = value


    def out_copy(v):
        return pltpu.make_async_copy(planes_buf.at[v], planes_ref.at[v], sem_planes.at[v])

    def one(v, offsets):
        low, high = offsets
        value = inflow_ref[v]
        shift = sy_ref[v]
        up = shift >= 0
        columns = range(lane_tiles + 2)
        fill_rows(padded, v, (0, lane_tiles + 1), PAD, rows, value)
        fill_rows(padded, v, columns, 0, PAD, jnp.where(first == 1, value, 0.0))
        fill_rows(padded, v, columns, PAD + rows, ROW, jnp.where(last == 1, value, 0.0))

        @pl.when(v % group == 0)
        def _():
            for load in loads(v // group):
                load.wait()

        scalars = sx_ref[v], shift, fx_ref[v], fy_ref[v]
        work = [
            (PAD + ROW * j, store_masked(planes_buf.at[v, j], bars, row0 + ROW * j, wall_ref[v]))
            for j in range(row_tiles)
        ]
        beyond = jnp.where(up, rows, -ROW)
        work.append((PAD + beyond, store_masked(outer.at[v], bars, row0 + beyond, 0.0)))
        advect(padded, v, scalars, work)
        out_copy(v).start()

        @pl.when(shift == CFL)
        def _():
            along_x, along_y = velocity(sx_ref, sy_ref, fx_ref, fy_ref, v)
            factors = 1.0, along_x, along_y, along_x * along_x + along_y * along_y

            def put(t, value):
                row = jnp.where(row0 + rows + ROW < bars[t], 0.0, value)
                h, r = divmod(t, half)
                for m in range(4):
                    total = last_row[h, m, r : r + 1, :] + (row * factors[m])[0:1, :]
                    last_row[h, m, r : r + 1, :] = total

            advect(padded, v, scalars, [(PAD + rows + ROW, put)])

        @pl.when(up)
        def _():
            for t in range(lane_tiles):
                source = pl.ds(PAD + rows - 1 - shift, 8)
                low_pack[t, pl.ds(low, 8), :] = padded[v, t + 1, source, :]

        @pl.when(shift == CFL)
        def _():
            for t in range(lane_tiles):
                low_pack[t, pl.ds(low + 8, 1), :] = padded[v, t + 1, PAD + rows - 1 : PAD + rows, :]

        @pl.when(jnp.logical_not(up))
        def _():
            for t in range(lane_tiles):
                high_pack[t, pl.ds(high, 8), :] = padded[v, t + 1, PAD : PAD + 8, :]

        return low + low_need(shift), high + high_need(shift)

    needs = lax.fori_loop(0, planes, one, (jnp.int32(0), jnp.int32(0)))
    sent = [end for _, begin, end in cuts if begin == 0]
    overflows = (needs[0] > sent[0]) | (needs[1] > sent[1])
    more_ref[0] = jnp.where(overflows, 1, 0)

    def pack_copy(n):
        pack, begin, end = cuts[n]
        source = (low_pack, high_pack)[pack].at[:, begin:end, :]
        return pltpu.make_async_copy(source, packs[n], sem_out.at[n])

    def each_pack(act):
        for n, (_, begin, _) in enumerate(cuts):
            if begin == 0:
                act(pack_copy(n))
            else:
                pl.when(overflows)(lambda n=n: act(pack_copy(n)))

    each_pack(lambda copy: copy.start())
    for h in range(2):
        put_sums(h, plan.tile, [last_row[h, m] for m in range(4)])
        for rising in (True, False):
            for part in range(2):
                tiles = range(h * half + part * half // 2, h * half + (part + 1) * half // 2)
                sums = [[None] * 4 for _ in tiles]
                for v in range(planes):
                    along_x, along_y = velocity(sx_ref, sy_ref, fx_ref, fy_ref, v)
                    goes = jnp.where((sy_ref[v] >= 0) == rising, 1.0, 0.0)
                    square = (along_x * along_x + along_y * along_y) * goes
                    factors = goes, along_x * goes, along_y * goes, square
                    for n, t in enumerate(tiles):
                        f = outer[v, t]
                        terms = [f * w for w in factors]
                        sums[n] = [b if a is None else a + b for a, b in zip(sums[n], terms)]
                begin = plan.starts[0 if rising else 1] + part * half // 2
                for m in range(4):
                    put_sums(h, begin + m * half, [sums[n][m] for n in range(len(tiles))])
    weights = [velocity(sx_ref, sy_ref, fx_ref, fy_ref, v) for v in range(planes)]

    def step(j, _):
        begin = plan.start(j)
        for h in range(2):
            sums = sum_moments(planes_buf, j, weights, range(h * half, (h + 1) * half))
            put_sums(h, begin, [sums[t][m] for m in range(4) for t in range(half)])
        return 0

    lax.fori_loop(0, row_tiles, step, 0)

    def finish(v, _):
        out_copy(v).wait()
        return 0

    lax.fori_loop(0, planes, finish, 0)
    each_pack(lambda copy: copy.wait())


def advance(plan, meta, small, heights, pop, cuts):
    planes, row_tiles, lane_tiles = pop.shape[:3]
    group = math.gcd(planes, 4)
    blocks = plan.starts[-1]
    half_sums = jax.ShapeDtypeStruct((blocks, ROW, LANE), F32)
    return pl.pallas_call(
        functools.partial(advance_kernel, plan, cuts, group),
        out_shape=[pltpu.HBM(pop.shape, F32), half_sums, half_sums, jax.ShapeDtypeStruct((1,), jnp.int32)]
        + [pltpu.HBM((lane_tiles, end - begin, LANE), F32) for _, begin, end in cuts],
        in_specs=[SMEM_SPEC] * 7 + [VMEM_SPEC, HBM_SPEC],
        out_specs=[HBM_SPEC, VMEM_SPEC, VMEM_SPEC, SMEM_SPEC] + [HBM_SPEC] * len(cuts),
        scratch_shapes=[
            pltpu.VMEM((planes, lane_tiles + 2, PAD + row_tiles * ROW + ROW, LANE), F32),
            pltpu.VMEM((planes, row_tiles, lane_tiles, ROW, LANE), F32),
            pltpu.VMEM((planes, lane_tiles, ROW, LANE), F32),
            pltpu.VMEM((2, 4, ROW, LANE), F32),
            pltpu.VMEM((lane_tiles, planes * LOW_ROWS + 16, LANE), F32),
            pltpu.VMEM((lane_tiles, planes * HIGH_ROWS + 16, LANE), F32),
            pltpu.VMEM((lane_tiles, ROW, LANE), jnp.int32),
            pltpu.SemaphoreType.DMA((planes // group, row_tiles)),
            pltpu.SemaphoreType.DMA((planes,)),
            pltpu.SemaphoreType.DMA((len(cuts),)),
        ],
        compiler_params=params(36),
        name="advance",
    )(*in_hbm(meta, *small, heights, pop))


def fold_kernel(mine_ref, received_ref, *out_refs):
    begin = 0
    for ref in out_refs:
        n = ref.shape[0]
        ref[...] = mine_ref[begin : begin + n] + received_ref[begin : begin + n]
        begin += n


def fold(mine, received, sizes):
    return pl.pallas_call(
        fold_kernel,
        out_shape=[jax.ShapeDtypeStruct((n, ROW, LANE), F32) for n in sizes],
        in_specs=[VMEM_SPEC] * 2,
        out_specs=[VMEM_SPEC] * len(sizes),
        compiler_params=params(8),
        name="fold",
    )(mine, received)


def join_low_kernel(own_ref, low_ref, *refs):
    out_ref = refs[-1]
    tile = own_ref.shape[0] // 2
    half = tile // 4
    out_ref[2 * tile :] = jnp.zeros((out_ref.shape[0] - 2 * tile, ROW, LANE), F32)
    out_ref[:tile] = own_ref[:tile] + low_ref[:tile]
    top = lax.broadcasted_iota(jnp.int32, (ROW, LANE), 0) == 0
    for m in range(4):
        for n in range(half):
            row = jnp.broadcast_to(low_ref[tile + m, n : n + 1, :], (ROW, LANE))
            index = tile + m * half + n
            out_ref[index] = own_ref[index] + jnp.where(top, row, 0.0)


def add_kernel(a_ref, b_ref, *refs):
    refs[-1][...] = a_ref[...] + b_ref[...]


def join_high_kernel(own_ref, high_ref, *refs):
    out_ref = refs[-1]
    tile = high_ref.shape[0]
    out_ref[2 * tile :] = jnp.zeros((out_ref.shape[0] - 2 * tile, ROW, LANE), F32)
    out_ref[:tile] = own_ref[:tile]
    out_ref[tile : 2 * tile] = own_ref[tile:] + high_ref[...]


def small_call(kernel, name, a, b, after=(), extra=0):
    operands = a, b, *after
    shape = (a.shape[0] + extra, *a.shape[1:])
    return pl.pallas_call(
        kernel,
        out_shape=jax.ShapeDtypeStruct(shape, F32),
        in_specs=[VMEM_SPEC] * 2 + [ANY_SPEC] * len(after),
        out_specs=VMEM_SPEC,
        compiler_params=params(8),
        name=name,
    )(*operands)


def profile(density, flux_x, flux_y, energy, factor):
    inverse = 1.0 / density
    mean_x = flux_x * inverse
    mean_y = flux_y * inverse
    temperature = 0.5 * (energy * inverse - mean_x * mean_x - mean_y * mean_y)
    rate = 1.0 - jnp.exp(-factor * density / (SPEED_TALLY * jnp.sqrt(temperature)))
    height = rate * (density / (2.0 * math.pi * temperature))
    return mean_x, mean_y, -0.5 / temperature, height, 1.0 - rate


def relax_cells(get, put, values, factor, weights):
    mean_x, mean_y, scale, height, keep = profile(*values, factor)
    for v, (along_x, along_y) in enumerate(weights):
        gap_x = along_x - mean_x
        gap_y = along_y - mean_y
        state = height * jnp.exp((gap_x * gap_x + gap_y * gap_y) * scale)
        put(v, keep * get(v) + state)


def relax_tile(buf, sums, base, core, factor, weights, k, h):
    mine_ref, other_ref = sums
    half = buf.shape[2] // 2
    for n in range(half):
        t = h * half + n
        values = []
        for m in range(4):
            index = base + m * half + n
            values.append(jnp.where(core == h, mine_ref[index], other_ref[index]))

        def put(v, value):
            buf[v, k, t] = value

        relax_cells(lambda v: buf[v, k, t], put, values, factor, weights)


def relax_kernel(sizes, meta_ref, sx_ref, sy_ref, fx_ref, fy_ref, factor_ref, planes_ref, *refs):
    sums_refs = refs[:-4]
    out_ref, buf, sem_in, sem_out = refs[-4:]
    planes, row_tiles, lane_tiles = planes_ref.shape[:3]
    half = lane_tiles // 2

    def copy(j, h, out):
        lanes = pl.ds(h * half, half)
        here = buf.at[:, j, lanes]
        if out:
            return pltpu.make_async_copy(here, out_ref.at[:, j, lanes], sem_out.at[2 * j + h])
        return pltpu.make_async_copy(planes_ref.at[:, j, lanes], here, sem_in.at[2 * j + h])

    def tile(k):
        return jnp.where(k < row_tiles - 2, k + 2, k + 2 - row_tiles)

    def start(k, _):
        for h in range(2):
            copy(tile(k), h, False).start()
        return 0

    lax.fori_loop(0, row_tiles, start, 0)
    weights = [velocity(sx_ref, sy_ref, fx_ref, fy_ref, v) for v in range(planes)]
    begin = 0
    for pair, size in enumerate(sizes):
        sums = sums_refs[2 * pair : 2 * pair + 2]

        def step(k, _, begin=begin, sums=sums):
            j = tile(k)
            for h in range(2):
                copy(j, h, False).wait()
                base = (k - begin) * 4 * half
                relax_tile(buf, sums, base, meta_ref[3], factor_ref[0], weights, j, h)
                copy(j, h, True).start()
            return 0

        lax.fori_loop(begin, begin + size, step, 0)
        begin += size

    def finish(j, _):
        for h in range(2):
            copy(j, h, True).wait()
        return 0

    lax.fori_loop(0, row_tiles, finish, 0)


def relax_all(sizes, meta, small, factor, sums, moved):
    planes, row_tiles, lane_tiles = moved.shape[:3]
    operands = [*in_hbm(meta, *small[:4]), factor, *in_hbm(moved), *sums]
    return pl.pallas_call(
        functools.partial(relax_kernel, sizes),
        out_shape=pltpu.HBM(moved.shape, F32),
        in_specs=[SMEM_SPEC] * 6 + [HBM_SPEC] + [VMEM_SPEC] * len(sums),
        out_specs=HBM_SPEC,
        scratch_shapes=[
            pltpu.VMEM((planes, row_tiles, lane_tiles, ROW, LANE), F32),
            pltpu.SemaphoreType.DMA((2 * row_tiles,)),
            pltpu.SemaphoreType.DMA((2 * row_tiles,)),
        ],
        compiler_params=params(24),
        name="relax_all",
    )(*operands)


def finish_kernel(cuts, meta_ref, sx_ref, sy_ref, fx_ref, fy_ref, inflow_ref, factor_ref, heights_ref,
                  m_low, o_low, m_high, o_high, before_ref, *refs):
    pack_refs = refs[: len(cuts)]
    out_ref, frames, buf, keeps, low_buf, high_buf, bars, sem_in, sem_planes, sem_out = refs[len(cuts) :]
    planes, row_tiles, lane_tiles = before_ref.shape[:3]
    half = lane_tiles // 2
    row0, first, last, core = (meta_ref[i] for i in range(4))
    needs = [low_need(sy_ref[0]), high_need(sy_ref[0])]
    for v in range(1, planes):
        needs = [needs[0] + low_need(sy_ref[v]), needs[1] + high_need(sy_ref[v])]

    def pack_copy(n):
        pack, begin, end = cuts[n]
        target = (low_buf, high_buf)[pack].at[:, 16 + begin : 16 + end, :]
        return pltpu.make_async_copy(pack_refs[n], target, sem_in.at[n])

    def cases(v):
        shift = sy_ref[v]
        from_low = (shift >= 0) & (first == 0)
        return from_low, (shift < 0) & (last == 0), from_low & (shift == CFL)

    tile_of = 0, row_tiles - 1, 1
    slot_of = 0, 0, 1

    def copy(v, case, out):
        here = buf.at[v, slot_of[case]]
        if out:
            return pltpu.make_async_copy(here, out_ref.at[v, tile_of[case]], sem_out.at[v, slot_of[case]])
        there = before_ref.at[v, tile_of[case]]
        return pltpu.make_async_copy(there, here, sem_planes.at[v, slot_of[case]])

    for n in range(len(cuts)):
        pl.when(needs[cuts[n][0]] > cuts[n][1])(lambda n=n: pack_copy(n).start())

    def start(v, _):
        for case, applies in enumerate(cases(v)):
            pl.when(applies)(lambda case=case: copy(v, case, False).start())
        return 0

    lax.fori_loop(0, planes, start, 0)
    prepare_heights(heights_ref, bars)
    for t in range(lane_tiles + 2):
        for r in (24, 32):
            frames[0, t, r : r + ROW, :] = jnp.zeros((ROW, LANE), F32)
        for r in (16, 24):
            frames[1, t, r : r + ROW, :] = jnp.zeros((ROW, LANE), F32)
    edges = ((m_low, o_low), 0), ((m_high, o_high), 4 * half), ((m_low, o_low), 4 * half)
    for case, (sums, base) in enumerate(edges):
        for t in range(lane_tiles):
            h, n = divmod(t, half)
            values = []
            for m in range(4):
                index = base + m * half + n
                values.append(jnp.where(core == h, sums[0][index], sums[1][index]))
            keeps[case, t] = profile(*values, factor_ref[0])[4]
    for n in range(len(cuts)):
        pl.when(needs[cuts[n][0]] > cuts[n][1])(lambda n=n: pack_copy(n).wait())

    def add_masked(v, case):
        first_row = row0 + ROW * tile_of[case]

        def put(t, value):
            part = jnp.where(first_row < bars[t], 0.0, value)
            buf[v, slot_of[case], t] = buf[v, slot_of[case], t] + keeps[case, t] * part

        return put

    def one(v, offsets):
        low, high = offsets
        value = inflow_ref[v]
        shift = sy_ref[v]
        scalars = sx_ref[v], shift, fx_ref[v], fy_ref[v]
        borders = (0, lane_tiles + 1)
        from_low, from_high, reaches_second = cases(v)

        @pl.when(from_low)
        def _():
            fill_rows(frames, 0, borders, 8, 16, value)
            for t in range(lane_tiles):
                for r in range(0, 16, ROW):
                    piece = low_buf[t, pl.ds(low + shift + 1 + r, ROW), :]
                    frames[0, t + 1, 8 + r : 8 + r + ROW, :] = piece
            copy(v, 0, False).wait()
            advect(frames, 0, scalars, [(24, add_masked(v, 0))])
            copy(v, 0, True).start()

        @pl.when(reaches_second)
        def _():
            copy(v, 2, False).wait()
            advect(frames, 0, scalars, [(32, add_masked(v, 2))])
            copy(v, 2, True).start()

        @pl.when(from_high)
        def _():
            fill_rows(frames, 1, borders, 32, 8, value)
            for t in range(lane_tiles):
                frames[1, t + 1, 32:40, :] = high_buf[t, pl.ds(16 + high, ROW), :]
            copy(v, 1, False).wait()
            advect(frames, 1, scalars, [(24, add_masked(v, 1))])
            copy(v, 1, True).start()

        return low + low_need(shift), high + high_need(shift)

    lax.fori_loop(0, planes, one, (jnp.int32(0), jnp.int32(0)))

    def end(v, _):
        for case, applies in enumerate(cases(v)):
            pl.when(applies)(lambda case=case: copy(v, case, True).wait())
        return 0

    lax.fori_loop(0, planes, end, 0)


def finish_edges(meta, small, factor, heights, sums, packs, cuts, out):
    planes, _, lane_tiles = out.shape[:3]
    fixed = [*in_hbm(meta, *small[:5]), factor, *in_hbm(heights)]
    operands = [*fixed, *sums, *in_hbm(out), *packs]
    return pl.pallas_call(
        functools.partial(finish_kernel, cuts),
        out_shape=pltpu.HBM(out.shape, F32),
        in_specs=[SMEM_SPEC] * 7 + [VMEM_SPEC] * 5 + [HBM_SPEC] + [ANY_SPEC] * len(cuts),
        out_specs=HBM_SPEC,
        scratch_shapes=[
            pltpu.VMEM((2, lane_tiles + 2, 48, LANE), F32),
            pltpu.VMEM((planes, 2, lane_tiles, ROW, LANE), F32),
            pltpu.VMEM((3, lane_tiles, ROW, LANE), F32),
            pltpu.VMEM((lane_tiles, planes * LOW_ROWS + 32, LANE), F32),
            pltpu.VMEM((lane_tiles, planes * HIGH_ROWS + 32, LANE), F32),
            pltpu.VMEM((lane_tiles, ROW, LANE), jnp.int32),
            pltpu.SemaphoreType.DMA((len(cuts),)),
            pltpu.SemaphoreType.DMA((planes, 2)),
            pltpu.SemaphoreType.DMA((planes, 2)),
        ],
        input_output_aliases={len(fixed) + len(sums): 0},
        compiler_params=params(24),
        name="finish_edges",
    )(*operands)


def per_device(populations, shift_x, shift_y, frac_x, frac_y, inflow, wall_state, heights,
               impact_frequency_factor):
    planes, row_count, col_count = populations.shape
    space_count, vel_count = lax.axis_size("space"), lax.axis_size("vel")
    row_tiles, lane_tiles = row_count // ROW, col_count // LANE
    space, vel = lax.axis_index("space"), lax.axis_index("vel")
    forward = [(i, i + 1) for i in range(space_count - 1)]
    backward = [(target, source) for source, target in forward]
    partner = [(i, i ^ 1) for i in range(vel_count)]
    across = [(i, i ^ 2) for i in range(vel_count)]

    meta = jnp.stack([space * row_count, space == 0, space == space_count - 1, vel % 2]).astype(jnp.int32)
    small = (shift_x, shift_y, frac_x, frac_y, inflow, wall_state)
    factor = impact_frequency_factor.reshape(1)
    bars = heights.reshape(lane_tiles, LANE)
    pop = populations.reshape(planes, row_tiles, ROW, lane_tiles, LANE).transpose(0, 1, 3, 2, 4)
    low_sent, high_sent = min(LOW_SENT, planes * LOW_ROWS), min(HIGH_SENT, planes * HIGH_ROWS)
    cuts = [
        (0, 0, low_sent),
        (1, 0, high_sent),
        (0, low_sent, planes * LOW_ROWS),
        (1, high_sent, planes * HIGH_ROWS),
    ]
    plan = Plan(row_tiles, lane_tiles // 2)

    moved, mine, theirs, more_needed, *packs = advance(plan, meta, small, bars, pop, cuts)
    received = lax.ppermute(theirs, "vel", partner)
    up, down, inside, edge_low, edge_high = fold(mine, received, plan.sizes)
    from_low = lax.ppermute(up, "space", forward)
    from_high = lax.ppermute(down, "space", backward)
    low_first = lax.ppermute(packs[0], "space", forward)
    high_first = lax.ppermute(packs[1], "space", backward)

    def total(sums, after=()):
        whole = small_call(add_kernel, "add", sums, lax.ppermute(sums, "vel", across), after)
        return whole, lax.ppermute(whole, "vel", partner)

    def send_more(low, high):
        return lax.ppermute(low, "space", forward), lax.ppermute(high, "space", backward)

    more = lax.cond(more_needed[0] > 0, send_more, lambda low, high: (low, high), packs[2], packs[3])
    sums_inside = total(inside)
    sums_low = total(small_call(join_low_kernel, "join_low", edge_low, from_low, (), 1))
    sums_high = total(small_call(join_high_kernel, "join_high", edge_high, from_high, (), 1))
    sizes = len(plan.inside), 2, 2
    out = relax_all(sizes, meta, small, factor, sums_inside + sums_high + sums_low, moved)
    halo = low_first, high_first, *more
    out = finish_edges(meta, small, factor, bars, sums_low + sums_high, halo, cuts, out)
    return out.transpose(0, 1, 3, 2, 4).reshape(planes, row_count, col_count)


def solution(mesh):
    return jax.shard_map(
        per_device,
        mesh=mesh,
        in_specs=(
            P("vel", "space", None),
            P("vel"),
            P("vel"),
            P("vel"),
            P("vel"),
            P("vel"),
            P("vel"),
            P(),
            P(),
        ),
        out_specs=P("vel", "space", None),
        check_vma=False,
    )
```

```python
import functools
import math

import jax
import jax.numpy as jnp
from jax import lax
from jax.experimental import pallas as pl
from jax.experimental.pallas import tpu as pltpu
from jax.sharding import PartitionSpec as P

SPEED_TALLY = 64
CFL = 8
LOW_ROWS = CFL + 1
HIGH_ROWS = CFL
ROW = 8
LANE = 128
PAD = 16
F32 = jnp.float32
LOW_SENT = 72
HIGH_SENT = 72

SMEM_SPEC = pl.BlockSpec(memory_space=pltpu.SMEM)
ANY_SPEC = pl.BlockSpec(memory_space=pl.ANY)
HBM_SPEC = pl.BlockSpec(memory_space=pltpu.HBM)
VMEM_SPEC = pl.BlockSpec(memory_space=pltpu.VMEM)


def params(mebibytes):
    return pltpu.CompilerParams(vmem_limit_bytes=mebibytes * 1024 * 1024)


def in_hbm(*arrays):
    return [pltpu.with_memory_space_constraint(x, pltpu.HBM) for x in arrays]


def place(rows):
    space = lax.axis_index("space")
    return space * rows, space == 0, space == lax.axis_size("space") - 1, lax.axis_index("vel") % 2


def low_need(shift):
    return jnp.where(shift >= 0, shift + 1, 0)


def high_need(shift):
    return jnp.where(shift < 0, -shift, 0)


def fill_rows(padded, v, columns, start, count, value):
    block = jnp.full((ROW, LANE), value, F32)
    for t in columns:
        for r in range(start, start + count, ROW):
            padded[v, t, r : r + ROW, :] = block


def prepare_heights(heights_ref, bars):
    lane_tiles = heights_ref.shape[0]
    sublane = lax.broadcasted_iota(jnp.int32, (ROW, LANE), 0)
    for t in range(lane_tiles):
        bars[t] = jnp.broadcast_to(heights_ref[t : t + 1, :], (ROW, LANE)) - sublane


def advect(padded, v, scalars, tiles):
    sx, sy, fx, fy = scalars
    lane_tiles = padded.shape[1] - 2
    lane = lax.broadcasted_iota(jnp.int32, (ROW, LANE), 1)
    near_roll = jnp.where(sx < 0, sx + LANE, sx)
    far_roll = jnp.where(sx + 1 < 0, sx + 1 + LANE, sx + 1)

    def moved(start, t):
        nearer = padded[v, t + 1, pl.ds(start, ROW), :]
        further = padded[v, t + 1, pl.ds(start - 1, ROW), :]
        line = (1.0 - fy) * nearer + fy * further
        if t < 0 or t == lane_tiles:
            return line, line
        return pltpu.roll(line, near_roll, 1), pltpu.roll(line, far_roll, 1)

    def blend(put, t, near, far):
        put(t, (1.0 - fx) * near + fx * far)

    @pl.when(sx >= 0)
    def _():
        own_near, own_far = lane >= sx, lane >= sx + 1
        for begin, put in tiles:
            before = moved(begin - sy, -1)
            for t in range(lane_tiles):
                here = moved(begin - sy, t)
                near = jnp.where(own_near, here[0], before[0])
                blend(put, t, near, jnp.where(own_far, here[1], before[1]))
                before = here

    @pl.when(sx < 0)
    def _():
        own_near, own_far = lane < sx + LANE, lane < sx + 1 + LANE
        for begin, put in tiles:
            here = moved(begin - sy, 0)
            for t in range(lane_tiles):
                after = moved(begin - sy, t + 1)
                near = jnp.where(own_near, here[0], after[0])
                blend(put, t, near, jnp.where(own_far, here[1], after[1]))
                here = after


def store_masked(target, bars, first_row, solid_value):
    def put(t, value):
        target[t] = jnp.where(first_row < bars[t], solid_value, value)

    return put


def velocity(sx_ref, sy_ref, fx_ref, fy_ref, v):
    return sx_ref[v].astype(F32) + fx_ref[v], sy_ref[v].astype(F32) + fy_ref[v]


def sum_moments(planes_ref, k, weights, lane_tile_range):
    sums = [[None] * 4 for _ in lane_tile_range]
    for v, (along_x, along_y) in enumerate(weights):
        square = along_x * along_x + along_y * along_y
        for n, t in enumerate(lane_tile_range):
            f = planes_ref[v, k, t]
            terms = (f, f * along_x, f * along_y, f * square)
            sums[n] = [b if a is None else a + b for a, b in zip(sums[n], terms)]
    return sums


class Plan:
    def __init__(self, row_tiles, half):
        self.tile = 4 * half
        self.inside = list(range(2, row_tiles - 2))
        self.sizes = [self.tile + 4, self.tile, len(self.inside) * self.tile, 2 * self.tile, 2 * self.tile]
        self.starts = [sum(self.sizes[:n]) for n in range(len(self.sizes) + 1)]
        self.row_tiles = row_tiles

    def start(self, j):
        low = self.starts[3] + self.tile * j
        high = self.starts[4] + self.tile * (j - self.row_tiles + 2)
        inside = self.starts[2] + self.tile * (j - 2)
        return jnp.where(j < 2, low, jnp.where(j >= self.row_tiles - 2, high, inside))


def advance_kernel(plan, cuts, group, sx_ref, sy_ref, fx_ref, fy_ref, inflow_ref, wall_ref,
                   heights_ref, pop_ref, *refs):
    planes_ref, mine_ref, theirs_ref, more_ref = refs[:4]
    packs = refs[4 : 4 + len(cuts)]
    (padded, planes_buf, outer, last_row, low_pack, high_pack, bars, sem_in, sem_planes, sem_out) = refs[
        4 + len(cuts) :
    ]
    planes, row_tiles, lane_tiles = pop_ref.shape[:3]
    half = lane_tiles // 2
    rows = row_tiles * ROW
    row0, first, last, core = place(rows)

    def loads(g):
        members = pl.ds(g * group, group)
        return [
            pltpu.make_async_copy(
                pop_ref.at[members, i],
                padded.at[members, 1 : 1 + lane_tiles, PAD + ROW * i : PAD + ROW * (i + 1), :],
                sem_in.at[g, i],
            )
            for i in range(row_tiles)
        ]

    def start(g, _):
        for load in loads(g):
            load.start()
        return 0

    lax.fori_loop(0, planes // group, start, 0)
    prepare_heights(heights_ref, bars)
    last_row[...] = jnp.zeros_like(last_row)

    def put_sums(h, first_block, sums):
        for is_mine, ref in ((True, mine_ref), (False, theirs_ref)):

            @pl.when((core == h) == is_mine)
            def _():
                for n, value in enumerate(sums):
                    ref[first_block + n] = value


    def out_copy(v):
        return pltpu.make_async_copy(planes_buf.at[v], planes_ref.at[v], sem_planes.at[v])

    def one(v, offsets):
        low, high = offsets
        value = inflow_ref[v]
        shift = sy_ref[v]
        up = shift >= 0
        columns = range(lane_tiles + 2)
        fill_rows(padded, v, (0, lane_tiles + 1), PAD, rows, value)
        fill_rows(padded, v, columns, 0, PAD, jnp.where(first, value, 0.0))
        fill_rows(padded, v, columns, PAD + rows, ROW, jnp.where(last, value, 0.0))

        @pl.when(v % group == 0)
        def _():
            for load in loads(v // group):
                load.wait()

        scalars = sx_ref[v], shift, fx_ref[v], fy_ref[v]
        work = [
            (PAD + ROW * j, store_masked(planes_buf.at[v, j], bars, row0 + ROW * j, wall_ref[v]))
            for j in range(row_tiles)
        ]
        beyond = jnp.where(up, rows, -ROW)
        work.append((PAD + beyond, store_masked(outer.at[v], bars, row0 + beyond, 0.0)))
        advect(padded, v, scalars, work)
        out_copy(v).start()

        @pl.when(shift == CFL)
        def _():
            along_x, along_y = velocity(sx_ref, sy_ref, fx_ref, fy_ref, v)
            factors = 1.0, along_x, along_y, along_x * along_x + along_y * along_y

            def put(t, value):
                row = jnp.where(row0 + rows + ROW < bars[t], 0.0, value)
                h, r = divmod(t, half)
                for m in range(4):
                    total = last_row[h, m, r : r + 1, :] + (row * factors[m])[0:1, :]
                    last_row[h, m, r : r + 1, :] = total

            advect(padded, v, scalars, [(PAD + rows + ROW, put)])

        @pl.when(up)
        def _():
            for t in range(lane_tiles):
                source = pl.ds(PAD + rows - 1 - shift, 8)
                low_pack[t, pl.ds(low, 8), :] = padded[v, t + 1, source, :]

        @pl.when(shift == CFL)
        def _():
            for t in range(lane_tiles):
                low_pack[t, pl.ds(low + 8, 1), :] = padded[v, t + 1, PAD + rows - 1 : PAD + rows, :]

        @pl.when(jnp.logical_not(up))
        def _():
            for t in range(lane_tiles):
                high_pack[t, pl.ds(high, 8), :] = padded[v, t + 1, PAD : PAD + 8, :]

        return low + low_need(shift), high + high_need(shift)

    needs = lax.fori_loop(0, planes, one, (jnp.int32(0), jnp.int32(0)))
    sent = [end for _, begin, end in cuts if begin == 0]
    overflows = (needs[0] > sent[0]) | (needs[1] > sent[1])
    more_ref[0] = jnp.where(overflows, 1, 0)

    def pack_copy(n):
        pack, begin, end = cuts[n]
        source = (low_pack, high_pack)[pack].at[:, begin:end, :]
        return pltpu.make_async_copy(source, packs[n], sem_out.at[n])

    def each_pack(act):
        for n, (_, begin, _) in enumerate(cuts):
            if begin == 0:
                act(pack_copy(n))
            else:
                pl.when(overflows)(lambda n=n: act(pack_copy(n)))

    each_pack(lambda copy: copy.start())
    for h in range(2):
        put_sums(h, plan.tile, [last_row[h, m] for m in range(4)])
        for rising in (True, False):
            for part in range(2):
                tiles = range(h * half + part * half // 2, h * half + (part + 1) * half // 2)
                sums = [[None] * 4 for _ in tiles]
                for v in range(planes):
                    along_x, along_y = velocity(sx_ref, sy_ref, fx_ref, fy_ref, v)
                    goes = jnp.where((sy_ref[v] >= 0) == rising, 1.0, 0.0)
                    square = (along_x * along_x + along_y * along_y) * goes
                    factors = goes, along_x * goes, along_y * goes, square
                    for n, t in enumerate(tiles):
                        f = outer[v, t]
                        terms = [f * w for w in factors]
                        sums[n] = [b if a is None else a + b for a, b in zip(sums[n], terms)]
                begin = plan.starts[0 if rising else 1] + part * half // 2
                for m in range(4):
                    put_sums(h, begin + m * half, [sums[n][m] for n in range(len(tiles))])
    weights = [velocity(sx_ref, sy_ref, fx_ref, fy_ref, v) for v in range(planes)]

    def step(j, _):
        begin = plan.start(j)
        for h in range(2):
            sums = sum_moments(planes_buf, j, weights, range(h * half, (h + 1) * half))
            put_sums(h, begin, [sums[t][m] for m in range(4) for t in range(half)])
        return 0

    lax.fori_loop(0, row_tiles, step, 0)

    def finish(v, _):
        out_copy(v).wait()
        return 0

    lax.fori_loop(0, planes, finish, 0)
    each_pack(lambda copy: copy.wait())


def advance(plan, small, heights, pop, cuts):
    planes, row_tiles, lane_tiles = pop.shape[:3]
    group = math.gcd(planes, 2)
    blocks = plan.starts[-1]
    half_sums = jax.ShapeDtypeStruct((blocks, ROW, LANE), F32)
    return pl.pallas_call(
        functools.partial(advance_kernel, plan, cuts, group),
        out_shape=[pltpu.HBM(pop.shape, F32), half_sums, half_sums, jax.ShapeDtypeStruct((1,), jnp.int32)]
        + [pltpu.HBM((lane_tiles, end - begin, LANE), F32) for _, begin, end in cuts],
        in_specs=[SMEM_SPEC] * 6 + [VMEM_SPEC, HBM_SPEC],
        out_specs=[HBM_SPEC, VMEM_SPEC, VMEM_SPEC, SMEM_SPEC] + [HBM_SPEC] * len(cuts),
        scratch_shapes=[
            pltpu.VMEM((planes, lane_tiles + 2, PAD + row_tiles * ROW + ROW, LANE), F32),
            pltpu.VMEM((planes, row_tiles, lane_tiles, ROW, LANE), F32),
            pltpu.VMEM((planes, lane_tiles, ROW, LANE), F32),
            pltpu.VMEM((2, 4, ROW, LANE), F32),
            pltpu.VMEM((lane_tiles, planes * LOW_ROWS + 16, LANE), F32),
            pltpu.VMEM((lane_tiles, planes * HIGH_ROWS + 16, LANE), F32),
            pltpu.VMEM((lane_tiles, ROW, LANE), jnp.int32),
            pltpu.SemaphoreType.DMA((planes // group, row_tiles)),
            pltpu.SemaphoreType.DMA((planes,)),
            pltpu.SemaphoreType.DMA((len(cuts),)),
        ],
        compiler_params=params(36),
        name="advance",
    )(*in_hbm(*small, heights, pop))


def fold_kernel(mine_ref, received_ref, *out_refs):
    begin = 0
    for ref in out_refs:
        n = ref.shape[0]
        ref[...] = mine_ref[begin : begin + n] + received_ref[begin : begin + n]
        begin += n


def fold(mine, received, sizes):
    return pl.pallas_call(
        fold_kernel,
        out_shape=[jax.ShapeDtypeStruct((n, ROW, LANE), F32) for n in sizes],
        in_specs=[VMEM_SPEC] * 2,
        out_specs=[VMEM_SPEC] * len(sizes),
        compiler_params=params(8),
        name="fold",
    )(mine, received)


def join_low_kernel(own_ref, low_ref, *refs):
    out_ref = refs[-1]
    tile = own_ref.shape[0] // 2
    half = tile // 4
    out_ref[2 * tile :] = jnp.zeros((out_ref.shape[0] - 2 * tile, ROW, LANE), F32)
    out_ref[:tile] = own_ref[:tile] + low_ref[:tile]
    top = lax.broadcasted_iota(jnp.int32, (ROW, LANE), 0) == 0
    for m in range(4):
        for n in range(half):
            row = jnp.broadcast_to(low_ref[tile + m, n : n + 1, :], (ROW, LANE))
            index = tile + m * half + n
            out_ref[index] = own_ref[index] + jnp.where(top, row, 0.0)


def add_kernel(a_ref, b_ref, *refs):
    refs[-1][...] = a_ref[...] + b_ref[...]


def join_high_kernel(own_ref, high_ref, *refs):
    out_ref = refs[-1]
    tile = high_ref.shape[0]
    out_ref[2 * tile :] = jnp.zeros((out_ref.shape[0] - 2 * tile, ROW, LANE), F32)
    out_ref[:tile] = own_ref[:tile]
    out_ref[tile : 2 * tile] = own_ref[tile:] + high_ref[...]


def small_call(kernel, name, a, b, after=(), extra=0):
    operands = a, b, *after
    shape = (a.shape[0] + extra, *a.shape[1:])
    return pl.pallas_call(
        kernel,
        out_shape=jax.ShapeDtypeStruct(shape, F32),
        in_specs=[VMEM_SPEC] * 2 + [ANY_SPEC] * len(after),
        out_specs=VMEM_SPEC,
        compiler_params=params(8),
        name=name,
    )(*operands)


def profile(density, flux_x, flux_y, energy, factor):
    inverse = 1.0 / density
    mean_x = flux_x * inverse
    mean_y = flux_y * inverse
    temperature = 0.5 * (energy * inverse - mean_x * mean_x - mean_y * mean_y)
    rate = 1.0 - jnp.exp(-factor * density / (SPEED_TALLY * jnp.sqrt(temperature)))
    height = rate * (density / (2.0 * math.pi * temperature))
    return mean_x, mean_y, -0.5 / temperature, height, 1.0 - rate


def relax_cells(get, put, values, factor, weights):
    mean_x, mean_y, scale, height, keep = profile(*values, factor)
    for v, (along_x, along_y) in enumerate(weights):
        gap_x = along_x - mean_x
        gap_y = along_y - mean_y
        state = height * jnp.exp((gap_x * gap_x + gap_y * gap_y) * scale)
        put(v, keep * get(v) + state)


def relax_tile(buf, sums, base, core, factor, weights, k, h):
    mine_ref, other_ref = sums
    half = buf.shape[2] // 2
    for n in range(half):
        t = h * half + n
        values = []
        for m in range(4):
            index = base + m * half + n
            values.append(jnp.where(core == h, mine_ref[index], other_ref[index]))

        def put(v, value):
            buf[v, k, t] = value

        relax_cells(lambda v: buf[v, k, t], put, values, factor, weights)


def relax_kernel(sizes, meta_ref, sx_ref, sy_ref, fx_ref, fy_ref, factor_ref, planes_ref, *refs):
    sums_refs = refs[:-4]
    out_ref, buf, sem_in, sem_out = refs[-4:]
    planes, row_tiles, lane_tiles = planes_ref.shape[:3]
    half = lane_tiles // 2

    def copy(j, h, out):
        lanes = pl.ds(h * half, half)
        here = buf.at[:, j, lanes]
        if out:
            return pltpu.make_async_copy(here, out_ref.at[:, j, lanes], sem_out.at[2 * j + h])
        return pltpu.make_async_copy(planes_ref.at[:, j, lanes], here, sem_in.at[2 * j + h])

    def tile(k):
        return jnp.where(k < row_tiles - 2, k + 2, k + 2 - row_tiles)

    def start(k, _):
        for h in range(2):
            copy(tile(k), h, False).start()
        return 0

    lax.fori_loop(0, row_tiles, start, 0)
    weights = [velocity(sx_ref, sy_ref, fx_ref, fy_ref, v) for v in range(planes)]
    begin = 0
    for pair, size in enumerate(sizes):
        sums = sums_refs[2 * pair : 2 * pair + 2]

        def step(k, _, begin=begin, sums=sums):
            j = tile(k)
            for h in range(2):
                copy(j, h, False).wait()
                base = (k - begin) * 4 * half
                relax_tile(buf, sums, base, meta_ref[3], factor_ref[0], weights, j, h)
                copy(j, h, True).start()
            return 0

        lax.fori_loop(begin, begin + size, step, 0)
        begin += size

    def finish(j, _):
        for h in range(2):
            copy(j, h, True).wait()
        return 0

    lax.fori_loop(0, row_tiles, finish, 0)


def relax_all(sizes, meta, small, factor, sums, moved):
    planes, row_tiles, lane_tiles = moved.shape[:3]
    operands = [*in_hbm(meta, *small[:4]), factor, *in_hbm(moved), *sums]
    return pl.pallas_call(
        functools.partial(relax_kernel, sizes),
        out_shape=pltpu.HBM(moved.shape, F32),
        in_specs=[SMEM_SPEC] * 6 + [HBM_SPEC] + [VMEM_SPEC] * len(sums),
        out_specs=HBM_SPEC,
        scratch_shapes=[
            pltpu.VMEM((planes, row_tiles, lane_tiles, ROW, LANE), F32),
            pltpu.SemaphoreType.DMA((2 * row_tiles,)),
            pltpu.SemaphoreType.DMA((2 * row_tiles,)),
        ],
        compiler_params=params(24),
        name="relax_all",
    )(*operands)


def finish_kernel(cuts, meta_ref, sx_ref, sy_ref, fx_ref, fy_ref, inflow_ref, factor_ref, heights_ref,
                  m_low, o_low, m_high, o_high, before_ref, *refs):
    pack_refs = refs[: len(cuts)]
    out_ref, frames, buf, keeps, low_buf, high_buf, bars, sem_in, sem_planes, sem_out = refs[len(cuts) :]
    planes, row_tiles, lane_tiles = before_ref.shape[:3]
    half = lane_tiles // 2
    row0, first, last, core = (meta_ref[i] for i in range(4))
    needs = [low_need(sy_ref[0]), high_need(sy_ref[0])]
    for v in range(1, planes):
        needs = [needs[0] + low_need(sy_ref[v]), needs[1] + high_need(sy_ref[v])]

    def pack_copy(n):
        pack, begin, end = cuts[n]
        target = (low_buf, high_buf)[pack].at[:, 16 + begin : 16 + end, :]
        return pltpu.make_async_copy(pack_refs[n], target, sem_in.at[n])

    def cases(v):
        shift = sy_ref[v]
        from_low = (shift >= 0) & (first == 0)
        return from_low, (shift < 0) & (last == 0), from_low & (shift == CFL)

    tile_of = 0, row_tiles - 1, 1
    slot_of = 0, 0, 1

    def copy(v, case, out):
        here = buf.at[v, slot_of[case]]
        if out:
            return pltpu.make_async_copy(here, out_ref.at[v, tile_of[case]], sem_out.at[v, slot_of[case]])
        there = before_ref.at[v, tile_of[case]]
        return pltpu.make_async_copy(there, here, sem_planes.at[v, slot_of[case]])

    for n in range(len(cuts)):
        pl.when(needs[cuts[n][0]] > cuts[n][1])(lambda n=n: pack_copy(n).start())

    def start(v, _):
        for case, applies in enumerate(cases(v)):
            pl.when(applies)(lambda case=case: copy(v, case, False).start())
        return 0

    lax.fori_loop(0, planes, start, 0)
    prepare_heights(heights_ref, bars)
    for t in range(lane_tiles + 2):
        for r in (24, 32):
            frames[0, t, r : r + ROW, :] = jnp.zeros((ROW, LANE), F32)
        for r in (16, 24):
            frames[1, t, r : r + ROW, :] = jnp.zeros((ROW, LANE), F32)
    edges = ((m_low, o_low), 0), ((m_high, o_high), 4 * half), ((m_low, o_low), 4 * half)
    for case, (sums, base) in enumerate(edges):
        for t in range(lane_tiles):
            h, n = divmod(t, half)
            values = []
            for m in range(4):
                index = base + m * half + n
                values.append(jnp.where(core == h, sums[0][index], sums[1][index]))
            keeps[case, t] = profile(*values, factor_ref[0])[4]
    for n in range(len(cuts)):
        pl.when(needs[cuts[n][0]] > cuts[n][1])(lambda n=n: pack_copy(n).wait())

    def add_masked(v, case):
        first_row = row0 + ROW * tile_of[case]

        def put(t, value):
            part = jnp.where(first_row < bars[t], 0.0, value)
            buf[v, slot_of[case], t] = buf[v, slot_of[case], t] + keeps[case, t] * part

        return put

    def one(v, offsets):
        low, high = offsets
        value = inflow_ref[v]
        shift = sy_ref[v]
        scalars = sx_ref[v], shift, fx_ref[v], fy_ref[v]
        borders = (0, lane_tiles + 1)
        from_low, from_high, reaches_second = cases(v)

        @pl.when(from_low)
        def _():
            fill_rows(frames, 0, borders, 8, 16, value)
            for t in range(lane_tiles):
                for r in range(0, 16, ROW):
                    piece = low_buf[t, pl.ds(low + shift + 1 + r, ROW), :]
                    frames[0, t + 1, 8 + r : 8 + r + ROW, :] = piece
            copy(v, 0, False).wait()
            advect(frames, 0, scalars, [(24, add_masked(v, 0))])
            copy(v, 0, True).start()

        @pl.when(reaches_second)
        def _():
            copy(v, 2, False).wait()
            advect(frames, 0, scalars, [(32, add_masked(v, 2))])
            copy(v, 2, True).start()

        @pl.when(from_high)
        def _():
            fill_rows(frames, 1, borders, 32, 8, value)
            for t in range(lane_tiles):
                frames[1, t + 1, 32:40, :] = high_buf[t, pl.ds(16 + high, ROW), :]
            copy(v, 1, False).wait()
            advect(frames, 1, scalars, [(24, add_masked(v, 1))])
            copy(v, 1, True).start()

        return low + low_need(shift), high + high_need(shift)

    lax.fori_loop(0, planes, one, (jnp.int32(0), jnp.int32(0)))

    def end(v, _):
        for case, applies in enumerate(cases(v)):
            pl.when(applies)(lambda case=case: copy(v, case, True).wait())
        return 0

    lax.fori_loop(0, planes, end, 0)


def finish_edges(meta, small, factor, heights, sums, packs, cuts, out):
    planes, _, lane_tiles = out.shape[:3]
    fixed = [*in_hbm(meta, *small[:5]), factor, *in_hbm(heights)]
    operands = [*fixed, *sums, *in_hbm(out), *packs]
    return pl.pallas_call(
        functools.partial(finish_kernel, cuts),
        out_shape=pltpu.HBM(out.shape, F32),
        in_specs=[SMEM_SPEC] * 7 + [VMEM_SPEC] * 5 + [HBM_SPEC] + [ANY_SPEC] * len(cuts),
        out_specs=HBM_SPEC,
        scratch_shapes=[
            pltpu.VMEM((2, lane_tiles + 2, 48, LANE), F32),
            pltpu.VMEM((planes, 2, lane_tiles, ROW, LANE), F32),
            pltpu.VMEM((3, lane_tiles, ROW, LANE), F32),
            pltpu.VMEM((lane_tiles, planes * LOW_ROWS + 32, LANE), F32),
            pltpu.VMEM((lane_tiles, planes * HIGH_ROWS + 32, LANE), F32),
            pltpu.VMEM((lane_tiles, ROW, LANE), jnp.int32),
            pltpu.SemaphoreType.DMA((len(cuts),)),
            pltpu.SemaphoreType.DMA((planes, 2)),
            pltpu.SemaphoreType.DMA((planes, 2)),
        ],
        input_output_aliases={len(fixed) + len(sums): 0},
        compiler_params=params(24),
        name="finish_edges",
    )(*operands)


def per_device(populations, shift_x, shift_y, frac_x, frac_y, inflow, wall_state, heights,
               impact_frequency_factor):
    planes, row_count, col_count = populations.shape
    space_count, vel_count = lax.axis_size("space"), lax.axis_size("vel")
    row_tiles, lane_tiles = row_count // ROW, col_count // LANE
    space, vel = lax.axis_index("space"), lax.axis_index("vel")
    forward = [(i, i + 1) for i in range(space_count - 1)]
    backward = [(target, source) for source, target in forward]
    partner = [(i, i ^ 1) for i in range(vel_count)]
    across = [(i, i ^ 2) for i in range(vel_count)]

    meta = jnp.stack([space * row_count, space == 0, space == space_count - 1, vel % 2]).astype(jnp.int32)
    small = (shift_x, shift_y, frac_x, frac_y, inflow, wall_state)
    factor = impact_frequency_factor.reshape(1)
    bars = heights.reshape(lane_tiles, LANE)
    pop = populations.reshape(planes, row_tiles, ROW, lane_tiles, LANE).transpose(0, 1, 3, 2, 4)
    low_sent, high_sent = min(LOW_SENT, planes * LOW_ROWS), min(HIGH_SENT, planes * HIGH_ROWS)
    cuts = [
        (0, 0, low_sent),
        (1, 0, high_sent),
        (0, low_sent, planes * LOW_ROWS),
        (1, high_sent, planes * HIGH_ROWS),
    ]
    plan = Plan(row_tiles, lane_tiles // 2)

    moved, mine, theirs, more_needed, *packs = advance(plan, small, bars, pop, cuts)
    received = lax.ppermute(theirs, "vel", partner)
    up, down, inside, edge_low, edge_high = fold(mine, received, plan.sizes)
    from_low = lax.ppermute(up, "space", forward)
    from_high = lax.ppermute(down, "space", backward)
    low_first = lax.ppermute(packs[0], "space", forward)
    high_first = lax.ppermute(packs[1], "space", backward)

    def total(sums, after=()):
        whole = small_call(add_kernel, "add", sums, lax.ppermute(sums, "vel", across), after)
        return whole, lax.ppermute(whole, "vel", partner)

    def send_more(low, high):
        return lax.ppermute(low, "space", forward), lax.ppermute(high, "space", backward)

    more = lax.cond(more_needed[0] > 0, send_more, lambda low, high: (low, high), packs[2], packs[3])
    sums_inside = total(inside)
    sums_low = total(small_call(join_low_kernel, "join_low", edge_low, from_low, (), 1))
    sums_high = total(small_call(join_high_kernel, "join_high", edge_high, from_high, (), 1))
    sizes = len(plan.inside), 2, 2
    out = relax_all(sizes, meta, small, factor, sums_inside + sums_high + sums_low, moved)
    halo = low_first, high_first, *more
    out = finish_edges(meta, small, factor, bars, sums_low + sums_high, halo, cuts, out)
    return out.transpose(0, 1, 3, 2, 4).reshape(planes, row_count, col_count)


def solution(mesh):
    return jax.shard_map(
        per_device,
        mesh=mesh,
        in_specs=(
            P("vel", "space", None),
            P("vel"),
            P("vel"),
            P("vel"),
            P("vel"),
            P("vel"),
            P("vel"),
            P(),
            P(),
        ),
        out_specs=P("vel", "space", None),
        check_vma=False,
    )
```

```python
import functools
import math

import jax
import jax.numpy as jnp
from jax import lax
from jax.experimental import pallas as pl
from jax.experimental.pallas import tpu as pltpu
from jax.sharding import PartitionSpec as P

SPEED_TALLY = 64
CFL = 8
LOW_ROWS = CFL + 1
HIGH_ROWS = CFL
ROW = 8
LANE = 128
PAD = 16
F32 = jnp.float32
LOW_SENT = 80
HIGH_SENT = 64

SMEM_SPEC = pl.BlockSpec(memory_space=pltpu.SMEM)
ANY_SPEC = pl.BlockSpec(memory_space=pl.ANY)
HBM_SPEC = pl.BlockSpec(memory_space=pltpu.HBM)
VMEM_SPEC = pl.BlockSpec(memory_space=pltpu.VMEM)


def params(mebibytes):
    return pltpu.CompilerParams(vmem_limit_bytes=mebibytes * 1024 * 1024)


def in_hbm(*arrays):
    return [pltpu.with_memory_space_constraint(x, pltpu.HBM) for x in arrays]


def place(rows):
    space = lax.axis_index("space")
    return space * rows, space == 0, space == lax.axis_size("space") - 1, lax.axis_index("vel") % 2


def low_need(shift):
    return jnp.where(shift >= 0, shift + 1, 0)


def high_need(shift):
    return jnp.where(shift < 0, -shift, 0)


def fill_rows(padded, v, columns, start, count, value):
    block = jnp.full((ROW, LANE), value, F32)
    for t in columns:
        for r in range(start, start + count, ROW):
            padded[v, t, r : r + ROW, :] = block


def prepare_heights(heights_ref, bars):
    lane_tiles = heights_ref.shape[0]
    sublane = lax.broadcasted_iota(jnp.int32, (ROW, LANE), 0)
    for t in range(lane_tiles):
        bars[t] = jnp.broadcast_to(heights_ref[t : t + 1, :], (ROW, LANE)) - sublane


def advect(padded, v, scalars, tiles):
    sx, sy, fx, fy = scalars
    lane_tiles = padded.shape[1] - 2
    lane = lax.broadcasted_iota(jnp.int32, (ROW, LANE), 1)
    near_roll = jnp.where(sx < 0, sx + LANE, sx)
    far_roll = jnp.where(sx + 1 < 0, sx + 1 + LANE, sx + 1)

    def moved(start, t):
        nearer = padded[v, t + 1, pl.ds(start, ROW), :]
        further = padded[v, t + 1, pl.ds(start - 1, ROW), :]
        line = (1.0 - fy) * nearer + fy * further
        if t < 0 or t == lane_tiles:
            return line, line
        return pltpu.roll(line, near_roll, 1), pltpu.roll(line, far_roll, 1)

    def blend(put, t, near, far):
        put(t, (1.0 - fx) * near + fx * far)

    @pl.when(sx >= 0)
    def _():
        own_near, own_far = lane >= sx, lane >= sx + 1
        for begin, put in tiles:
            before = moved(begin - sy, -1)
            for t in range(lane_tiles):
                here = moved(begin - sy, t)
                near = jnp.where(own_near, here[0], before[0])
                blend(put, t, near, jnp.where(own_far, here[1], before[1]))
                before = here

    @pl.when(sx < 0)
    def _():
        own_near, own_far = lane < sx + LANE, lane < sx + 1 + LANE
        for begin, put in tiles:
            here = moved(begin - sy, 0)
            for t in range(lane_tiles):
                after = moved(begin - sy, t + 1)
                near = jnp.where(own_near, here[0], after[0])
                blend(put, t, near, jnp.where(own_far, here[1], after[1]))
                here = after


def store_masked(target, bars, first_row, solid_value):
    def put(t, value):
        target[t] = jnp.where(first_row < bars[t], solid_value, value)

    return put


def velocity(sx_ref, sy_ref, fx_ref, fy_ref, v):
    return sx_ref[v].astype(F32) + fx_ref[v], sy_ref[v].astype(F32) + fy_ref[v]


def sum_moments(planes_ref, k, weights, lane_tile_range):
    sums = [[None] * 4 for _ in lane_tile_range]
    for v, (along_x, along_y) in enumerate(weights):
        square = along_x * along_x + along_y * along_y
        for n, t in enumerate(lane_tile_range):
            f = planes_ref[v, k, t]
            terms = (f, f * along_x, f * along_y, f * square)
            sums[n] = [b if a is None else a + b for a, b in zip(sums[n], terms)]
    return sums


class Plan:
    def __init__(self, row_tiles, half):
        self.tile = 4 * half
        self.inside = list(range(2, row_tiles - 2))
        self.sizes = [self.tile + 4, self.tile, len(self.inside) * self.tile, 2 * self.tile, 2 * self.tile]
        self.starts = [sum(self.sizes[:n]) for n in range(len(self.sizes) + 1)]
        self.row_tiles = row_tiles

    def start(self, j):
        low = self.starts[3] + self.tile * j
        high = self.starts[4] + self.tile * (j - self.row_tiles + 2)
        inside = self.starts[2] + self.tile * (j - 2)
        return jnp.where(j < 2, low, jnp.where(j >= self.row_tiles - 2, high, inside))


def advance_kernel(plan, cuts, group, sx_ref, sy_ref, fx_ref, fy_ref, inflow_ref, wall_ref,
                   heights_ref, pop_ref, *refs):
    planes_ref, mine_ref, theirs_ref, more_ref = refs[:4]
    packs = refs[4 : 4 + len(cuts)]
    (padded, planes_buf, outer, last_row, low_pack, high_pack, bars, sem_in, sem_planes, sem_out) = refs[
        4 + len(cuts) :
    ]
    planes, row_tiles, lane_tiles = pop_ref.shape[:3]
    half = lane_tiles // 2
    rows = row_tiles * ROW
    row0, first, last, core = place(rows)

    def loads(g):
        members = pl.ds(g * group, group)
        return [
            pltpu.make_async_copy(
                pop_ref.at[members, i],
                padded.at[members, 1 : 1 + lane_tiles, PAD + ROW * i : PAD + ROW * (i + 1), :],
                sem_in.at[g, i],
            )
            for i in range(row_tiles)
        ]

    def start(g, _):
        for load in loads(g):
            load.start()
        return 0

    lax.fori_loop(0, planes // group, start, 0)
    prepare_heights(heights_ref, bars)
    last_row[...] = jnp.zeros_like(last_row)

    def put_sums(h, first_block, sums):
        for is_mine, ref in ((True, mine_ref), (False, theirs_ref)):

            @pl.when((core == h) == is_mine)
            def _():
                for n, value in enumerate(sums):
                    ref[first_block + n] = value


    def out_copy(v):
        return pltpu.make_async_copy(planes_buf.at[v], planes_ref.at[v], sem_planes.at[v])

    def one(v, offsets):
        low, high = offsets
        value = inflow_ref[v]
        shift = sy_ref[v]
        up = shift >= 0
        columns = range(lane_tiles + 2)
        fill_rows(padded, v, (0, lane_tiles + 1), PAD, rows, value)
        fill_rows(padded, v, columns, 0, PAD, jnp.where(first, value, 0.0))
        fill_rows(padded, v, columns, PAD + rows, ROW, jnp.where(last, value, 0.0))

        @pl.when(v % group == 0)
        def _():
            for load in loads(v // group):
                load.wait()

        scalars = sx_ref[v], shift, fx_ref[v], fy_ref[v]
        work = [
            (PAD + ROW * j, store_masked(planes_buf.at[v, j], bars, row0 + ROW * j, wall_ref[v]))
            for j in range(row_tiles)
        ]
        beyond = jnp.where(up, rows, -ROW)
        work.append((PAD + beyond, store_masked(outer.at[v], bars, row0 + beyond, 0.0)))
        advect(padded, v, scalars, work)
        out_copy(v).start()

        @pl.when(shift == CFL)
        def _():
            along_x, along_y = velocity(sx_ref, sy_ref, fx_ref, fy_ref, v)
            factors = 1.0, along_x, along_y, along_x * along_x + along_y * along_y

            def put(t, value):
                row = jnp.where(row0 + rows + ROW < bars[t], 0.0, value)
                h, r = divmod(t, half)
                for m in range(4):
                    total = last_row[h, m, r : r + 1, :] + (row * factors[m])[0:1, :]
                    last_row[h, m, r : r + 1, :] = total

            advect(padded, v, scalars, [(PAD + rows + ROW, put)])

        @pl.when(up)
        def _():
            for t in range(lane_tiles):
                source = pl.ds(PAD + rows - 1 - shift, 8)
                low_pack[t, pl.ds(low, 8), :] = padded[v, t + 1, source, :]

        @pl.when(shift == CFL)
        def _():
            for t in range(lane_tiles):
                low_pack[t, pl.ds(low + 8, 1), :] = padded[v, t + 1, PAD + rows - 1 : PAD + rows, :]

        @pl.when(jnp.logical_not(up))
        def _():
            for t in range(lane_tiles):
                high_pack[t, pl.ds(high, 8), :] = padded[v, t + 1, PAD : PAD + 8, :]

        return low + low_need(shift), high + high_need(shift)

    needs = lax.fori_loop(0, planes, one, (jnp.int32(0), jnp.int32(0)))
    sent = [end for _, begin, end in cuts if begin == 0]
    overflows = (needs[0] > sent[0]) | (needs[1] > sent[1])
    more_ref[0] = jnp.where(overflows, 1, 0)

    def pack_copy(n):
        pack, begin, end = cuts[n]
        source = (low_pack, high_pack)[pack].at[:, begin:end, :]
        return pltpu.make_async_copy(source, packs[n], sem_out.at[n])

    def each_pack(act):
        for n, (_, begin, _) in enumerate(cuts):
            if begin == 0:
                act(pack_copy(n))
            else:
                pl.when(overflows)(lambda n=n: act(pack_copy(n)))

    each_pack(lambda copy: copy.start())
    for h in range(2):
        put_sums(h, plan.tile, [last_row[h, m] for m in range(4)])
        for rising in (True, False):
            for part in range(2):
                tiles = range(h * half + part * half // 2, h * half + (part + 1) * half // 2)
                sums = [[None] * 4 for _ in tiles]
                for v in range(planes):
                    along_x, along_y = velocity(sx_ref, sy_ref, fx_ref, fy_ref, v)
                    goes = jnp.where((sy_ref[v] >= 0) == rising, 1.0, 0.0)
                    square = (along_x * along_x + along_y * along_y) * goes
                    factors = goes, along_x * goes, along_y * goes, square
                    for n, t in enumerate(tiles):
                        f = outer[v, t]
                        terms = [f * w for w in factors]
                        sums[n] = [b if a is None else a + b for a, b in zip(sums[n], terms)]
                begin = plan.starts[0 if rising else 1] + part * half // 2
                for m in range(4):
                    put_sums(h, begin + m * half, [sums[n][m] for n in range(len(tiles))])
    weights = [velocity(sx_ref, sy_ref, fx_ref, fy_ref, v) for v in range(planes)]

    def step(j, _):
        begin = plan.start(j)
        for h in range(2):
            sums = sum_moments(planes_buf, j, weights, range(h * half, (h + 1) * half))
            put_sums(h, begin, [sums[t][m] for m in range(4) for t in range(half)])
        return 0

    lax.fori_loop(0, row_tiles, step, 0)

    def finish(v, _):
        out_copy(v).wait()
        return 0

    lax.fori_loop(0, planes, finish, 0)
    each_pack(lambda copy: copy.wait())


def advance(plan, small, heights, pop, cuts):
    planes, row_tiles, lane_tiles = pop.shape[:3]
    group = math.gcd(planes, 2)
    blocks = plan.starts[-1]
    half_sums = jax.ShapeDtypeStruct((blocks, ROW, LANE), F32)
    return pl.pallas_call(
        functools.partial(advance_kernel, plan, cuts, group),
        out_shape=[pltpu.HBM(pop.shape, F32), half_sums, half_sums, jax.ShapeDtypeStruct((1,), jnp.int32)]
        + [pltpu.HBM((lane_tiles, end - begin, LANE), F32) for _, begin, end in cuts],
        in_specs=[SMEM_SPEC] * 6 + [VMEM_SPEC, HBM_SPEC],
        out_specs=[HBM_SPEC, VMEM_SPEC, VMEM_SPEC, SMEM_SPEC] + [HBM_SPEC] * len(cuts),
        scratch_shapes=[
            pltpu.VMEM((planes, lane_tiles + 2, PAD + row_tiles * ROW + ROW, LANE), F32),
            pltpu.VMEM((planes, row_tiles, lane_tiles, ROW, LANE), F32),
            pltpu.VMEM((planes, lane_tiles, ROW, LANE), F32),
            pltpu.VMEM((2, 4, ROW, LANE), F32),
            pltpu.VMEM((lane_tiles, planes * LOW_ROWS + 16, LANE), F32),
            pltpu.VMEM((lane_tiles, planes * HIGH_ROWS + 16, LANE), F32),
            pltpu.VMEM((lane_tiles, ROW, LANE), jnp.int32),
            pltpu.SemaphoreType.DMA((planes // group, row_tiles)),
            pltpu.SemaphoreType.DMA((planes,)),
            pltpu.SemaphoreType.DMA((len(cuts),)),
        ],
        compiler_params=params(36),
        name="advance",
    )(*in_hbm(*small, heights, pop))


def fold_kernel(mine_ref, received_ref, *out_refs):
    begin = 0
    for ref in out_refs:
        n = ref.shape[0]
        ref[...] = mine_ref[begin : begin + n] + received_ref[begin : begin + n]
        begin += n


def fold(mine, received, sizes):
    return pl.pallas_call(
        fold_kernel,
        out_shape=[jax.ShapeDtypeStruct((n, ROW, LANE), F32) for n in sizes],
        in_specs=[VMEM_SPEC] * 2,
        out_specs=[VMEM_SPEC] * len(sizes),
        compiler_params=params(8),
        name="fold",
    )(mine, received)


def join_low_kernel(own_ref, low_ref, *refs):
    out_ref = refs[-1]
    tile = own_ref.shape[0] // 2
    half = tile // 4
    out_ref[2 * tile :] = jnp.zeros((out_ref.shape[0] - 2 * tile, ROW, LANE), F32)
    out_ref[:tile] = own_ref[:tile] + low_ref[:tile]
    top = lax.broadcasted_iota(jnp.int32, (ROW, LANE), 0) == 0
    for m in range(4):
        for n in range(half):
            row = jnp.broadcast_to(low_ref[tile + m, n : n + 1, :], (ROW, LANE))
            index = tile + m * half + n
            out_ref[index] = own_ref[index] + jnp.where(top, row, 0.0)


def add_kernel(a_ref, b_ref, *refs):
    refs[-1][...] = a_ref[...] + b_ref[...]


def join_high_kernel(own_ref, high_ref, *refs):
    out_ref = refs[-1]
    tile = high_ref.shape[0]
    out_ref[2 * tile :] = jnp.zeros((out_ref.shape[0] - 2 * tile, ROW, LANE), F32)
    out_ref[:tile] = own_ref[:tile]
    out_ref[tile : 2 * tile] = own_ref[tile:] + high_ref[...]


def small_call(kernel, name, a, b, after=(), extra=0):
    operands = a, b, *after
    shape = (a.shape[0] + extra, *a.shape[1:])
    return pl.pallas_call(
        kernel,
        out_shape=jax.ShapeDtypeStruct(shape, F32),
        in_specs=[VMEM_SPEC] * 2 + [ANY_SPEC] * len(after),
        out_specs=VMEM_SPEC,
        compiler_params=params(8),
        name=name,
    )(*operands)


def profile(density, flux_x, flux_y, energy, factor):
    inverse = 1.0 / density
    mean_x = flux_x * inverse
    mean_y = flux_y * inverse
    temperature = 0.5 * (energy * inverse - mean_x * mean_x - mean_y * mean_y)
    rate = 1.0 - jnp.exp(-factor * density / (SPEED_TALLY * jnp.sqrt(temperature)))
    height = rate * (density / (2.0 * math.pi * temperature))
    return mean_x, mean_y, -0.5 / temperature, height, 1.0 - rate


def relax_cells(get, put, values, factor, weights):
    mean_x, mean_y, scale, height, keep = profile(*values, factor)
    for v, (along_x, along_y) in enumerate(weights):
        gap_x = along_x - mean_x
        gap_y = along_y - mean_y
        state = height * jnp.exp((gap_x * gap_x + gap_y * gap_y) * scale)
        put(v, keep * get(v) + state)


def relax_tile(buf, sums, base, core, factor, weights, k, h):
    mine_ref, other_ref = sums
    half = buf.shape[2] // 2
    for n in range(half):
        t = h * half + n
        values = []
        for m in range(4):
            index = base + m * half + n
            values.append(jnp.where(core == h, mine_ref[index], other_ref[index]))

        def put(v, value):
            buf[v, k, t] = value

        relax_cells(lambda v: buf[v, k, t], put, values, factor, weights)


def relax_kernel(sizes, meta_ref, sx_ref, sy_ref, fx_ref, fy_ref, factor_ref, planes_ref, *refs):
    sums_refs = refs[:-4]
    out_ref, buf, sem_in, sem_out = refs[-4:]
    planes, row_tiles, lane_tiles = planes_ref.shape[:3]
    half = lane_tiles // 2

    def copy(j, h, out):
        lanes = pl.ds(h * half, half)
        here = buf.at[:, j, lanes]
        if out:
            return pltpu.make_async_copy(here, out_ref.at[:, j, lanes], sem_out.at[2 * j + h])
        return pltpu.make_async_copy(planes_ref.at[:, j, lanes], here, sem_in.at[2 * j + h])

    def tile(k):
        return jnp.where(k < row_tiles - 2, k + 2, k + 2 - row_tiles)

    def start(k, _):
        for h in range(2):
            copy(tile(k), h, False).start()
        return 0

    lax.fori_loop(0, row_tiles, start, 0)
    weights = [velocity(sx_ref, sy_ref, fx_ref, fy_ref, v) for v in range(planes)]
    begin = 0
    for pair, size in enumerate(sizes):
        sums = sums_refs[2 * pair : 2 * pair + 2]

        def step(k, _, begin=begin, sums=sums):
            j = tile(k)
            for h in range(2):
                copy(j, h, False).wait()
                base = (k - begin) * 4 * half
                relax_tile(buf, sums, base, meta_ref[3], factor_ref[0], weights, j, h)
                copy(j, h, True).start()
            return 0

        lax.fori_loop(begin, begin + size, step, 0)
        begin += size

    def finish(j, _):
        for h in range(2):
            copy(j, h, True).wait()
        return 0

    lax.fori_loop(0, row_tiles, finish, 0)


def relax_all(sizes, meta, small, factor, sums, moved):
    planes, row_tiles, lane_tiles = moved.shape[:3]
    operands = [*in_hbm(meta, *small[:4]), factor, *in_hbm(moved), *sums]
    return pl.pallas_call(
        functools.partial(relax_kernel, sizes),
        out_shape=pltpu.HBM(moved.shape, F32),
        in_specs=[SMEM_SPEC] * 6 + [HBM_SPEC] + [VMEM_SPEC] * len(sums),
        out_specs=HBM_SPEC,
        scratch_shapes=[
            pltpu.VMEM((planes, row_tiles, lane_tiles, ROW, LANE), F32),
            pltpu.SemaphoreType.DMA((2 * row_tiles,)),
            pltpu.SemaphoreType.DMA((2 * row_tiles,)),
        ],
        compiler_params=params(24),
        name="relax_all",
    )(*operands)


def finish_kernel(cuts, meta_ref, sx_ref, sy_ref, fx_ref, fy_ref, inflow_ref, factor_ref, heights_ref,
                  m_low, o_low, m_high, o_high, before_ref, *refs):
    pack_refs = refs[: len(cuts)]
    out_ref, frames, buf, keeps, low_buf, high_buf, bars, sem_in, sem_planes, sem_out = refs[len(cuts) :]
    planes, row_tiles, lane_tiles = before_ref.shape[:3]
    half = lane_tiles // 2
    row0, first, last, core = (meta_ref[i] for i in range(4))
    needs = [low_need(sy_ref[0]), high_need(sy_ref[0])]
    for v in range(1, planes):
        needs = [needs[0] + low_need(sy_ref[v]), needs[1] + high_need(sy_ref[v])]

    def pack_copy(n):
        pack, begin, end = cuts[n]
        target = (low_buf, high_buf)[pack].at[:, 16 + begin : 16 + end, :]
        return pltpu.make_async_copy(pack_refs[n], target, sem_in.at[n])

    def cases(v):
        shift = sy_ref[v]
        from_low = (shift >= 0) & (first == 0)
        return from_low, (shift < 0) & (last == 0), from_low & (shift == CFL)

    tile_of = 0, row_tiles - 1, 1
    slot_of = 0, 0, 1

    def copy(v, case, out):
        here = buf.at[v, slot_of[case]]
        if out:
            return pltpu.make_async_copy(here, out_ref.at[v, tile_of[case]], sem_out.at[v, slot_of[case]])
        there = before_ref.at[v, tile_of[case]]
        return pltpu.make_async_copy(there, here, sem_planes.at[v, slot_of[case]])

    for n in range(len(cuts)):
        pl.when(needs[cuts[n][0]] > cuts[n][1])(lambda n=n: pack_copy(n).start())

    def start(v, _):
        for case, applies in enumerate(cases(v)):
            pl.when(applies)(lambda case=case: copy(v, case, False).start())
        return 0

    lax.fori_loop(0, planes, start, 0)
    prepare_heights(heights_ref, bars)
    for t in range(lane_tiles + 2):
        for r in (24, 32):
            frames[0, t, r : r + ROW, :] = jnp.zeros((ROW, LANE), F32)
        for r in (16, 24):
            frames[1, t, r : r + ROW, :] = jnp.zeros((ROW, LANE), F32)
    edges = ((m_low, o_low), 0), ((m_high, o_high), 4 * half), ((m_low, o_low), 4 * half)
    for case, (sums, base) in enumerate(edges):
        for t in range(lane_tiles):
            h, n = divmod(t, half)
            values = []
            for m in range(4):
                index = base + m * half + n
                values.append(jnp.where(core == h, sums[0][index], sums[1][index]))
            keeps[case, t] = profile(*values, factor_ref[0])[4]
    for n in range(len(cuts)):
        pl.when(needs[cuts[n][0]] > cuts[n][1])(lambda n=n: pack_copy(n).wait())

    def add_masked(v, case):
        first_row = row0 + ROW * tile_of[case]

        def put(t, value):
            part = jnp.where(first_row < bars[t], 0.0, value)
            buf[v, slot_of[case], t] = buf[v, slot_of[case], t] + keeps[case, t] * part

        return put

    def one(v, offsets):
        low, high = offsets
        value = inflow_ref[v]
        shift = sy_ref[v]
        scalars = sx_ref[v], shift, fx_ref[v], fy_ref[v]
        borders = (0, lane_tiles + 1)
        from_low, from_high, reaches_second = cases(v)

        @pl.when(from_low)
        def _():
            fill_rows(frames, 0, borders, 8, 16, value)
            for t in range(lane_tiles):
                for r in range(0, 16, ROW):
                    piece = low_buf[t, pl.ds(low + shift + 1 + r, ROW), :]
                    frames[0, t + 1, 8 + r : 8 + r + ROW, :] = piece
            copy(v, 0, False).wait()
            advect(frames, 0, scalars, [(24, add_masked(v, 0))])
            copy(v, 0, True).start()

        @pl.when(reaches_second)
        def _():
            copy(v, 2, False).wait()
            advect(frames, 0, scalars, [(32, add_masked(v, 2))])
            copy(v, 2, True).start()

        @pl.when(from_high)
        def _():
            fill_rows(frames, 1, borders, 32, 8, value)
            for t in range(lane_tiles):
                frames[1, t + 1, 32:40, :] = high_buf[t, pl.ds(16 + high, ROW), :]
            copy(v, 1, False).wait()
            advect(frames, 1, scalars, [(24, add_masked(v, 1))])
            copy(v, 1, True).start()

        return low + low_need(shift), high + high_need(shift)

    lax.fori_loop(0, planes, one, (jnp.int32(0), jnp.int32(0)))

    def end(v, _):
        for case, applies in enumerate(cases(v)):
            pl.when(applies)(lambda case=case: copy(v, case, True).wait())
        return 0

    lax.fori_loop(0, planes, end, 0)


def finish_edges(meta, small, factor, heights, sums, packs, cuts, out):
    planes, _, lane_tiles = out.shape[:3]
    fixed = [*in_hbm(meta, *small[:5]), factor, *in_hbm(heights)]
    operands = [*fixed, *sums, *in_hbm(out), *packs]
    return pl.pallas_call(
        functools.partial(finish_kernel, cuts),
        out_shape=pltpu.HBM(out.shape, F32),
        in_specs=[SMEM_SPEC] * 7 + [VMEM_SPEC] * 5 + [HBM_SPEC] + [ANY_SPEC] * len(cuts),
        out_specs=HBM_SPEC,
        scratch_shapes=[
            pltpu.VMEM((2, lane_tiles + 2, 48, LANE), F32),
            pltpu.VMEM((planes, 2, lane_tiles, ROW, LANE), F32),
            pltpu.VMEM((3, lane_tiles, ROW, LANE), F32),
            pltpu.VMEM((lane_tiles, planes * LOW_ROWS + 32, LANE), F32),
            pltpu.VMEM((lane_tiles, planes * HIGH_ROWS + 32, LANE), F32),
            pltpu.VMEM((lane_tiles, ROW, LANE), jnp.int32),
            pltpu.SemaphoreType.DMA((len(cuts),)),
            pltpu.SemaphoreType.DMA((planes, 2)),
            pltpu.SemaphoreType.DMA((planes, 2)),
        ],
        input_output_aliases={len(fixed) + len(sums): 0},
        compiler_params=params(24),
        name="finish_edges",
    )(*operands)


def per_device(populations, shift_x, shift_y, frac_x, frac_y, inflow, wall_state, heights,
               impact_frequency_factor):
    planes, row_count, col_count = populations.shape
    space_count, vel_count = lax.axis_size("space"), lax.axis_size("vel")
    row_tiles, lane_tiles = row_count // ROW, col_count // LANE
    space, vel = lax.axis_index("space"), lax.axis_index("vel")
    forward = [(i, i + 1) for i in range(space_count - 1)]
    backward = [(target, source) for source, target in forward]
    partner = [(i, i ^ 1) for i in range(vel_count)]
    across = [(i, i ^ 2) for i in range(vel_count)]

    meta = jnp.stack([space * row_count, space == 0, space == space_count - 1, vel % 2]).astype(jnp.int32)
    small = (shift_x, shift_y, frac_x, frac_y, inflow, wall_state)
    factor = impact_frequency_factor.reshape(1)
    bars = heights.reshape(lane_tiles, LANE)
    pop = populations.reshape(planes, row_tiles, ROW, lane_tiles, LANE).transpose(0, 1, 3, 2, 4)
    low_sent, high_sent = min(LOW_SENT, planes * LOW_ROWS), min(HIGH_SENT, planes * HIGH_ROWS)
    cuts = [
        (0, 0, low_sent),
        (1, 0, high_sent),
        (0, low_sent, planes * LOW_ROWS),
        (1, high_sent, planes * HIGH_ROWS),
    ]
    plan = Plan(row_tiles, lane_tiles // 2)

    moved, mine, theirs, more_needed, *packs = advance(plan, small, bars, pop, cuts)
    received = lax.ppermute(theirs, "vel", partner)
    up, down, inside, edge_low, edge_high = fold(mine, received, plan.sizes)
    from_low = lax.ppermute(up, "space", forward)
    from_high = lax.ppermute(down, "space", backward)
    low_first = lax.ppermute(packs[0], "space", forward)
    high_first = lax.ppermute(packs[1], "space", backward)

    def total(sums, after=()):
        whole = small_call(add_kernel, "add", sums, lax.ppermute(sums, "vel", across), after)
        return whole, lax.ppermute(whole, "vel", partner)

    def send_more(low, high):
        return lax.ppermute(low, "space", forward), lax.ppermute(high, "space", backward)

    more = lax.cond(more_needed[0] > 0, send_more, lambda low, high: (low, high), packs[2], packs[3])
    sums_inside = total(inside)
    sums_low = total(small_call(join_low_kernel, "join_low", edge_low, from_low, (), 1))
    sums_high = total(small_call(join_high_kernel, "join_high", edge_high, from_high, (), 1))
    sizes = len(plan.inside), 2, 2
    out = relax_all(sizes, meta, small, factor, sums_inside + sums_high + sums_low, moved)
    halo = low_first, high_first, *more
    out = finish_edges(meta, small, factor, bars, sums_low + sums_high, halo, cuts, out)
    return out.transpose(0, 1, 3, 2, 4).reshape(planes, row_count, col_count)


def solution(mesh):
    return jax.shard_map(
        per_device,
        mesh=mesh,
        in_specs=(
            P("vel", "space", None),
            P("vel"),
            P("vel"),
            P("vel"),
            P("vel"),
            P("vel"),
            P("vel"),
            P(),
            P(),
        ),
        out_specs=P("vel", "space", None),
        check_vma=False,
    )
```

```python
import functools
import math

import jax
import jax.numpy as jnp
from jax import lax
from jax.experimental import pallas as pl
from jax.experimental.pallas import tpu as pltpu
from jax.sharding import PartitionSpec as P

SPEED_TALLY = 64
CFL = 8
LOW_ROWS = CFL + 1
HIGH_ROWS = CFL
ROW = 8
LANE = 128
PAD = 16
F32 = jnp.float32
LOW_SENT = 80
HIGH_SENT = 64

SMEM_SPEC = pl.BlockSpec(memory_space=pltpu.SMEM)
ANY_SPEC = pl.BlockSpec(memory_space=pl.ANY)
HBM_SPEC = pl.BlockSpec(memory_space=pltpu.HBM)
VMEM_SPEC = pl.BlockSpec(memory_space=pltpu.VMEM)


def params(mebibytes):
    return pltpu.CompilerParams(vmem_limit_bytes=mebibytes * 1024 * 1024)


def in_hbm(*arrays):
    return [pltpu.with_memory_space_constraint(x, pltpu.HBM) for x in arrays]


def place(rows):
    space = lax.axis_index("space")
    return space * rows, space == 0, space == lax.axis_size("space") - 1, lax.axis_index("vel") % 2


def low_need(shift):
    return jnp.where(shift >= 0, shift + 1, 0)


def high_need(shift):
    return jnp.where(shift < 0, -shift, 0)


def fill_rows(padded, v, columns, start, count, value):
    block = jnp.full((ROW, LANE), value, F32)
    for t in columns:
        for r in range(start, start + count, ROW):
            padded[v, t, r : r + ROW, :] = block


def prepare_heights(heights_ref, bars):
    lane_tiles = heights_ref.shape[0]
    sublane = lax.broadcasted_iota(jnp.int32, (ROW, LANE), 0)
    for t in range(lane_tiles):
        bars[t] = jnp.broadcast_to(heights_ref[t : t + 1, :], (ROW, LANE)) - sublane


def advect(padded, v, scalars, tiles):
    sx, sy, fx, fy = scalars
    lane_tiles = padded.shape[1] - 2
    lane = lax.broadcasted_iota(jnp.int32, (ROW, LANE), 1)
    near_roll = jnp.where(sx < 0, sx + LANE, sx)
    far_roll = jnp.where(sx + 1 < 0, sx + 1 + LANE, sx + 1)

    def moved(start, t):
        nearer = padded[v, t + 1, pl.ds(start, ROW), :]
        further = padded[v, t + 1, pl.ds(start - 1, ROW), :]
        line = (1.0 - fy) * nearer + fy * further
        if t < 0 or t == lane_tiles:
            return line, line
        return pltpu.roll(line, near_roll, 1), pltpu.roll(line, far_roll, 1)

    def blend(put, t, near, far):
        put(t, (1.0 - fx) * near + fx * far)

    @pl.when(sx >= 0)
    def _():
        own_near, own_far = lane >= sx, lane >= sx + 1
        for begin, put in tiles:
            before = moved(begin - sy, -1)
            for t in range(lane_tiles):
                here = moved(begin - sy, t)
                near = jnp.where(own_near, here[0], before[0])
                blend(put, t, near, jnp.where(own_far, here[1], before[1]))
                before = here

    @pl.when(sx < 0)
    def _():
        own_near, own_far = lane < sx + LANE, lane < sx + 1 + LANE
        for begin, put in tiles:
            here = moved(begin - sy, 0)
            for t in range(lane_tiles):
                after = moved(begin - sy, t + 1)
                near = jnp.where(own_near, here[0], after[0])
                blend(put, t, near, jnp.where(own_far, here[1], after[1]))
                here = after


def store_masked(target, bars, first_row, solid_value):
    def put(t, value):
        target[t] = jnp.where(first_row < bars[t], solid_value, value)

    return put


def velocity(sx_ref, sy_ref, fx_ref, fy_ref, v):
    return sx_ref[v].astype(F32) + fx_ref[v], sy_ref[v].astype(F32) + fy_ref[v]


def sum_moments(planes_ref, k, weights, lane_tile_range):
    sums = [[None] * 4 for _ in lane_tile_range]
    for v, (along_x, along_y) in enumerate(weights):
        square = along_x * along_x + along_y * along_y
        for n, t in enumerate(lane_tile_range):
            f = planes_ref[v, k, t]
            terms = (f, f * along_x, f * along_y, f * square)
            sums[n] = [b if a is None else a + b for a, b in zip(sums[n], terms)]
    return sums


class Plan:
    def __init__(self, row_tiles, half):
        self.tile = 4 * half
        self.inside = list(range(2, row_tiles - 2))
        self.sizes = [self.tile + 4, self.tile, len(self.inside) * self.tile, 2 * self.tile, 2 * self.tile]
        self.starts = [sum(self.sizes[:n]) for n in range(len(self.sizes) + 1)]
        self.row_tiles = row_tiles

    def start(self, j):
        low = self.starts[3] + self.tile * j
        high = self.starts[4] + self.tile * (j - self.row_tiles + 2)
        inside = self.starts[2] + self.tile * (j - 2)
        return jnp.where(j < 2, low, jnp.where(j >= self.row_tiles - 2, high, inside))


def advance_kernel(plan, cuts, group, sx_ref, sy_ref, fx_ref, fy_ref, inflow_ref, wall_ref,
                   heights_ref, pop_ref, *refs):
    planes_ref, mine_ref, theirs_ref, more_ref = refs[:4]
    packs = refs[4 : 4 + len(cuts)]
    (padded, planes_buf, outer, last_row, low_pack, high_pack, bars, sem_in, sem_planes, sem_out) = refs[
        4 + len(cuts) :
    ]
    planes, row_tiles, lane_tiles = pop_ref.shape[:3]
    half = lane_tiles // 2
    rows = row_tiles * ROW
    row0, first, last, core = place(rows)

    def loads(g):
        members = pl.ds(g * group, group)
        return [
            pltpu.make_async_copy(
                pop_ref.at[members, i],
                padded.at[members, 1 : 1 + lane_tiles, PAD + ROW * i : PAD + ROW * (i + 1), :],
                sem_in.at[g, i],
            )
            for i in range(row_tiles)
        ]

    def start(g, _):
        for load in loads(g):
            load.start()
        return 0

    lax.fori_loop(0, planes // group, start, 0)
    prepare_heights(heights_ref, bars)
    last_row[...] = jnp.zeros_like(last_row)

    def put_sums(h, first_block, sums):
        for is_mine, ref in ((True, mine_ref), (False, theirs_ref)):

            @pl.when((core == h) == is_mine)
            def _():
                for n, value in enumerate(sums):
                    ref[first_block + n] = value


    def out_copy(v):
        return pltpu.make_async_copy(planes_buf.at[v], planes_ref.at[v], sem_planes.at[v])

    def one(v, offsets):
        low, high = offsets
        value = inflow_ref[v]
        shift = sy_ref[v]
        up = shift >= 0
        columns = range(lane_tiles + 2)
        fill_rows(padded, v, (0, lane_tiles + 1), PAD, rows, value)
        fill_rows(padded, v, columns, 0, PAD, jnp.where(first, value, 0.0))
        fill_rows(padded, v, columns, PAD + rows, ROW, jnp.where(last, value, 0.0))

        @pl.when(v % group == 0)
        def _():
            for load in loads(v // group):
                load.wait()

        scalars = sx_ref[v], shift, fx_ref[v], fy_ref[v]
        work = [
            (PAD + ROW * j, store_masked(planes_buf.at[v, j], bars, row0 + ROW * j, wall_ref[v]))
            for j in range(row_tiles)
        ]
        beyond = jnp.where(up, rows, -ROW)
        work.append((PAD + beyond, store_masked(outer.at[v], bars, row0 + beyond, 0.0)))
        advect(padded, v, scalars, work)
        out_copy(v).start()

        @pl.when(shift == CFL)
        def _():
            along_x, along_y = velocity(sx_ref, sy_ref, fx_ref, fy_ref, v)
            factors = 1.0, along_x, along_y, along_x * along_x + along_y * along_y

            def put(t, value):
                row = jnp.where(row0 + rows + ROW < bars[t], 0.0, value)
                h, r = divmod(t, half)
                for m in range(4):
                    total = last_row[h, m, r : r + 1, :] + (row * factors[m])[0:1, :]
                    last_row[h, m, r : r + 1, :] = total

            advect(padded, v, scalars, [(PAD + rows + ROW, put)])

        @pl.when(up)
        def _():
            for t in range(lane_tiles):
                source = pl.ds(PAD + rows - 1 - shift, 8)
                low_pack[t, pl.ds(low, 8), :] = padded[v, t + 1, source, :]

        @pl.when(shift == CFL)
        def _():
            for t in range(lane_tiles):
                low_pack[t, pl.ds(low + 8, 1), :] = padded[v, t + 1, PAD + rows - 1 : PAD + rows, :]

        @pl.when(jnp.logical_not(up))
        def _():
            for t in range(lane_tiles):
                high_pack[t, pl.ds(high, 8), :] = padded[v, t + 1, PAD : PAD + 8, :]

        return low + low_need(shift), high + high_need(shift)

    needs = lax.fori_loop(0, planes, one, (jnp.int32(0), jnp.int32(0)))
    sent = [end for _, begin, end in cuts if begin == 0]
    overflows = (needs[0] > sent[0]) | (needs[1] > sent[1])
    more_ref[0] = jnp.where(overflows, 1, 0)

    def pack_copy(n):
        pack, begin, end = cuts[n]
        source = (low_pack, high_pack)[pack].at[:, begin:end, :]
        return pltpu.make_async_copy(source, packs[n], sem_out.at[n])

    def each_pack(act):
        for n, (_, begin, _) in enumerate(cuts):
            if begin == 0:
                act(pack_copy(n))
            else:
                pl.when(overflows)(lambda n=n: act(pack_copy(n)))

    each_pack(lambda copy: copy.start())
    for h in range(2):
        put_sums(h, plan.tile, [last_row[h, m] for m in range(4)])
        for rising in (True, False):
            for part in range(2):
                tiles = range(h * half + part * half // 2, h * half + (part + 1) * half // 2)
                sums = [[None] * 4 for _ in tiles]
                for v in range(planes):
                    along_x, along_y = velocity(sx_ref, sy_ref, fx_ref, fy_ref, v)
                    goes = jnp.where((sy_ref[v] >= 0) == rising, 1.0, 0.0)
                    square = (along_x * along_x + along_y * along_y) * goes
                    factors = goes, along_x * goes, along_y * goes, square
                    for n, t in enumerate(tiles):
                        f = outer[v, t]
                        terms = [f * w for w in factors]
                        sums[n] = [b if a is None else a + b for a, b in zip(sums[n], terms)]
                begin = plan.starts[0 if rising else 1] + part * half // 2
                for m in range(4):
                    put_sums(h, begin + m * half, [sums[n][m] for n in range(len(tiles))])
    weights = [velocity(sx_ref, sy_ref, fx_ref, fy_ref, v) for v in range(planes)]

    def step(j, _):
        begin = plan.start(j)
        for h in range(2):
            sums = sum_moments(planes_buf, j, weights, range(h * half, (h + 1) * half))
            put_sums(h, begin, [sums[t][m] for m in range(4) for t in range(half)])
        return 0

    lax.fori_loop(0, row_tiles, step, 0)

    def finish(v, _):
        out_copy(v).wait()
        return 0

    lax.fori_loop(0, planes, finish, 0)
    each_pack(lambda copy: copy.wait())


def advance(plan, small, heights, pop, cuts):
    planes, row_tiles, lane_tiles = pop.shape[:3]
    group = math.gcd(planes, 2)
    blocks = plan.starts[-1]
    half_sums = jax.ShapeDtypeStruct((blocks, ROW, LANE), F32)
    return pl.pallas_call(
        functools.partial(advance_kernel, plan, cuts, group),
        out_shape=[pltpu.HBM(pop.shape, F32), half_sums, half_sums, jax.ShapeDtypeStruct((1,), jnp.int32)]
        + [pltpu.HBM((lane_tiles, end - begin, LANE), F32) for _, begin, end in cuts],
        in_specs=[SMEM_SPEC] * 6 + [VMEM_SPEC, HBM_SPEC],
        out_specs=[HBM_SPEC, VMEM_SPEC, VMEM_SPEC, SMEM_SPEC] + [HBM_SPEC] * len(cuts),
        scratch_shapes=[
            pltpu.VMEM((planes, lane_tiles + 2, PAD + row_tiles * ROW + ROW, LANE), F32),
            pltpu.VMEM((planes, row_tiles, lane_tiles, ROW, LANE), F32),
            pltpu.VMEM((planes, lane_tiles, ROW, LANE), F32),
            pltpu.VMEM((2, 4, ROW, LANE), F32),
            pltpu.VMEM((lane_tiles, planes * LOW_ROWS + 16, LANE), F32),
            pltpu.VMEM((lane_tiles, planes * HIGH_ROWS + 16, LANE), F32),
            pltpu.VMEM((lane_tiles, ROW, LANE), jnp.int32),
            pltpu.SemaphoreType.DMA((planes // group, row_tiles)),
            pltpu.SemaphoreType.DMA((planes,)),
            pltpu.SemaphoreType.DMA((len(cuts),)),
        ],
        compiler_params=params(36),
        name="advance",
    )(*in_hbm(*small, heights, pop))


def fold_kernel(mine_ref, received_ref, *out_refs):
    begin = 0
    for ref in out_refs:
        n = ref.shape[0]
        ref[...] = mine_ref[begin : begin + n] + received_ref[begin : begin + n]
        begin += n


def fold(mine, received, sizes):
    return pl.pallas_call(
        fold_kernel,
        out_shape=[jax.ShapeDtypeStruct((n, ROW, LANE), F32) for n in sizes],
        in_specs=[VMEM_SPEC] * 2,
        out_specs=[VMEM_SPEC] * len(sizes),
        compiler_params=params(8),
        name="fold",
    )(mine, received)


def join_low_kernel(own_ref, low_ref, *refs):
    out_ref = refs[-1]
    tile = own_ref.shape[0] // 2
    half = tile // 4
    out_ref[2 * tile :] = jnp.zeros((out_ref.shape[0] - 2 * tile, ROW, LANE), F32)
    out_ref[:tile] = own_ref[:tile] + low_ref[:tile]
    top = lax.broadcasted_iota(jnp.int32, (ROW, LANE), 0) == 0
    for m in range(4):
        for n in range(half):
            row = jnp.broadcast_to(low_ref[tile + m, n : n + 1, :], (ROW, LANE))
            index = tile + m * half + n
            out_ref[index] = own_ref[index] + jnp.where(top, row, 0.0)


def add_kernel(a_ref, b_ref, *refs):
    refs[-1][...] = a_ref[...] + b_ref[...]


def join_high_kernel(own_ref, high_ref, *refs):
    out_ref = refs[-1]
    tile = high_ref.shape[0]
    out_ref[2 * tile :] = jnp.zeros((out_ref.shape[0] - 2 * tile, ROW, LANE), F32)
    out_ref[:tile] = own_ref[:tile]
    out_ref[tile : 2 * tile] = own_ref[tile:] + high_ref[...]


def small_call(kernel, name, a, b, after=(), extra=0):
    operands = a, b, *after
    shape = (a.shape[0] + extra, *a.shape[1:])
    return pl.pallas_call(
        kernel,
        out_shape=jax.ShapeDtypeStruct(shape, F32),
        in_specs=[VMEM_SPEC] * 2 + [ANY_SPEC] * len(after),
        out_specs=VMEM_SPEC,
        compiler_params=params(8),
        name=name,
    )(*operands)


def profile(density, flux_x, flux_y, energy, factor):
    inverse = 1.0 / density
    mean_x = flux_x * inverse
    mean_y = flux_y * inverse
    temperature = 0.5 * (energy * inverse - mean_x * mean_x - mean_y * mean_y)
    rate = 1.0 - jnp.exp(-factor * density / (SPEED_TALLY * jnp.sqrt(temperature)))
    height = rate * (density / (2.0 * math.pi * temperature))
    return mean_x, mean_y, -0.5 / temperature, height, 1.0 - rate


def relax_cells(get, put, values, factor, weights):
    mean_x, mean_y, scale, height, keep = profile(*values, factor)
    for v, (along_x, along_y) in enumerate(weights):
        gap_x = along_x - mean_x
        gap_y = along_y - mean_y
        state = height * jnp.exp((gap_x * gap_x + gap_y * gap_y) * scale)
        put(v, keep * get(v) + state)


def relax_tile(buf, sums, base, core, factor, weights, k, h):
    mine_ref, other_ref = sums
    half = buf.shape[2] // 2
    for n in range(half):
        t = h * half + n
        values = []
        for m in range(4):
            index = base + m * half + n
            values.append(jnp.where(core == h, mine_ref[index], other_ref[index]))

        def put(v, value):
            buf[v, k, t] = value

        relax_cells(lambda v: buf[v, k, t], put, values, factor, weights)


def relax_kernel(sizes, sx_ref, sy_ref, fx_ref, fy_ref, factor_ref, planes_ref, *refs):
    sums_refs = refs[:-4]
    out_ref, buf, sem_in, sem_out = refs[-4:]
    planes, row_tiles, lane_tiles = planes_ref.shape[:3]
    half = lane_tiles // 2

    def copy(j, h, out):
        lanes = pl.ds(h * half, half)
        here = buf.at[:, j, lanes]
        if out:
            return pltpu.make_async_copy(here, out_ref.at[:, j, lanes], sem_out.at[2 * j + h])
        return pltpu.make_async_copy(planes_ref.at[:, j, lanes], here, sem_in.at[2 * j + h])

    def tile(k):
        return jnp.where(k < row_tiles - 2, k + 2, k + 2 - row_tiles)

    def start(k, _):
        for h in range(2):
            copy(tile(k), h, False).start()
        return 0

    lax.fori_loop(0, row_tiles, start, 0)
    weights = [velocity(sx_ref, sy_ref, fx_ref, fy_ref, v) for v in range(planes)]
    core = lax.axis_index("vel") % 2
    begin = 0
    for pair, size in enumerate(sizes):
        sums = sums_refs[2 * pair : 2 * pair + 2]

        def step(k, _, begin=begin, sums=sums):
            j = tile(k)
            for h in range(2):
                copy(j, h, False).wait()
                base = (k - begin) * 4 * half
                relax_tile(buf, sums, base, core, factor_ref[0], weights, j, h)
                copy(j, h, True).start()
            return 0

        lax.fori_loop(begin, begin + size, step, 0)
        begin += size

    def finish(j, _):
        for h in range(2):
            copy(j, h, True).wait()
        return 0

    lax.fori_loop(0, row_tiles, finish, 0)


def relax_all(sizes, small, factor, sums, moved):
    planes, row_tiles, lane_tiles = moved.shape[:3]
    operands = [*in_hbm(*small[:4]), factor, *in_hbm(moved), *sums]
    return pl.pallas_call(
        functools.partial(relax_kernel, sizes),
        out_shape=pltpu.HBM(moved.shape, F32),
        in_specs=[SMEM_SPEC] * 5 + [HBM_SPEC] + [VMEM_SPEC] * len(sums),
        out_specs=HBM_SPEC,
        scratch_shapes=[
            pltpu.VMEM((planes, row_tiles, lane_tiles, ROW, LANE), F32),
            pltpu.SemaphoreType.DMA((2 * row_tiles,)),
            pltpu.SemaphoreType.DMA((2 * row_tiles,)),
        ],
        compiler_params=params(24),
        name="relax_all",
    )(*operands)


def finish_kernel(cuts, sx_ref, sy_ref, fx_ref, fy_ref, inflow_ref, factor_ref, heights_ref,
                  m_low, o_low, m_high, o_high, before_ref, *refs):
    pack_refs = refs[: len(cuts)]
    out_ref, frames, buf, keeps, low_buf, high_buf, bars, sem_in, sem_planes, sem_out = refs[len(cuts) :]
    planes, row_tiles, lane_tiles = before_ref.shape[:3]
    half = lane_tiles // 2
    row0, first, last, core = place(row_tiles * ROW)
    needs = [low_need(sy_ref[0]), high_need(sy_ref[0])]
    for v in range(1, planes):
        needs = [needs[0] + low_need(sy_ref[v]), needs[1] + high_need(sy_ref[v])]

    def pack_copy(n):
        pack, begin, end = cuts[n]
        target = (low_buf, high_buf)[pack].at[:, 16 + begin : 16 + end, :]
        return pltpu.make_async_copy(pack_refs[n], target, sem_in.at[n])

    def cases(v):
        shift = sy_ref[v]
        from_low = (shift >= 0) & jnp.logical_not(first)
        return from_low, (shift < 0) & jnp.logical_not(last), from_low & (shift == CFL)

    tile_of = 0, row_tiles - 1, 1
    slot_of = 0, 0, 1

    def copy(v, case, out):
        here = buf.at[v, slot_of[case]]
        if out:
            return pltpu.make_async_copy(here, out_ref.at[v, tile_of[case]], sem_out.at[v, slot_of[case]])
        there = before_ref.at[v, tile_of[case]]
        return pltpu.make_async_copy(there, here, sem_planes.at[v, slot_of[case]])

    for n in range(len(cuts)):
        pl.when(needs[cuts[n][0]] > cuts[n][1])(lambda n=n: pack_copy(n).start())

    def start(v, _):
        for case, applies in enumerate(cases(v)):
            pl.when(applies)(lambda case=case: copy(v, case, False).start())
        return 0

    lax.fori_loop(0, planes, start, 0)
    prepare_heights(heights_ref, bars)
    for t in range(lane_tiles + 2):
        for r in (24, 32):
            frames[0, t, r : r + ROW, :] = jnp.zeros((ROW, LANE), F32)
        for r in (16, 24):
            frames[1, t, r : r + ROW, :] = jnp.zeros((ROW, LANE), F32)
    edges = ((m_low, o_low), 0), ((m_high, o_high), 4 * half), ((m_low, o_low), 4 * half)
    for case, (sums, base) in enumerate(edges):
        for t in range(lane_tiles):
            h, n = divmod(t, half)
            values = []
            for m in range(4):
                index = base + m * half + n
                values.append(jnp.where(core == h, sums[0][index], sums[1][index]))
            keeps[case, t] = profile(*values, factor_ref[0])[4]
    for n in range(len(cuts)):
        pl.when(needs[cuts[n][0]] > cuts[n][1])(lambda n=n: pack_copy(n).wait())

    def add_masked(v, case):
        first_row = row0 + ROW * tile_of[case]

        def put(t, value):
            part = jnp.where(first_row < bars[t], 0.0, value)
            buf[v, slot_of[case], t] = buf[v, slot_of[case], t] + keeps[case, t] * part

        return put

    def one(v, offsets):
        low, high = offsets
        value = inflow_ref[v]
        shift = sy_ref[v]
        scalars = sx_ref[v], shift, fx_ref[v], fy_ref[v]
        borders = (0, lane_tiles + 1)
        from_low, from_high, reaches_second = cases(v)

        @pl.when(from_low)
        def _():
            fill_rows(frames, 0, borders, 16, 8, value)
            for t in range(lane_tiles):
                frames[0, t + 1, 16:24, :] = low_buf[t, pl.ds(low + shift + 9, ROW), :]

            @pl.when(shift == CFL)
            def _():
                fill_rows(frames, 0, borders, 8, 8, value)
                for t in range(lane_tiles):
                    frames[0, t + 1, 8:16, :] = low_buf[t, pl.ds(low + shift + 1, ROW), :]

            copy(v, 0, False).wait()
            advect(frames, 0, scalars, [(24, add_masked(v, 0))])
            copy(v, 0, True).start()

        @pl.when(reaches_second)
        def _():
            copy(v, 2, False).wait()
            advect(frames, 0, scalars, [(32, add_masked(v, 2))])
            copy(v, 2, True).start()

        @pl.when(from_high)
        def _():
            fill_rows(frames, 1, borders, 32, 8, value)
            for t in range(lane_tiles):
                frames[1, t + 1, 32:40, :] = high_buf[t, pl.ds(16 + high, ROW), :]
            copy(v, 1, False).wait()
            advect(frames, 1, scalars, [(24, add_masked(v, 1))])
            copy(v, 1, True).start()

        return low + low_need(shift), high + high_need(shift)

    lax.fori_loop(0, planes, one, (jnp.int32(0), jnp.int32(0)))

    def end(v, _):
        for case, applies in enumerate(cases(v)):
            pl.when(applies)(lambda case=case: copy(v, case, True).wait())
        return 0

    lax.fori_loop(0, planes, end, 0)


def finish_edges(small, factor, heights, sums, packs, cuts, out):
    planes, _, lane_tiles = out.shape[:3]
    fixed = [*in_hbm(*small[:5]), factor, *in_hbm(heights)]
    operands = [*fixed, *sums, *in_hbm(out), *packs]
    return pl.pallas_call(
        functools.partial(finish_kernel, cuts),
        out_shape=pltpu.HBM(out.shape, F32),
        in_specs=[SMEM_SPEC] * 6 + [VMEM_SPEC] * 5 + [HBM_SPEC] + [ANY_SPEC] * len(cuts),
        out_specs=HBM_SPEC,
        scratch_shapes=[
            pltpu.VMEM((2, lane_tiles + 2, 48, LANE), F32),
            pltpu.VMEM((planes, 2, lane_tiles, ROW, LANE), F32),
            pltpu.VMEM((3, lane_tiles, ROW, LANE), F32),
            pltpu.VMEM((lane_tiles, planes * LOW_ROWS + 32, LANE), F32),
            pltpu.VMEM((lane_tiles, planes * HIGH_ROWS + 32, LANE), F32),
            pltpu.VMEM((lane_tiles, ROW, LANE), jnp.int32),
            pltpu.SemaphoreType.DMA((len(cuts),)),
            pltpu.SemaphoreType.DMA((planes, 2)),
            pltpu.SemaphoreType.DMA((planes, 2)),
        ],
        input_output_aliases={len(fixed) + len(sums): 0},
        compiler_params=params(24),
        name="finish_edges",
    )(*operands)


def per_device(populations, shift_x, shift_y, frac_x, frac_y, inflow, wall_state, heights,
               impact_frequency_factor):
    planes, row_count, col_count = populations.shape
    space_count, vel_count = lax.axis_size("space"), lax.axis_size("vel")
    row_tiles, lane_tiles = row_count // ROW, col_count // LANE
    forward = [(i, i + 1) for i in range(space_count - 1)]
    backward = [(target, source) for source, target in forward]
    partner = [(i, i ^ 1) for i in range(vel_count)]
    across = [(i, i ^ 2) for i in range(vel_count)]

    small = (shift_x, shift_y, frac_x, frac_y, inflow, wall_state)
    factor = impact_frequency_factor.reshape(1)
    bars = heights.reshape(lane_tiles, LANE)
    pop = populations.reshape(planes, row_tiles, ROW, lane_tiles, LANE).transpose(0, 1, 3, 2, 4)
    low_sent, high_sent = min(LOW_SENT, planes * LOW_ROWS), min(HIGH_SENT, planes * HIGH_ROWS)
    cuts = [
        (0, 0, low_sent),
        (1, 0, high_sent),
        (0, low_sent, planes * LOW_ROWS),
        (1, high_sent, planes * HIGH_ROWS),
    ]
    plan = Plan(row_tiles, lane_tiles // 2)

    moved, mine, theirs, more_needed, *packs = advance(plan, small, bars, pop, cuts)
    received = lax.ppermute(theirs, "vel", partner)
    up, down, inside, edge_low, edge_high = fold(mine, received, plan.sizes)
    from_low = lax.ppermute(up, "space", forward)
    from_high = lax.ppermute(down, "space", backward)
    low_first = lax.ppermute(packs[0], "space", forward)
    high_first = lax.ppermute(packs[1], "space", backward)

    def total(sums, after=()):
        whole = small_call(add_kernel, "add", sums, lax.ppermute(sums, "vel", across), after)
        return whole, lax.ppermute(whole, "vel", partner)

    def send_more(low, high):
        return lax.ppermute(low, "space", forward), lax.ppermute(high, "space", backward)

    more = lax.cond(more_needed[0] > 0, send_more, lambda low, high: (low, high), packs[2], packs[3])
    sums_inside = total(inside)
    sums_low = total(small_call(join_low_kernel, "join_low", edge_low, from_low, (), 1))
    sums_high = total(small_call(join_high_kernel, "join_high", edge_high, from_high, (), 1))
    sizes = len(plan.inside), 2, 2
    out = relax_all(sizes, small, factor, sums_inside + sums_high + sums_low, moved)
    halo = low_first, high_first, *more
    out = finish_edges(small, factor, bars, sums_low + sums_high, halo, cuts, out)
    return out.transpose(0, 1, 3, 2, 4).reshape(planes, row_count, col_count)


def solution(mesh):
    return jax.shard_map(
        per_device,
        mesh=mesh,
        in_specs=(
            P("vel", "space", None),
            P("vel"),
            P("vel"),
            P("vel"),
            P("vel"),
            P("vel"),
            P("vel"),
            P(),
            P(),
        ),
        out_specs=P("vel", "space", None),
        check_vma=False,
    )
```

```python
import functools
import math

import jax
import jax.numpy as jnp
from jax import lax
from jax.experimental import pallas as pl
from jax.experimental.pallas import tpu as pltpu
from jax.sharding import PartitionSpec as P

SPEED_TALLY = 64
CFL = 8
LOW_ROWS = CFL + 1
HIGH_ROWS = CFL
ROW = 8
LANE = 128
PAD = 16
F32 = jnp.float32
LOW_SENT = 72
HIGH_SENT = 64

SMEM_SPEC = pl.BlockSpec(memory_space=pltpu.SMEM)
ANY_SPEC = pl.BlockSpec(memory_space=pl.ANY)
HBM_SPEC = pl.BlockSpec(memory_space=pltpu.HBM)
VMEM_SPEC = pl.BlockSpec(memory_space=pltpu.VMEM)


def params(mebibytes):
    return pltpu.CompilerParams(vmem_limit_bytes=mebibytes * 1024 * 1024)


def in_hbm(*arrays):
    return [pltpu.with_memory_space_constraint(x, pltpu.HBM) for x in arrays]


def place(rows):
    space = lax.axis_index("space")
    return space * rows, space == 0, space == lax.axis_size("space") - 1, lax.axis_index("vel") % 2


def low_need(shift):
    return jnp.where(shift >= 0, shift + 1, 0)


def high_need(shift):
    return jnp.where(shift < 0, -shift, 0)


def fill_rows(padded, v, columns, start, count, value):
    block = jnp.full((ROW, LANE), value, F32)
    for t in columns:
        for r in range(start, start + count, ROW):
            padded[v, t, r : r + ROW, :] = block


def prepare_heights(heights_ref, bars):
    lane_tiles = heights_ref.shape[0]
    sublane = lax.broadcasted_iota(jnp.int32, (ROW, LANE), 0)
    for t in range(lane_tiles):
        bars[t] = jnp.broadcast_to(heights_ref[t : t + 1, :], (ROW, LANE)) - sublane


def advect(padded, v, scalars, tiles):
    sx, sy, fx, fy = scalars
    lane_tiles = padded.shape[1] - 2
    lane = lax.broadcasted_iota(jnp.int32, (ROW, LANE), 1)
    near_roll = jnp.where(sx < 0, sx + LANE, sx)
    far_roll = jnp.where(sx + 1 < 0, sx + 1 + LANE, sx + 1)

    def moved(start, t):
        nearer = padded[v, t + 1, pl.ds(start, ROW), :]
        further = padded[v, t + 1, pl.ds(start - 1, ROW), :]
        line = (1.0 - fy) * nearer + fy * further
        if t < 0 or t == lane_tiles:
            return line, line
        return pltpu.roll(line, near_roll, 1), pltpu.roll(line, far_roll, 1)

    def blend(put, t, near, far):
        put(t, (1.0 - fx) * near + fx * far)

    @pl.when(sx >= 0)
    def _():
        own_near, own_far = lane >= sx, lane >= sx + 1
        for begin, put in tiles:
            before = moved(begin - sy, -1)
            for t in range(lane_tiles):
                here = moved(begin - sy, t)
                near = jnp.where(own_near, here[0], before[0])
                blend(put, t, near, jnp.where(own_far, here[1], before[1]))
                before = here

    @pl.when(sx < 0)
    def _():
        own_near, own_far = lane < sx + LANE, lane < sx + 1 + LANE
        for begin, put in tiles:
            here = moved(begin - sy, 0)
            for t in range(lane_tiles):
                after = moved(begin - sy, t + 1)
                near = jnp.where(own_near, here[0], after[0])
                blend(put, t, near, jnp.where(own_far, here[1], after[1]))
                here = after


def store_masked(target, bars, first_row, solid_value):
    def put(t, value):
        target[t] = jnp.where(first_row < bars[t], solid_value, value)

    return put


def velocity(sx_ref, sy_ref, fx_ref, fy_ref, v):
    return sx_ref[v].astype(F32) + fx_ref[v], sy_ref[v].astype(F32) + fy_ref[v]


def sum_moments(planes_ref, k, weights, lane_tile_range):
    sums = [[None] * 4 for _ in lane_tile_range]
    for v, (along_x, along_y) in enumerate(weights):
        square = along_x * along_x + along_y * along_y
        for n, t in enumerate(lane_tile_range):
            f = planes_ref[v, k, t]
            terms = (f, f * along_x, f * along_y, f * square)
            sums[n] = [b if a is None else a + b for a, b in zip(sums[n], terms)]
    return sums


class Plan:
    def __init__(self, row_tiles, half):
        self.tile = 4 * half
        self.inside = list(range(2, row_tiles - 2))
        self.sizes = [self.tile + 4, self.tile, len(self.inside) * self.tile, 2 * self.tile, 2 * self.tile]
        self.starts = [sum(self.sizes[:n]) for n in range(len(self.sizes) + 1)]
        self.row_tiles = row_tiles

    def start(self, j):
        low = self.starts[3] + self.tile * j
        high = self.starts[4] + self.tile * (j - self.row_tiles + 2)
        inside = self.starts[2] + self.tile * (j - 2)
        return jnp.where(j < 2, low, jnp.where(j >= self.row_tiles - 2, high, inside))


def advance_kernel(plan, cuts, group, sx_ref, sy_ref, fx_ref, fy_ref, inflow_ref, wall_ref,
                   heights_ref, pop_ref, *refs):
    planes_ref, mine_ref, theirs_ref, more_ref = refs[:4]
    packs = refs[4 : 4 + len(cuts)]
    (padded, planes_buf, outer, last_row, low_pack, high_pack, bars, sem_in, sem_planes, sem_out) = refs[
        4 + len(cuts) :
    ]
    planes, row_tiles, lane_tiles = pop_ref.shape[:3]
    half = lane_tiles // 2
    rows = row_tiles * ROW
    row0, first, last, core = place(rows)

    def loads(g):
        members = pl.ds(g * group, group)
        return [
            pltpu.make_async_copy(
                pop_ref.at[members, i],
                padded.at[members, 1 : 1 + lane_tiles, PAD + ROW * i : PAD + ROW * (i + 1), :],
                sem_in.at[g, i],
            )
            for i in range(row_tiles)
        ]

    def start(g, _):
        for load in loads(g):
            load.start()
        return 0

    lax.fori_loop(0, planes // group, start, 0)
    prepare_heights(heights_ref, bars)
    last_row[...] = jnp.zeros_like(last_row)

    def put_sums(h, first_block, sums):
        for is_mine, ref in ((True, mine_ref), (False, theirs_ref)):

            @pl.when((core == h) == is_mine)
            def _():
                for n, value in enumerate(sums):
                    ref[first_block + n] = value


    def out_copy(v):
        return pltpu.make_async_copy(planes_buf.at[v], planes_ref.at[v], sem_planes.at[v])

    def one(v, offsets):
        low, high = offsets
        value = inflow_ref[v]
        shift = sy_ref[v]
        up = shift >= 0
        columns = range(lane_tiles + 2)
        fill_rows(padded, v, (0, lane_tiles + 1), PAD, rows, value)
        fill_rows(padded, v, columns, 0, PAD, jnp.where(first, value, 0.0))
        fill_rows(padded, v, columns, PAD + rows, ROW, jnp.where(last, value, 0.0))

        @pl.when(v % group == 0)
        def _():
            for load in loads(v // group):
                load.wait()

        scalars = sx_ref[v], shift, fx_ref[v], fy_ref[v]
        work = [
            (PAD + ROW * j, store_masked(planes_buf.at[v, j], bars, row0 + ROW * j, wall_ref[v]))
            for j in range(row_tiles)
        ]
        beyond = jnp.where(up, rows, -ROW)
        work.append((PAD + beyond, store_masked(outer.at[v], bars, row0 + beyond, 0.0)))
        advect(padded, v, scalars, work)
        out_copy(v).start()

        @pl.when(shift == CFL)
        def _():
            along_x, along_y = velocity(sx_ref, sy_ref, fx_ref, fy_ref, v)
            factors = 1.0, along_x, along_y, along_x * along_x + along_y * along_y

            def put(t, value):
                row = jnp.where(row0 + rows + ROW < bars[t], 0.0, value)
                h, r = divmod(t, half)
                for m in range(4):
                    total = last_row[h, m, r : r + 1, :] + (row * factors[m])[0:1, :]
                    last_row[h, m, r : r + 1, :] = total

            advect(padded, v, scalars, [(PAD + rows + ROW, put)])

        @pl.when(up)
        def _():
            for t in range(lane_tiles):
                source = pl.ds(PAD + rows - 1 - shift, 8)
                low_pack[t, pl.ds(low, 8), :] = padded[v, t + 1, source, :]

        @pl.when(shift == CFL)
        def _():
            for t in range(lane_tiles):
                low_pack[t, pl.ds(low + 8, 1), :] = padded[v, t + 1, PAD + rows - 1 : PAD + rows, :]

        @pl.when(jnp.logical_not(up))
        def _():
            for t in range(lane_tiles):
                high_pack[t, pl.ds(high, 8), :] = padded[v, t + 1, PAD : PAD + 8, :]

        return low + low_need(shift), high + high_need(shift)

    needs = lax.fori_loop(0, planes, one, (jnp.int32(0), jnp.int32(0)))
    sent = [end for _, begin, end in cuts if begin == 0]
    overflows = (needs[0] > sent[0]) | (needs[1] > sent[1])
    more_ref[0] = jnp.where(overflows, 1, 0)

    def pack_copy(n):
        pack, begin, end = cuts[n]
        source = (low_pack, high_pack)[pack].at[:, begin:end, :]
        return pltpu.make_async_copy(source, packs[n], sem_out.at[n])

    def each_pack(act):
        for n, (_, begin, _) in enumerate(cuts):
            if begin == 0:
                act(pack_copy(n))
            else:
                pl.when(overflows)(lambda n=n: act(pack_copy(n)))

    each_pack(lambda copy: copy.start())
    for h in range(2):
        put_sums(h, plan.tile, [last_row[h, m] for m in range(4)])
        for rising in (True, False):
            for part in range(2):
                tiles = range(h * half + part * half // 2, h * half + (part + 1) * half // 2)
                sums = [[None] * 4 for _ in tiles]
                for v in range(planes):
                    along_x, along_y = velocity(sx_ref, sy_ref, fx_ref, fy_ref, v)
                    goes = jnp.where((sy_ref[v] >= 0) == rising, 1.0, 0.0)
                    square = (along_x * along_x + along_y * along_y) * goes
                    factors = goes, along_x * goes, along_y * goes, square
                    for n, t in enumerate(tiles):
                        f = outer[v, t]
                        terms = [f * w for w in factors]
                        sums[n] = [b if a is None else a + b for a, b in zip(sums[n], terms)]
                begin = plan.starts[0 if rising else 1] + part * half // 2
                for m in range(4):
                    put_sums(h, begin + m * half, [sums[n][m] for n in range(len(tiles))])
    weights = [velocity(sx_ref, sy_ref, fx_ref, fy_ref, v) for v in range(planes)]

    def step(j, _):
        begin = plan.start(j)
        for h in range(2):
            sums = sum_moments(planes_buf, j, weights, range(h * half, (h + 1) * half))
            put_sums(h, begin, [sums[t][m] for m in range(4) for t in range(half)])
        return 0

    lax.fori_loop(0, row_tiles, step, 0)

    def finish(v, _):
        out_copy(v).wait()
        return 0

    lax.fori_loop(0, planes, finish, 0)
    each_pack(lambda copy: copy.wait())


def advance(plan, small, heights, pop, cuts):
    planes, row_tiles, lane_tiles = pop.shape[:3]
    group = math.gcd(planes, 2)
    blocks = plan.starts[-1]
    half_sums = jax.ShapeDtypeStruct((blocks, ROW, LANE), F32)
    return pl.pallas_call(
        functools.partial(advance_kernel, plan, cuts, group),
        out_shape=[pltpu.HBM(pop.shape, F32), half_sums, half_sums, jax.ShapeDtypeStruct((1,), jnp.int32)]
        + [pltpu.HBM((lane_tiles, end - begin, LANE), F32) for _, begin, end in cuts],
        in_specs=[SMEM_SPEC] * 6 + [VMEM_SPEC, HBM_SPEC],
        out_specs=[HBM_SPEC, VMEM_SPEC, VMEM_SPEC, SMEM_SPEC] + [HBM_SPEC] * len(cuts),
        scratch_shapes=[
            pltpu.VMEM((planes, lane_tiles + 2, PAD + row_tiles * ROW + ROW, LANE), F32),
            pltpu.VMEM((planes, row_tiles, lane_tiles, ROW, LANE), F32),
            pltpu.VMEM((planes, lane_tiles, ROW, LANE), F32),
            pltpu.VMEM((2, 4, ROW, LANE), F32),
            pltpu.VMEM((lane_tiles, planes * LOW_ROWS + 16, LANE), F32),
            pltpu.VMEM((lane_tiles, planes * HIGH_ROWS + 16, LANE), F32),
            pltpu.VMEM((lane_tiles, ROW, LANE), jnp.int32),
            pltpu.SemaphoreType.DMA((planes // group, row_tiles)),
            pltpu.SemaphoreType.DMA((planes,)),
            pltpu.SemaphoreType.DMA((len(cuts),)),
        ],
        compiler_params=params(36),
        name="advance",
    )(*in_hbm(*small, heights, pop))


def fold_kernel(mine_ref, received_ref, *out_refs):
    begin = 0
    for ref in out_refs:
        n = ref.shape[0]
        ref[...] = mine_ref[begin : begin + n] + received_ref[begin : begin + n]
        begin += n


def fold(mine, received, sizes):
    return pl.pallas_call(
        fold_kernel,
        out_shape=[jax.ShapeDtypeStruct((n, ROW, LANE), F32) for n in sizes],
        in_specs=[VMEM_SPEC] * 2,
        out_specs=[VMEM_SPEC] * len(sizes),
        compiler_params=params(8),
        name="fold",
    )(mine, received)


def join_low_kernel(own_ref, low_ref, *refs):
    out_ref = refs[-1]
    tile = own_ref.shape[0] // 2
    half = tile // 4
    out_ref[2 * tile :] = jnp.zeros((out_ref.shape[0] - 2 * tile, ROW, LANE), F32)
    out_ref[:tile] = own_ref[:tile] + low_ref[:tile]
    top = lax.broadcasted_iota(jnp.int32, (ROW, LANE), 0) == 0
    for m in range(4):
        for n in range(half):
            row = jnp.broadcast_to(low_ref[tile + m, n : n + 1, :], (ROW, LANE))
            index = tile + m * half + n
            out_ref[index] = own_ref[index] + jnp.where(top, row, 0.0)


def add_kernel(a_ref, b_ref, *refs):
    refs[-1][...] = a_ref[...] + b_ref[...]


def join_high_kernel(own_ref, high_ref, *refs):
    out_ref = refs[-1]
    tile = high_ref.shape[0]
    out_ref[2 * tile :] = jnp.zeros((out_ref.shape[0] - 2 * tile, ROW, LANE), F32)
    out_ref[:tile] = own_ref[:tile]
    out_ref[tile : 2 * tile] = own_ref[tile:] + high_ref[...]


def small_call(kernel, name, a, b, after=(), extra=0):
    operands = a, b, *after
    shape = (a.shape[0] + extra, *a.shape[1:])
    return pl.pallas_call(
        kernel,
        out_shape=jax.ShapeDtypeStruct(shape, F32),
        in_specs=[VMEM_SPEC] * 2 + [ANY_SPEC] * len(after),
        out_specs=VMEM_SPEC,
        compiler_params=params(8),
        name=name,
    )(*operands)


def profile(density, flux_x, flux_y, energy, factor):
    inverse = 1.0 / density
    mean_x = flux_x * inverse
    mean_y = flux_y * inverse
    temperature = 0.5 * (energy * inverse - mean_x * mean_x - mean_y * mean_y)
    rate = 1.0 - jnp.exp(-factor * density / (SPEED_TALLY * jnp.sqrt(temperature)))
    height = rate * (density / (2.0 * math.pi * temperature))
    return mean_x, mean_y, -0.5 / temperature, height, 1.0 - rate


def relax_cells(get, put, values, factor, weights):
    mean_x, mean_y, scale, height, keep = profile(*values, factor)
    for v, (along_x, along_y) in enumerate(weights):
        gap_x = along_x - mean_x
        gap_y = along_y - mean_y
        state = height * jnp.exp((gap_x * gap_x + gap_y * gap_y) * scale)
        put(v, keep * get(v) + state)


def relax_tile(buf, sums, base, core, factor, weights, k, h):
    mine_ref, other_ref = sums
    half = buf.shape[2] // 2
    for n in range(half):
        t = h * half + n
        values = []
        for m in range(4):
            index = base + m * half + n
            values.append(jnp.where(core == h, mine_ref[index], other_ref[index]))

        def put(v, value):
            buf[v, k, t] = value

        relax_cells(lambda v: buf[v, k, t], put, values, factor, weights)


def relax_kernel(sizes, sx_ref, sy_ref, fx_ref, fy_ref, factor_ref, planes_ref, *refs):
    sums_refs = refs[:-4]
    out_ref, buf, sem_in, sem_out = refs[-4:]
    planes, row_tiles, lane_tiles = planes_ref.shape[:3]
    half = lane_tiles // 2

    def copy(j, h, out):
        lanes = pl.ds(h * half, half)
        here = buf.at[:, j, lanes]
        if out:
            return pltpu.make_async_copy(here, out_ref.at[:, j, lanes], sem_out.at[2 * j + h])
        return pltpu.make_async_copy(planes_ref.at[:, j, lanes], here, sem_in.at[2 * j + h])

    def tile(k):
        return jnp.where(k < row_tiles - 2, k + 2, k + 2 - row_tiles)

    def start(k, _):
        for h in range(2):
            copy(tile(k), h, False).start()
        return 0

    lax.fori_loop(0, row_tiles, start, 0)
    weights = [velocity(sx_ref, sy_ref, fx_ref, fy_ref, v) for v in range(planes)]
    core = lax.axis_index("vel") % 2
    begin = 0
    for pair, size in enumerate(sizes):
        sums = sums_refs[2 * pair : 2 * pair + 2]

        def step(k, _, begin=begin, sums=sums):
            j = tile(k)
            for h in range(2):
                copy(j, h, False).wait()
                base = (k - begin) * 4 * half
                relax_tile(buf, sums, base, core, factor_ref[0], weights, j, h)
                copy(j, h, True).start()
            return 0

        lax.fori_loop(begin, begin + size, step, 0)
        begin += size

    def finish(j, _):
        for h in range(2):
            copy(j, h, True).wait()
        return 0

    lax.fori_loop(0, row_tiles, finish, 0)


def relax_all(sizes, small, factor, sums, moved):
    planes, row_tiles, lane_tiles = moved.shape[:3]
    operands = [*in_hbm(*small[:4]), factor, *in_hbm(moved), *sums]
    return pl.pallas_call(
        functools.partial(relax_kernel, sizes),
        out_shape=pltpu.HBM(moved.shape, F32),
        in_specs=[SMEM_SPEC] * 5 + [HBM_SPEC] + [VMEM_SPEC] * len(sums),
        out_specs=HBM_SPEC,
        scratch_shapes=[
            pltpu.VMEM((planes, row_tiles, lane_tiles, ROW, LANE), F32),
            pltpu.SemaphoreType.DMA((2 * row_tiles,)),
            pltpu.SemaphoreType.DMA((2 * row_tiles,)),
        ],
        compiler_params=params(24),
        name="relax_all",
    )(*operands)


def finish_kernel(cuts, sx_ref, sy_ref, fx_ref, fy_ref, inflow_ref, factor_ref, heights_ref,
                  m_low, o_low, m_high, o_high, before_ref, *refs):
    pack_refs = refs[: len(cuts)]
    out_ref, frames, buf, keeps, low_buf, high_buf, bars, sem_in, sem_planes, sem_out = refs[len(cuts) :]
    planes, row_tiles, lane_tiles = before_ref.shape[:3]
    half = lane_tiles // 2
    row0, first, last, core = place(row_tiles * ROW)
    needs = [low_need(sy_ref[0]), high_need(sy_ref[0])]
    for v in range(1, planes):
        needs = [needs[0] + low_need(sy_ref[v]), needs[1] + high_need(sy_ref[v])]

    def pack_copy(n):
        pack, begin, end = cuts[n]
        target = (low_buf, high_buf)[pack].at[:, 16 + begin : 16 + end, :]
        return pltpu.make_async_copy(pack_refs[n], target, sem_in.at[n])

    def cases(v):
        shift = sy_ref[v]
        from_low = (shift >= 0) & jnp.logical_not(first)
        return from_low, (shift < 0) & jnp.logical_not(last), from_low & (shift == CFL)

    tile_of = 0, row_tiles - 1, 1
    slot_of = 0, 0, 1

    def copy(v, case, out):
        here = buf.at[v, slot_of[case]]
        if out:
            return pltpu.make_async_copy(here, out_ref.at[v, tile_of[case]], sem_out.at[v, slot_of[case]])
        there = before_ref.at[v, tile_of[case]]
        return pltpu.make_async_copy(there, here, sem_planes.at[v, slot_of[case]])

    for n in range(len(cuts)):
        pl.when(needs[cuts[n][0]] > cuts[n][1])(lambda n=n: pack_copy(n).start())

    def start(v, _):
        for case, applies in enumerate(cases(v)):
            pl.when(applies)(lambda case=case: copy(v, case, False).start())
        return 0

    lax.fori_loop(0, planes, start, 0)
    prepare_heights(heights_ref, bars)
    for t in range(lane_tiles + 2):
        for r in (24, 32):
            frames[0, t, r : r + ROW, :] = jnp.zeros((ROW, LANE), F32)
        for r in (16, 24):
            frames[1, t, r : r + ROW, :] = jnp.zeros((ROW, LANE), F32)
    edges = ((m_low, o_low), 0), ((m_high, o_high), 4 * half), ((m_low, o_low), 4 * half)
    for case, (sums, base) in enumerate(edges):
        for t in range(lane_tiles):
            h, n = divmod(t, half)
            values = []
            for m in range(4):
                index = base + m * half + n
                values.append(jnp.where(core == h, sums[0][index], sums[1][index]))
            keeps[case, t] = profile(*values, factor_ref[0])[4]
    for n in range(len(cuts)):
        pl.when(needs[cuts[n][0]] > cuts[n][1])(lambda n=n: pack_copy(n).wait())

    def add_masked(v, case):
        first_row = row0 + ROW * tile_of[case]

        def put(t, value):
            part = jnp.where(first_row < bars[t], 0.0, value)
            buf[v, slot_of[case], t] = buf[v, slot_of[case], t] + keeps[case, t] * part

        return put

    def one(v, offsets):
        low, high = offsets
        value = inflow_ref[v]
        shift = sy_ref[v]
        scalars = sx_ref[v], shift, fx_ref[v], fy_ref[v]
        borders = (0, lane_tiles + 1)
        from_low, from_high, reaches_second = cases(v)

        @pl.when(from_low)
        def _():
            fill_rows(frames, 0, borders, 16, 8, value)
            for t in range(lane_tiles):
                frames[0, t + 1, 16:24, :] = low_buf[t, pl.ds(low + shift + 9, ROW), :]

            @pl.when(shift == CFL)
            def _():
                fill_rows(frames, 0, borders, 8, 8, value)
                for t in range(lane_tiles):
                    frames[0, t + 1, 8:16, :] = low_buf[t, pl.ds(low + shift + 1, ROW), :]

            copy(v, 0, False).wait()
            advect(frames, 0, scalars, [(24, add_masked(v, 0))])
            copy(v, 0, True).start()

        @pl.when(reaches_second)
        def _():
            copy(v, 2, False).wait()
            advect(frames, 0, scalars, [(32, add_masked(v, 2))])
            copy(v, 2, True).start()

        @pl.when(from_high)
        def _():
            fill_rows(frames, 1, borders, 32, 8, value)
            for t in range(lane_tiles):
                frames[1, t + 1, 32:40, :] = high_buf[t, pl.ds(16 + high, ROW), :]
            copy(v, 1, False).wait()
            advect(frames, 1, scalars, [(24, add_masked(v, 1))])
            copy(v, 1, True).start()

        return low + low_need(shift), high + high_need(shift)

    lax.fori_loop(0, planes, one, (jnp.int32(0), jnp.int32(0)))

    def end(v, _):
        for case, applies in enumerate(cases(v)):
            pl.when(applies)(lambda case=case: copy(v, case, True).wait())
        return 0

    lax.fori_loop(0, planes, end, 0)


def finish_edges(small, factor, heights, sums, packs, cuts, out):
    planes, _, lane_tiles = out.shape[:3]
    fixed = [*in_hbm(*small[:5]), factor, *in_hbm(heights)]
    operands = [*fixed, *sums, *in_hbm(out), *packs]
    return pl.pallas_call(
        functools.partial(finish_kernel, cuts),
        out_shape=pltpu.HBM(out.shape, F32),
        in_specs=[SMEM_SPEC] * 6 + [VMEM_SPEC] * 5 + [HBM_SPEC] + [ANY_SPEC] * len(cuts),
        out_specs=HBM_SPEC,
        scratch_shapes=[
            pltpu.VMEM((2, lane_tiles + 2, 48, LANE), F32),
            pltpu.VMEM((planes, 2, lane_tiles, ROW, LANE), F32),
            pltpu.VMEM((3, lane_tiles, ROW, LANE), F32),
            pltpu.VMEM((lane_tiles, planes * LOW_ROWS + 32, LANE), F32),
            pltpu.VMEM((lane_tiles, planes * HIGH_ROWS + 32, LANE), F32),
            pltpu.VMEM((lane_tiles, ROW, LANE), jnp.int32),
            pltpu.SemaphoreType.DMA((len(cuts),)),
            pltpu.SemaphoreType.DMA((planes, 2)),
            pltpu.SemaphoreType.DMA((planes, 2)),
        ],
        input_output_aliases={len(fixed) + len(sums): 0},
        compiler_params=params(24),
        name="finish_edges",
    )(*operands)


def per_device(populations, shift_x, shift_y, frac_x, frac_y, inflow, wall_state, heights,
               impact_frequency_factor):
    planes, row_count, col_count = populations.shape
    space_count, vel_count = lax.axis_size("space"), lax.axis_size("vel")
    row_tiles, lane_tiles = row_count // ROW, col_count // LANE
    forward = [(i, i + 1) for i in range(space_count - 1)]
    backward = [(target, source) for source, target in forward]
    partner = [(i, i ^ 1) for i in range(vel_count)]
    across = [(i, i ^ 2) for i in range(vel_count)]

    small = (shift_x, shift_y, frac_x, frac_y, inflow, wall_state)
    factor = impact_frequency_factor.reshape(1)
    bars = heights.reshape(lane_tiles, LANE)
    pop = populations.reshape(planes, row_tiles, ROW, lane_tiles, LANE).transpose(0, 1, 3, 2, 4)
    low_sent, high_sent = min(LOW_SENT, planes * LOW_ROWS), min(HIGH_SENT, planes * HIGH_ROWS)
    cuts = [
        (0, 0, low_sent),
        (1, 0, high_sent),
        (0, low_sent, planes * LOW_ROWS),
        (1, high_sent, planes * HIGH_ROWS),
    ]
    plan = Plan(row_tiles, lane_tiles // 2)

    moved, mine, theirs, more_needed, *packs = advance(plan, small, bars, pop, cuts)
    received = lax.ppermute(theirs, "vel", partner)
    up, down, inside, edge_low, edge_high = fold(mine, received, plan.sizes)
    from_low = lax.ppermute(up, "space", forward)
    from_high = lax.ppermute(down, "space", backward)
    low_first = lax.ppermute(packs[0], "space", forward)
    high_first = lax.ppermute(packs[1], "space", backward)

    def total(sums, after=()):
        whole = small_call(add_kernel, "add", sums, lax.ppermute(sums, "vel", across), after)
        return whole, lax.ppermute(whole, "vel", partner)

    def send_more(low, high):
        return lax.ppermute(low, "space", forward), lax.ppermute(high, "space", backward)

    more = lax.cond(more_needed[0] > 0, send_more, lambda low, high: (low, high), packs[2], packs[3])
    sums_inside = total(inside)
    sums_low = total(small_call(join_low_kernel, "join_low", edge_low, from_low, (), 1))
    sums_high = total(small_call(join_high_kernel, "join_high", edge_high, from_high, (), 1))
    sizes = len(plan.inside), 2, 2
    out = relax_all(sizes, small, factor, sums_inside + sums_high + sums_low, moved)
    halo = low_first, high_first, *more
    out = finish_edges(small, factor, bars, sums_low + sums_high, halo, cuts, out)
    return out.transpose(0, 1, 3, 2, 4).reshape(planes, row_count, col_count)


def solution(mesh):
    return jax.shard_map(
        per_device,
        mesh=mesh,
        in_specs=(
            P("vel", "space", None),
            P("vel"),
            P("vel"),
            P("vel"),
            P("vel"),
            P("vel"),
            P("vel"),
            P(),
            P(),
        ),
        out_specs=P("vel", "space", None),
        check_vma=False,
    )
```
